128 devices in a mesh: pool: 16 (over y, x), tp: 8 (over z, core).
Axes of the slice: x: 4, y: 4, z: 4, core: 2. Of those that a mesh axis runs over, the one named last changes fastest.
Arguments:
- hidden: bfloat16 [8192, 8192], P('pool', 'tp'), may hold values from -6 to 6
- w_query: bfloat16 [8192, 4096], P(None, 'tp'), may hold values from -0.15625 to 0.15625
- w_keyval: bfloat16 [8192, 2048], P(None, 'tp'), may hold values from -0.0625 to 0.0625
- store: bfloat16 [1024, 8, 64, 2, 128], P('pool', 'tp'), may hold values from -270 to 270
- page_owner: int32 [16, 32], replicated, may hold values from 0 to 15, as said below
- page_slot: int32 [16, 32], replicated, may hold values from 0 to 63, as said below
- new_owner: int32 [16, 8], replicated, may hold values from 0 to 15, as said below
Outputs:
- attended: bfloat16 [8192, 4096], P('pool', 'tp')
- new_store: bfloat16 [512, 8, 64, 2, 128], P('pool', 'tp')
The draws below stay inside these ranges and needn't reach their ends.
Inputs may be any that keep to these rules, and one draw needn't show every extreme that they name: `page_owner`: one request has at most 4 pages on one owner, and every request has exactly 4 pages on some owner. `page_slot`: pages on one owner have distinct slots. `new_owner`: at most 2 pages of one request go to one owner, and in every draw one owner receives exactly 2 pages from every request.
All inputs are finite; a program needn't handle non-finite values.
Results may differ from the reference program's by a relative error of at most 0.02.
Values may be sent and summed in bfloat16 or wider, within the bound.
No kernel may reach another device: no remote copies, remote signals or barrier semaphores. Data moves between devices by JAX's collectives and lax.ppermute only.
A program may use at most 192 MiB of HBM per device.

```python
import math
import jax
import jax.numpy as jnp
from jax import lax

D = 8192
QH = 32
KVH = 8
HD = 128
PAGE = 64
PUSH_CAP = 2
SUF = 512
PREF_PAGES = 32
REQUESTS = 16
TOKENS = 8192
CAP = 4
STORE = 64
NEW_PAGES = 8
NEW_SLOTS = 32
N_POOL = 16


def page_layout(key):
    full_key, rest_key, block_key = jax.random.split(key, 3)
    full_owner = jax.random.permutation(full_key, N_POOL).astype(jnp.int32)

    def per_request(request_key, owner_full):
        spread_key, shuffle_key = jax.random.split(request_key)
        others = jax.random.permutation(spread_key, (N_POOL - 1) * CAP)[:PREF_PAGES - CAP] // CAP
        others = (others + (others >= owner_full).astype(others.dtype)).astype(jnp.int32)
        chosen = jnp.concatenate([jnp.full((CAP,), owner_full, jnp.int32), others])
        return chosen[jax.random.permutation(shuffle_key, PREF_PAGES)]
    owners = jax.vmap(per_request)(jax.random.split(rest_key, REQUESTS), full_owner)
    same_owner = owners[:, :, None] == owners[:, None, :]
    earlier = jnp.arange(PREF_PAGES)[None, :] < jnp.arange(PREF_PAGES)[:, None]
    ranks = jnp.sum(same_owner & earlier[None], axis=2).astype(jnp.int32)
    blocks = jax.vmap(lambda block_seed: jax.random.permutation(block_seed, N_POOL))(jax.random.split(block_key, N_POOL)).astype(jnp.int32)
    first_owner = full_owner[0]
    chosen_row = blocks[first_owner]
    shifted = (chosen_row - chosen_row[0] + N_POOL - 1) % N_POOL
    blocks = jnp.where(jnp.arange(N_POOL)[:, None] == first_owner, shifted[None, :], blocks)
    request_ids = jnp.broadcast_to(jnp.arange(REQUESTS, dtype=jnp.int32)[:, None], owners.shape)
    slot_ids = blocks[owners, request_ids] * CAP + ranks
    return (owners.astype(jnp.int32), slot_ids.astype(jnp.int32))


def draw_page_owner(key, part):
    owners, slot_ids = page_layout(key)
    return owners


def draw_page_slot(key, part):
    owners, slot_ids = page_layout(key)
    return slot_ids


def draw_new_owner(key, part):
    key = jax.random.fold_in(key, 5)
    busy_key, rest_key = jax.random.split(key)
    busiest = jax.random.randint(busy_key, (), 0, N_POOL, jnp.int32)

    def per_request(request_key):
        spread_key, shuffle_key = jax.random.split(request_key)
        others = jax.random.permutation(spread_key, (N_POOL - 1) * PUSH_CAP)[:NEW_PAGES - PUSH_CAP] // PUSH_CAP
        others = (others + (others >= busiest).astype(others.dtype)).astype(jnp.int32)
        chosen = jnp.concatenate([jnp.full((PUSH_CAP,), busiest, jnp.int32), others])
        return chosen[jax.random.permutation(shuffle_key, NEW_PAGES)]
    return jax.vmap(per_request)(jax.random.split(rest_key, REQUESTS)).astype(jnp.int32)


def draw_store(key, part):
    key = jax.random.fold_in(key, 11)
    base_key = jax.random.fold_in(key, 0)
    shape = (N_POOL * STORE, KVH, PAGE, 2, HD)
    values = jnp.clip(jax.random.normal(base_key, shape, jnp.float32), -4.0, 4.0)
    return values.astype(jnp.bfloat16)


def levels(rng, shape, cuts, low, high):
    def one(position, parts):
        steps = jax.random.uniform(jax.random.fold_in(jax.random.fold_in(rng, 6), position), (parts,), jnp.float32, low / len(cuts), high / len(cuts))
        return jnp.repeat(jnp.exp(steps), shape[position] // parts).reshape((-1,) + (1,) * (len(shape) - position - 1))

    gain = one(*cuts[0])
    for cut in cuts[1:]:
        gain = gain * one(*cut)
    return gain


def bell_draw(key, shape, width, limit, cuts=(), kind=jnp.bfloat16):
    array = width * jax.random.normal(key, shape, jnp.float32)
    if cuts:
        array = array * levels(key, shape, cuts, -0.22, 0.18)
    return jnp.clip(array, -limit, limit).astype(kind)


def setup_inputs(seed: int = 0) -> dict:
    key_list = jax.random.split(jax.random.key(seed), 8)
    hidden = bell_draw(key_list[0], (TOKENS, D), 1.0, 6.0, ((0, 16), (1, 8)))
    w_query = bell_draw(key_list[1], (D, QH * HD), (D // 6) ** -0.5, 0.15625, ((1, 8),))
    w_keyval = bell_draw(key_list[2], (D, KVH * 2 * HD), D ** -0.5, 0.0625, ((1, 8),))
    store = draw_store(jax.random.fold_in(key_list[7], 71), 0)
    page_owner = draw_page_owner(jax.random.fold_in(key_list[7], 71), 0)
    page_slot = draw_page_slot(jax.random.fold_in(key_list[7], 71), 0)
    new_owner = draw_new_owner(jax.random.fold_in(key_list[7], 71), 0)
    return dict(hidden=hidden, w_query=w_query, w_keyval=w_keyval, store=store, page_owner=page_owner, page_slot=page_slot, new_owner=new_owner)


neg_big = -1e+30

def rope_tables(row_count, offset):
    half_dim = HD // 2
    frequency = 500000.0 ** (-(jnp.arange(half_dim, dtype=jnp.float32) * (2.0 / HD)))
    positions = (offset + jnp.arange(row_count, dtype=jnp.int32)).astype(jnp.float32)
    angles = positions[:, None] * frequency[None, :]
    return (jnp.cos(angles), jnp.sin(angles))

def rotate(values, cosine, sine_table):
    half_dim = HD // 2
    first_half = values[..., :half_dim]
    second_half = values[..., half_dim:]
    cosine = cosine[:, None, :]
    sine_table = sine_table[:, None, :]
    return jnp.concatenate([first_half * cosine - second_half * sine_table, second_half * cosine + first_half * sine_table], axis=-1)

def reference(hidden, w_query, w_keyval, store, page_owner, page_slot, new_owner):
    group_size = QH // KVH
    inv_root = 1.0 / math.sqrt(HD)
    cosine, sine_table = rope_tables(SUF, PREF_PAGES * PAGE)
    causal = jnp.arange(SUF)[:, None] >= jnp.arange(SUF)[None, :]
    visible = jnp.concatenate([jnp.ones((SUF, PREF_PAGES * PAGE), dtype=bool), causal], axis=1)

    def one_request(request):
        row_block = lax.dynamic_slice_in_dim(hidden, request * SUF, SUF, 0)
        widened = row_block.astype(jnp.float32)
        inv_norm = lax.rsqrt(lax.optimization_barrier(jnp.mean(widened * widened, axis=1, keepdims=True)) + 1e-05)
        query_sum = jnp.dot(row_block, w_query, preferred_element_type=jnp.float32) * inv_norm
        keyval_sum = jnp.dot(row_block, w_keyval, preferred_element_type=jnp.float32) * inv_norm
        queries = rotate(query_sum.reshape(SUF, QH, HD), cosine, sine_table).astype(jnp.bfloat16)
        keyval = keyval_sum.reshape(SUF, KVH, 2, HD)
        fresh_kv = jnp.stack([rotate(keyval[:, :, 0], cosine, sine_table), keyval[:, :, 1]], axis=2).astype(jnp.bfloat16)
        queries = lax.optimization_barrier(queries)
        owners = lax.dynamic_index_in_dim(page_owner, request, 0, keepdims=False)
        slot_ids = lax.dynamic_index_in_dim(page_slot, request, 0, keepdims=False)
        page_data = store[(owners * STORE + slot_ids).astype(jnp.int32)]
        cached = jnp.transpose(page_data, (0, 2, 1, 3, 4)).reshape(PREF_PAGES * PAGE, KVH, 2, HD)
        cache_all = lax.optimization_barrier(jnp.concatenate([cached, fresh_kv], axis=0))
        cache_wide = cache_all.astype(jnp.float32)
        grouped = queries.reshape(SUF, KVH, group_size, HD).astype(jnp.float32)
        scores = jnp.einsum('qhgd,khd->hgqk', grouped, cache_wide[:, :, 0]) * inv_root
        scores = jnp.where(visible, scores, neg_big)
        row_max = lax.optimization_barrier(jnp.max(scores, axis=3, keepdims=True))
        weights = jnp.exp(scores - row_max)
        totals = lax.optimization_barrier(jnp.sum(weights, axis=3))
        rounded = lax.optimization_barrier(weights.astype(jnp.bfloat16)).astype(jnp.float32)
        summed = jnp.einsum('hgqk,khd->qhgd', rounded, cache_wide[:, :, 1])
        result = summed / jnp.transpose(totals, (2, 0, 1))[..., None]
        return (result.reshape(SUF, QH * HD).astype(jnp.bfloat16), fresh_kv)
    results, fresh_all = lax.map(one_request, jnp.arange(REQUESTS, dtype=jnp.int32))
    attended = results.reshape(TOKENS, QH * HD)
    new_pages = fresh_all.reshape(REQUESTS, NEW_PAGES, PAGE, KVH, 2, HD)
    new_pages = jnp.transpose(new_pages, (0, 1, 3, 2, 4, 5)).reshape(REQUESTS * NEW_PAGES, KVH, PAGE, 2, HD)
    targets = new_owner.reshape(-1).astype(jnp.int32)
    to_owner = (targets[:, None] == jnp.arange(N_POOL, dtype=jnp.int32)[None, :]).astype(jnp.int32)
    earlier_count = jnp.cumsum(to_owner, axis=0) - to_owner
    placed = lax.optimization_barrier(jnp.sum(earlier_count * to_owner, axis=1)).astype(jnp.int32)
    target_slot = (targets * NEW_SLOTS + placed).astype(jnp.int32)
    new_store = jnp.zeros((N_POOL * NEW_SLOTS, KVH, PAGE, 2, HD), jnp.bfloat16).at[target_slot].set(new_pages)
    return (attended, new_store)
```

```python
import functools
import math

import jax
import jax.numpy as jnp
from jax import lax
from jax.experimental import pallas as pl
from jax.experimental.pallas import tpu as pltpu
from jax.sharding import PartitionSpec as P

D = 8192
HD = 128
PAGE = 64
CAP = 4
PUSH_CAP = 2
HEADS = 4
FEAT = 1024
QW = 512
KVW = 256
POOL = 16
PAGES = 32
NEW_PAGES = 8
SLOTS = 32
CHUNKS = (48, 16)
MIB = 1024 * 1024
SCALE = math.log2(math.e) / math.sqrt(HD)
F32 = jnp.float32
BF16 = jnp.bfloat16
ANY = pl.BlockSpec(memory_space=pl.ANY)
VMEM = pl.BlockSpec(memory_space=pltpu.VMEM)
SMEM = pl.BlockSpec(memory_space=pltpu.SMEM)


def params(mib):
    return pltpu.CompilerParams(vmem_limit_bytes=mib * MIB)


def cost(flops, nbytes):
    return pl.CostEstimate(flops=flops, bytes_accessed=nbytes, transcendentals=0)


def shape(dims, dtype):
    return jax.ShapeDtypeStruct(dims, dtype)


def gather_kernel(owner_ref, slot_ref, store_ref, out_ref, sems, counts):
    me = lax.axis_index("pool")

    def copy(slot, index):
        return pltpu.make_async_copy(store_ref.at[slot], out_ref.at[index], sems.at[index])

    def start_request(request, _):
        def start_page(page, rank):
            mine = owner_ref[request, page] == me

            @pl.when(mine)
            def _():
                copy(slot_ref[request, page], request * CAP + rank).start()

            return rank + mine.astype(jnp.int32)

        counts[request] = lax.fori_loop(0, PAGES, start_page, jnp.int32(0), unroll=8)
        return 0

    def finish_request(request, _):
        def finish_page(rank, _):
            copy(0, request * CAP + rank).wait()
            return 0

        return lax.fori_loop(0, counts[request], finish_page, 0)

    lax.fori_loop(0, POOL, start_request, 0)
    lax.fori_loop(0, POOL, finish_request, 0)


def gather_pages(page_owner, page_slot, store):
    return pl.pallas_call(
        gather_kernel,
        out_shape=shape((POOL * CAP, 2 * PAGE, HD), BF16),
        in_specs=[SMEM, SMEM, ANY],
        out_specs=ANY,
        scratch_shapes=[
            pltpu.SemaphoreType.DMA((POOL * CAP,)),
            pltpu.SMEM((POOL,), jnp.int32),
        ],
        cost_estimate=cost(0, 4 * MIB),
        name="gather_pages",
    )(page_owner, page_slot, store)


def split_matrix():
    row = lax.broadcasted_iota(jnp.int32, (2 * PAGE, 2 * PAGE), 0)
    column = lax.broadcasted_iota(jnp.int32, (2 * PAGE, 2 * PAGE), 1)
    wanted = jnp.where(row < PAGE, 2 * row, 2 * (row - PAGE) + 1)
    return (column == wanted).astype(BF16)


def split_kernel(owner_ref, pages_ref, keys_ref, values_ref, counts):
    me = lax.axis_index("pool")
    picker = split_matrix()
    for owner in range(POOL):
        counts[owner] = 0
    values_ref[:, HD:] = jnp.ones((PAGES * PAGE, HD), BF16)
    for page in range(PAGES):
        owner = owner_ref[me, page]
        rank = counts[owner]
        counts[owner] = rank + 1
        both = jnp.dot(picker, pages_ref[owner * CAP + rank], preferred_element_type=F32)
        rows = pl.ds(page * PAGE, PAGE)
        keys_ref[rows, :] = both[:PAGE].astype(BF16)
        values_ref[rows, :HD] = both[PAGE:].astype(BF16)


def split_pages(page_owner, pages):
    return pl.pallas_call(
        split_kernel,
        out_shape=[
            shape((PAGES * PAGE, HD), BF16),
            shape((PAGES * PAGE, 2 * HD), BF16),
        ],
        in_specs=[SMEM, VMEM],
        out_specs=[VMEM, VMEM],
        scratch_shapes=[pltpu.SMEM((POOL,), jnp.int32)],
        compiler_params=params(16),
        cost_estimate=cost(2 * 2048 * 128 * 256, 4 * MIB),
        name="split_pages",
    )(page_owner, pages)


def block_index(z_step, other_core):
    index = lax.axis_index("tp")
    z = lax.rem(index // 2 + z_step, 4)
    core = lax.rem(index, 2)
    return 2 * z + (1 - core if other_core else core)


def squares_of(rows):
    wide = rows.astype(F32)
    total = None
    for lane in range(0, FEAT, HD):
        part = wide[:, lane : lane + HD]
        total = part * part if total is None else total + part * part
    return total


def weight_copies(wq_ref, wkv_ref, wq_buf, wkv_buf, sems, blocks):
    copies = []
    for i, (z_step, other) in enumerate(blocks):
        start = pl.multiple_of(block_index(z_step, other) * FEAT, FEAT)
        rows = pl.ds(start, FEAT)
        copies.append(
            (
                pltpu.make_async_copy(wq_ref.at[rows, :], wq_buf.at[i], sems.at[2 * i]),
                pltpu.make_async_copy(wkv_ref.at[rows, :], wkv_buf.at[i], sems.at[2 * i + 1]),
            )
        )
    return copies


EARLY = ((0, False), (0, True), (3, False), (3, True), (1, False), (1, True))
LATE = ((2, False), (2, True))


def early_kernel(*refs):
    count = len(EARLY)
    x_refs = refs[:count]
    wq_ref, wkv_ref, q_ref, kv_ref, sq_ref, x_buf, wq_buf, wkv_buf, x_sems, w_sems = refs[count:]
    x_copies = [
        pltpu.make_async_copy(x_refs[i], x_buf.at[i], x_sems.at[i]) for i in range(count)
    ]
    w_copies = weight_copies(wq_ref, wkv_ref, wq_buf, wkv_buf, w_sems, EARLY)
    for i in range(count):
        x_copies[i].start()
        w_copies[i][0].start()
        w_copies[i][1].start()
    for i in range(count):
        x_copies[i].wait()
        w_copies[i][0].wait()
        w_copies[i][1].wait()
        rows = x_buf[i]
        q_part = jnp.dot(rows, wq_buf[i], preferred_element_type=F32)
        kv_part = jnp.dot(rows, wkv_buf[i], preferred_element_type=F32)
        sq_part = squares_of(rows)
        if i == 0:
            q_ref[...] = q_part
            kv_ref[...] = kv_part
            sq_ref[...] = sq_part
        else:
            q_ref[...] += q_part
            kv_ref[...] += kv_part
            sq_ref[...] += sq_part


def project_early(blocks, w_query, w_keyval):
    rows = blocks[0].shape[0]
    count = len(EARLY)
    return pl.pallas_call(
        early_kernel,
        out_shape=[shape((rows, QW), F32), shape((rows, KVW), F32), shape((rows, HD), F32)],
        in_specs=[ANY] * (count + 2),
        out_specs=[VMEM] * 3,
        scratch_shapes=[
            pltpu.VMEM((count, rows, FEAT), BF16),
            pltpu.VMEM((count, FEAT, QW), BF16),
            pltpu.VMEM((count, FEAT, KVW), BF16),
            pltpu.SemaphoreType.DMA((count,)),
            pltpu.SemaphoreType.DMA((2 * count,)),
        ],
        compiler_params=params(32),
        cost_estimate=cost(
            2 * rows * count * FEAT * (QW + KVW), count * FEAT * (QW + KVW + rows) * 2
        ),
        name="project_early",
    )(*blocks, w_query, w_keyval)


def turn(values, cosine, sine):
    return values * cosine + pltpu.roll(values, HD // 2, 1) * sine


def late_kernel(
    length,
    owner_ref,
    top_ref,
    bottom_ref,
    top_other_ref,
    bottom_other_ref,
    q_in,
    kv_in,
    sq_in,
    cos_ref,
    sin_ref,
    wq_ref,
    wkv_ref,
    q_ref,
    kv_ref,
    send_ref,
    x_buf,
    wq_buf,
    wkv_buf,
    x_sems,
    w_sems,
    counts,
):
    half = top_ref.shape[0]
    sources = ((top_ref, bottom_ref), (top_other_ref, bottom_other_ref))
    x_copies = [
        pltpu.make_async_copy(
            sources[i][j], x_buf.at[i, pl.ds(j * half, half), :], x_sems.at[2 * i + j]
        )
        for i in range(2)
        for j in range(2)
    ]
    w_copies = weight_copies(wq_ref, wkv_ref, wq_buf, wkv_buf, w_sems, LATE)
    for i in range(2):
        for copy in (x_copies[2 * i], x_copies[2 * i + 1], *w_copies[i]):
            copy.start()
    q_sum = q_in[...]
    kv_sum = kv_in[...]
    squares = sq_in[...]
    for i in range(2):
        for copy in (x_copies[2 * i], x_copies[2 * i + 1], *w_copies[i]):
            copy.wait()
        rows = x_buf[i]
        q_sum += jnp.dot(rows, wq_buf[i], preferred_element_type=F32)
        kv_sum += jnp.dot(rows, wkv_buf[i], preferred_element_type=F32)
        squares += squares_of(rows)
    inv_norm = lax.rsqrt(jnp.sum(squares, axis=1, keepdims=True) / D + 1e-05)
    cosine = cos_ref[...]
    sine = sin_ref[...]
    for head in range(HEADS):
        lanes = slice(head * HD, (head + 1) * HD)
        q_ref[:, lanes] = turn(q_sum[:, lanes] * inv_norm, cosine, sine).astype(BF16)
    keys = turn(kv_sum[:, :HD] * inv_norm, cosine, sine).astype(BF16)
    values = (kv_sum[:, HD:] * inv_norm).astype(BF16)
    kv_ref[:, :HD] = keys
    kv_ref[:, HD:] = values
    row = lax.broadcasted_iota(jnp.int32, (2 * length, 2 * length), 0)
    column = lax.broadcasted_iota(jnp.int32, (2 * length, 2 * length), 1)
    picker = (column == (row >> 1) + (row & 1) * length).astype(BF16)
    me = lax.axis_index("pool")
    for owner in range(POOL):
        counts[owner] = 0
    for page in range(NEW_PAGES):
        owner = owner_ref[me, page]
        rank = counts[owner]
        counts[owner] = rank + 1
        rows = slice(page * length, (page + 1) * length)
        both = jnp.concatenate([keys[rows], values[rows]], axis=0)
        mixed = jnp.dot(picker, both, preferred_element_type=F32).astype(BF16)
        send_ref[owner * PUSH_CAP + rank] = mixed


def project_late(length, new_owner, halves, sums, cosine, sine, w_query, w_keyval):
    rows = sums[0].shape[0]
    return pl.pallas_call(
        functools.partial(late_kernel, length),
        out_shape=[
            shape((rows, QW), BF16),
            shape((rows, KVW), BF16),
            shape((POOL * PUSH_CAP, 2 * length, HD), BF16),
        ],
        in_specs=[SMEM] + [ANY] * 4 + [VMEM] * 5 + [ANY] * 2,
        out_specs=[VMEM] * 3,
        scratch_shapes=[
            pltpu.VMEM((2, rows, FEAT), BF16),
            pltpu.VMEM((2, FEAT, QW), BF16),
            pltpu.VMEM((2, FEAT, KVW), BF16),
            pltpu.SemaphoreType.DMA((4,)),
            pltpu.SemaphoreType.DMA((4,)),
            pltpu.SMEM((POOL,), jnp.int32),
        ],
        compiler_params=params(24),
        cost_estimate=cost(2 * rows * 2 * FEAT * (QW + KVW), 2 * FEAT * (QW + KVW + rows) * 2),
        name="project_late",
    )(new_owner, *halves, *sums, cosine, sine, w_query, w_keyval)


def dot_nt(a, b):
    return lax.dot_general(a, b, (((1,), (1,)), ((), ())), preferred_element_type=F32)


def prefix_kernel(q_ref, keys_ref, values_ref, sum_ref, top_ref, total_ref):
    block = 128

    def one(index, _):
        rows = pl.ds(pl.multiple_of(index * block, block), block)
        for head in range(HEADS):
            lanes = slice(head * HD, (head + 1) * HD)
            scores = dot_nt(q_ref[rows, lanes], keys_ref[...])
            top = jnp.max(scores, axis=1, keepdims=True)
            weights = jnp.exp2((scores - top) * SCALE).astype(BF16)
            both = jnp.dot(weights, values_ref[...], preferred_element_type=F32)
            sum_ref[rows, lanes] = both[:, :HD]
            total_ref[rows, lanes] = both[:, HD:]
            top_ref[rows, lanes] = jnp.broadcast_to(top, (block, HD))
        return 0

    lax.fori_loop(0, q_ref.shape[0] // block, one, 0)


def attend_prefix(queries, keys, values):
    rows = queries.shape[0]
    return pl.pallas_call(
        prefix_kernel,
        out_shape=[shape((rows, QW), F32)] * 3,
        in_specs=[VMEM] * 3,
        out_specs=[VMEM] * 3,
        compiler_params=params(32),
        cost_estimate=cost(2 * rows * 4 * 2048 * 512, 4 * MIB),
        name="attend_prefix",
    )(queries, keys, values)


def positions(length, offset, dims, axis):
    index = lax.broadcasted_iota(jnp.int32, dims, axis)
    return lax.div(index, jnp.int32(length)) * PAGE + offset + lax.rem(index, jnp.int32(length))


def suffix_kernel(*refs):
    count = len(CHUNKS)
    q_refs = refs[:count]
    kv_refs = refs[count : 2 * count]
    partial_refs = [refs[2 * count + 3 * i : 2 * count + 3 * i + 3] for i in range(count)]
    out_ref, keys_buf, values_buf = refs[5 * count :]
    row_total = NEW_PAGES * PAGE
    base = 0
    key_positions = []
    offset = 0
    for i, length in enumerate(CHUNKS):
        rows = NEW_PAGES * length
        keys_buf[base : base + rows, :] = kv_refs[i][:, :HD]
        values_buf[base : base + rows, :HD] = kv_refs[i][:, HD:]
        key_positions.append(positions(length, offset, (1, rows), 1))
        base += rows
        offset += length
    values_buf[:, HD:] = jnp.ones((row_total, HD), BF16)
    key_position = jnp.concatenate(key_positions, axis=1)
    offset = 0
    for i, length in enumerate(CHUNKS):
        rows = NEW_PAGES * length
        allowed = positions(length, offset, (rows, 1), 0) >= key_position
        sum_ref, top_ref, total_ref = partial_refs[i]
        for head in range(HEADS):
            lanes = slice(head * HD, (head + 1) * HD)
            scores = dot_nt(q_refs[i][:, lanes], keys_buf[...])
            scores = jnp.where(allowed, scores, -1e30)
            before = top_ref[:, lanes]
            top = jnp.maximum(jnp.max(scores, axis=1, keepdims=True), before)
            weights = jnp.exp2((scores - top[:, :1]) * SCALE).astype(BF16)
            both = jnp.dot(weights, values_buf[...], preferred_element_type=F32)
            factor = jnp.exp2((before - top) * SCALE)
            result = (both[:, :HD] + sum_ref[:, lanes] * factor) / (
                both[:, HD:] + total_ref[:, lanes] * factor
            )
            out_ref[:, offset : offset + length, lanes] = result.astype(BF16).reshape(
                NEW_PAGES, length, HD
            )
        offset += length


def attend_suffix(queries, keyvals, partials):
    count = len(CHUNKS)
    rows = NEW_PAGES * PAGE
    return pl.pallas_call(
        suffix_kernel,
        out_shape=shape((NEW_PAGES, PAGE, QW), BF16),
        in_specs=[VMEM] * (5 * count),
        out_specs=VMEM,
        scratch_shapes=[pltpu.VMEM((rows, HD), BF16), pltpu.VMEM((rows, 2 * HD), BF16)],
        compiler_params=params(32),
        cost_estimate=cost(2 * rows * 4 * 512 * 512, 8 * MIB),
        name="attend_suffix",
    )(*queries, *keyvals, *[p for partial in partials for p in partial])


def place_kernel(offset, first, owner_ref, received_ref, *refs):
    out_ref, zeros, sems = refs[-3:]
    me = lax.axis_index("pool")
    height = received_ref.shape[1]
    zeros[...] = jnp.zeros_like(zeros)

    def target(slot):
        return out_ref.at[slot, pl.ds(2 * offset, height), :]

    def request_loop(request, slot):
        def page_loop(page, state):
            slot, rank = state
            mine = owner_ref[request, page] == me

            @pl.when(mine)
            def _():
                source = received_ref.at[request * PUSH_CAP + rank]
                pltpu.make_async_copy(source, target(slot), sems.at[slot]).start()

            step = mine.astype(jnp.int32)
            return slot + step, rank + step

        slot, _ = lax.fori_loop(0, NEW_PAGES, page_loop, (slot, jnp.int32(0)), unroll=True)
        return slot

    used = lax.fori_loop(0, POOL, request_loop, jnp.int32(0))

    def clear(slot, _):
        pltpu.make_async_copy(zeros, target(slot), sems.at[slot]).start()
        return 0

    lax.fori_loop(used, SLOTS, clear, 0)

    def finish(slot, _):
        pltpu.make_async_copy(zeros, target(slot), sems.at[slot]).wait()
        return 0

    lax.fori_loop(0, SLOTS, finish, 0)


def place_pages(offset, new_owner, received, placed):
    first = placed is None
    height = received.shape[1]
    return pl.pallas_call(
        functools.partial(place_kernel, offset, first),
        out_shape=shape((SLOTS, 2 * PAGE, HD), BF16),
        in_specs=[SMEM, ANY] + ([] if first else [ANY]),
        out_specs=ANY,
        scratch_shapes=[pltpu.VMEM((height, HD), BF16), pltpu.SemaphoreType.DMA((SLOTS,))],
        input_output_aliases={} if first else {2: 0},
        cost_estimate=cost(0, 2 * SLOTS * height * HD * 2),
        name="place_pages",
    )(new_owner, received, *([] if first else [placed]))


def shift(values, step):
    pairs = [(i, ((i // 2 + step) % 4) * 2 + i % 2) for i in range(8)]
    return lax.ppermute(values, "tp", pairs)


def swap(values):
    return lax.ppermute(values, "tp", [(i, i ^ 1) for i in range(8)])


def rope_tables(row_count, offset):
    half_dim = HD // 2
    frequency = 500000.0 ** (-(jnp.arange(half_dim, dtype=F32) * (2.0 / HD)))
    place = (offset + jnp.arange(row_count, dtype=jnp.int32)).astype(F32)
    angles = place[:, None] * frequency[None, :]
    cosine, sine = jnp.cos(angles), jnp.sin(angles)
    return jnp.concatenate([cosine, cosine], 1), jnp.concatenate([-sine, sine], 1)


def take(values, offset, length):
    parts = values.reshape(NEW_PAGES, PAGE, values.shape[1])[:, offset : offset + length]
    return parts.reshape(NEW_PAGES * length, values.shape[1])


def body(hidden, w_query, w_keyval, store, page_owner, page_slot, new_owner):
    offsets = [sum(CHUNKS[:i]) for i in range(len(CHUNKS))]
    chunks = [take(hidden, o, n) for o, n in zip(offsets, CHUNKS)]
    ahead = [shift(x, 1) for x in chunks]
    behind = [shift(x, -1) for x in chunks]
    packed = gather_pages(page_owner, page_slot, store.reshape(64, 2 * PAGE, HD))
    pages = lax.all_to_all(packed, "pool", split_axis=0, concat_axis=0, tiled=True)
    cosine, sine = rope_tables(NEW_PAGES * PAGE, PAGES * PAGE)
    keys, values = split_pages(page_owner, pages)
    queries, keyvals, partials = [], [], []
    placed = None
    for i, (offset, length) in enumerate(zip(offsets, CHUNKS)):
        half = NEW_PAGES * length // 2
        top = shift(ahead[i][:half], 1)
        bottom = shift(behind[i][half:], -1)
        blocks = (
            chunks[i],
            swap(chunks[i]),
            ahead[i],
            swap(ahead[i]),
            behind[i],
            swap(behind[i]),
        )
        sums = project_early(blocks, w_query, w_keyval)
        q, kv, send = project_late(
            length,
            new_owner,
            (top, bottom, swap(top), swap(bottom)),
            sums,
            take(cosine, offset, length),
            take(sine, offset, length),
            w_query,
            w_keyval,
        )
        received = lax.all_to_all(send, "pool", split_axis=0, concat_axis=0, tiled=True)
        placed = place_pages(offset, new_owner, received, placed)
        queries.append(q)
        keyvals.append(kv)
        partials.append(attend_prefix(q, keys, values))
    attended = attend_suffix(queries, keyvals, partials).reshape(NEW_PAGES * PAGE, QW)
    return attended, placed.reshape(SLOTS, 1, PAGE, 2, HD)


def solution(mesh):
    in_specs = (
        P("pool", "tp"),
        P(None, "tp"),
        P(None, "tp"),
        P("pool", "tp", None, None, None),
        P(),
        P(),
        P(),
    )
    out_specs = (P("pool", "tp"), P("pool", "tp", None, None, None))
    return jax.shard_map(body, mesh=mesh, in_specs=in_specs, out_specs=out_specs, check_vma=False)
```

```python
import functools
import math

import jax
import jax.numpy as jnp
from jax import lax
from jax.experimental import pallas as pl
from jax.experimental.pallas import tpu as pltpu
from jax.sharding import PartitionSpec as P

D = 8192
HD = 128
PAGE = 64
CAP = 4
PUSH_CAP = 2
HEADS = 4
FEAT = 1024
QW = 512
KVW = 256
POOL = 16
PAGES = 32
NEW_PAGES = 8
SLOTS = 32
ROWS = 512
TAKE, PUSH, PLACE = 16, 17, 18
MIB = 1024 * 1024
SCALE = math.log2(math.e) / math.sqrt(HD)
F32 = jnp.float32
BF16 = jnp.bfloat16
HBM = pl.BlockSpec(memory_space=pltpu.HBM)
VMEM = pl.BlockSpec(memory_space=pltpu.VMEM)
SMEM = pl.BlockSpec(memory_space=pltpu.SMEM)


def params(mib):
    return pltpu.CompilerParams(vmem_limit_bytes=mib * MIB)


def cost(flops, nbytes):
    return pl.CostEstimate(flops=flops, bytes_accessed=nbytes, transcendentals=0)


def shape(dims, dtype):
    return jax.ShapeDtypeStruct(dims, dtype)


def ranks_of(owners, lanes):
    ranks = jnp.zeros_like(owners)
    for j in range(owners.shape[1]):
        ranks += ((owners == owners[:, j : j + 1]) & (lanes > j)).astype(jnp.int32)
    return ranks


def table_kernel(page_owner_ref, page_slot_ref, new_owner_ref, out_ref):
    me = lax.axis_index("pool")
    out_ref[...] = jnp.zeros_like(out_ref)
    owners, slots = page_owner_ref[...], page_slot_ref[...]
    lanes = lax.broadcasted_iota(jnp.int32, owners.shape, 1)
    rows = lax.broadcasted_iota(jnp.int32, owners.shape, 0)
    ranks = ranks_of(owners, lanes)
    for k in range(CAP):
        chosen = jnp.where((owners == me) & (ranks == k), slots, 0)
        out_ref[:POOL, k : k + 1] = jnp.sum(chosen, axis=1, keepdims=True)
    mine = jnp.where(rows == me, owners * CAP + ranks, 0)
    out_ref[TAKE : TAKE + 1, :PAGES] = jnp.sum(mine, axis=0, keepdims=True)
    targets = new_owner_ref[...]
    target_lanes = lax.broadcasted_iota(jnp.int32, targets.shape, 1)
    target_rows = lax.broadcasted_iota(jnp.int32, targets.shape, 0)
    ranks = ranks_of(targets, target_lanes)
    mine = jnp.where(target_rows == me, targets * PUSH_CAP + ranks, 0)
    out_ref[PUSH : PUSH + 1, :NEW_PAGES] = jnp.sum(mine, axis=0, keepdims=True)
    kept = (targets == me).astype(jnp.int32)
    slot = jnp.zeros_like(targets)
    for j in range(NEW_PAGES):
        slot += jnp.where(target_lanes > j, kept[:, j : j + 1], 0)
    in_row = jnp.sum(kept, axis=1, keepdims=True)
    for r in range(POOL):
        slot += jnp.where(target_rows > r, in_row[r : r + 1, :], 0)
    source = jnp.zeros((POOL, SLOTS), jnp.int32)
    slot_lanes = lax.broadcasted_iota(jnp.int32, source.shape, 1)
    slot_rows = lax.broadcasted_iota(jnp.int32, source.shape, 0)
    for j in range(NEW_PAGES):
        hit = (kept[:, j : j + 1] > 0) & (slot[:, j : j + 1] == slot_lanes)
        source += jnp.where(hit, slot_rows * PUSH_CAP + ranks[:, j : j + 1] + 1, 0)
    out_ref[PLACE : PLACE + 1, :SLOTS] = jnp.sum(source, axis=0, keepdims=True)


def make_table(page_owner, page_slot, new_owner):
    return pl.pallas_call(
        table_kernel,
        out_shape=shape((24, HD), jnp.int32),
        in_specs=[VMEM] * 3,
        out_specs=VMEM,
        compiler_params=params(4),
        cost_estimate=cost(0, 16384),
        name="make_table",
    )(page_owner, page_slot, new_owner)


def gather_kernel(table_ref, store_ref, out_ref):
    def one(index, _):
        out_ref[index] = store_ref[table_ref[index >> 2, index & 3]]
        return 0

    lax.fori_loop(0, POOL * CAP, one, 0, unroll=8)


def gather_pages(table, store):
    return pl.pallas_call(
        gather_kernel,
        out_shape=shape((POOL * CAP, 2 * PAGE, HD), BF16),
        in_specs=[SMEM, VMEM],
        out_specs=VMEM,
        compiler_params=params(8),
        cost_estimate=cost(0, 4 * MIB),
        name="gather_pages",
    )(table, store)


def split_kernel(table_ref, pages_ref, keys_ref, values_ref):
    row = lax.broadcasted_iota(jnp.int32, (2 * PAGE, 2 * PAGE), 0)
    column = lax.broadcasted_iota(jnp.int32, (2 * PAGE, 2 * PAGE), 1)
    wanted = jnp.where(row < PAGE, 2 * row, 2 * (row - PAGE) + 1)
    picker = (column == wanted).astype(BF16)
    values_ref[:, HD:] = jnp.ones((PAGES * PAGE, HD), BF16)
    for page in range(PAGES):
        both = jnp.dot(picker, pages_ref[table_ref[TAKE, page]], preferred_element_type=F32)
        rows = pl.ds(page * PAGE, PAGE)
        keys_ref[rows, :] = both[:PAGE].astype(BF16)
        values_ref[rows, :HD] = both[PAGE:].astype(BF16)


def split_pages(table, pages):
    return pl.pallas_call(
        split_kernel,
        out_shape=[
            shape((PAGES * PAGE, HD), BF16),
            shape((PAGES * PAGE, 2 * HD), BF16),
        ],
        in_specs=[SMEM, VMEM],
        out_specs=[VMEM, VMEM],
        compiler_params=params(8),
        cost_estimate=cost(2 * 2048 * 128 * 256, 4 * MIB),
        name="split_pages",
    )(table, pages)


def block_index(z_step, other_core):
    index = lax.axis_index("tp")
    z = lax.rem(index // 2 + z_step, 4)
    core = lax.rem(index, 2)
    return 2 * z + (1 - core if other_core else core)


def squares_of(rows):
    wide = rows.astype(F32)
    total = None
    for lane in range(0, FEAT, HD):
        part = wide[:, lane : lane + HD]
        total = part * part if total is None else total + part * part
    return total


def weight_copies(refs, buffers, sems, blocks):
    copies = []
    for i, (z_step, other) in enumerate(blocks):
        rows = pl.ds(pl.multiple_of(block_index(z_step, other) * FEAT, FEAT), FEAT)
        copies.append(
            [
                pltpu.make_async_copy(ref.at[rows, :], buffer.at[i], sems.at[len(refs) * i + j])
                for j, (ref, buffer) in enumerate(zip(refs, buffers))
            ]
        )
    for group in copies:
        for copy in group:
            copy.start()
    return copies


EARLY = ((0, False), (0, True), (3, False), (3, True), (1, False), (1, True))
LATE = ((2, False), (2, True))


def early_kernel(*refs):
    count = len(EARLY)
    x_refs = refs[:count]
    wq_ref, wkv_ref, q_ref, kv_ref, sq_ref, wq_buf, wkv_buf, sems = refs[count:]
    copies = weight_copies((wq_ref, wkv_ref), (wq_buf, wkv_buf), sems, EARLY)
    for i in range(count):
        copies[i][0].wait()
        copies[i][1].wait()
        rows = x_refs[i][...]
        q_part = jnp.dot(rows, wq_buf[i], preferred_element_type=F32)
        kv_part = jnp.dot(rows, wkv_buf[i], preferred_element_type=F32)
        sq_part = squares_of(rows)
        if i == 0:
            q_ref[...] = q_part
            kv_ref[...] = kv_part
            sq_ref[...] = sq_part
        else:
            q_ref[...] += q_part
            kv_ref[...] += kv_part
            sq_ref[...] += sq_part


def project_early(blocks, w_query, w_keyval):
    rows = blocks[0].shape[0]
    count = len(EARLY)
    return pl.pallas_call(
        early_kernel,
        out_shape=[shape((rows, QW), F32), shape((rows, KVW), F32), shape((rows, HD), F32)],
        in_specs=[VMEM] * count + [HBM] * 2,
        out_specs=[VMEM] * 3,
        scratch_shapes=[
            pltpu.VMEM((count, FEAT, QW), BF16),
            pltpu.VMEM((count, FEAT, KVW), BF16),
            pltpu.SemaphoreType.DMA((2 * count,)),
        ],
        compiler_params=params(16),
        cost_estimate=cost(
            2 * rows * count * FEAT * (QW + KVW), count * FEAT * (QW + KVW + rows) * 2
        ),
        name="project_early",
    )(*blocks, w_query, w_keyval)


def turn(values, cosine, sine):
    return values * cosine + pltpu.roll(values, HD // 2, 1) * sine


def late_dot(x_refs, buffers, index):
    parts = [
        jnp.dot(ref[...], buffers[index], preferred_element_type=F32)
        for ref in x_refs[2 * index : 2 * index + 2]
    ]
    return jnp.concatenate(parts, axis=0)


def keyval_kernel(table_ref, *refs):
    x_refs = refs[:4]
    kv_in, sq_in, cos_ref, sin_ref, wkv_ref = refs[4:9]
    keys_ref, values_ref, inv_ref, send_ref, wkv_buf, sems = refs[9:]
    copies = weight_copies((wkv_ref,), (wkv_buf,), sems, LATE)
    squares = sq_in[...]
    for i in range(2):
        halves = [squares_of(ref[...]) for ref in x_refs[2 * i : 2 * i + 2]]
        squares += jnp.concatenate(halves, axis=0)
    mean = jnp.sum(squares, axis=1, keepdims=True) / D
    inv_norm = jnp.broadcast_to(lax.rsqrt(mean + 1e-05), (ROWS, HD))
    inv_ref[...] = inv_norm
    kv_sum = kv_in[...]
    for i in range(2):
        copies[i][0].wait()
        kv_sum += late_dot(x_refs, wkv_buf, i)
    keys = turn(kv_sum[:, :HD] * inv_norm, cos_ref[...], sin_ref[...]).astype(BF16)
    values = (kv_sum[:, HD:] * inv_norm).astype(BF16)
    keys_ref[...] = keys
    values_ref[:, :HD] = values
    values_ref[:, HD:] = jnp.ones((ROWS, HD), BF16)
    row = lax.broadcasted_iota(jnp.int32, (2 * PAGE, 2 * PAGE), 0)
    column = lax.broadcasted_iota(jnp.int32, (2 * PAGE, 2 * PAGE), 1)
    picker = (column == (row >> 1) + (row & 1) * PAGE).astype(BF16)
    for page in range(NEW_PAGES):
        rows = slice(page * PAGE, (page + 1) * PAGE)
        both = jnp.concatenate([keys[rows], values[rows]], axis=0)
        mixed = jnp.dot(picker, both, preferred_element_type=F32).astype(BF16)
        send_ref[table_ref[PUSH, page]] = mixed


def project_keyval(table, halves, kv_sum, squares, cosine, sine, w_keyval):
    return pl.pallas_call(
        keyval_kernel,
        out_shape=[
            shape((ROWS, HD), BF16),
            shape((ROWS, 2 * HD), BF16),
            shape((ROWS, HD), F32),
            shape((POOL * PUSH_CAP, 2 * PAGE, HD), BF16),
        ],
        in_specs=[SMEM] + [VMEM] * 8 + [HBM],
        out_specs=[VMEM] * 4,
        scratch_shapes=[pltpu.VMEM((2, FEAT, KVW), BF16), pltpu.SemaphoreType.DMA((2,))],
        compiler_params=params(12),
        cost_estimate=cost(2 * ROWS * 2 * FEAT * KVW, 2 * FEAT * (KVW + ROWS) * 2),
        name="project_keyval",
    )(table, *halves, kv_sum, squares, cosine, sine, w_keyval)


def dot_nt(a, b):
    return lax.dot_general(a, b, (((1,), (1,)), ((), ())), preferred_element_type=F32)


def attend_kernel(*refs):
    x_refs = refs[:4]
    q_in, inv_ref, cos_ref, sin_ref, wq_ref = refs[4:9]
    keys_ref, values_ref, own_keys_ref, own_values_ref, out_ref, wq_buf, q_buf, sems = refs[9:]
    copies = weight_copies((wq_ref,), (wq_buf,), sems, LATE)
    q_sum = q_in[...]
    for i in range(2):
        copies[i][0].wait()
        q_sum += late_dot(x_refs, wq_buf, i)
    inv_norm = inv_ref[...]
    for head in range(HEADS):
        part = q_sum[:, head * HD : (head + 1) * HD] * inv_norm
        q_buf[head] = turn(part, cos_ref[...], sin_ref[...]).astype(BF16)
    block = 128
    allowed = lax.broadcasted_iota(jnp.int32, (block, block), 0) >= lax.broadcasted_iota(
        jnp.int32, (block, block), 1
    )

    def one_head(head, _):
        lanes = pl.ds(pl.multiple_of(head * HD, HD), HD)
        for b in range(ROWS // block):
            rows = slice(b * block, (b + 1) * block)
            queries = q_buf[head, rows, :]
            scores = dot_nt(queries, keys_ref[...])
            own = dot_nt(queries, own_keys_ref[: (b + 1) * block, :])
            last = jnp.where(allowed, own[:, b * block :], -1e30)
            own = last if b == 0 else jnp.concatenate([own[:, : b * block], last], axis=1)
            top = jnp.maximum(
                jnp.max(scores, axis=1, keepdims=True), jnp.max(own, axis=1, keepdims=True)
            )
            weights = jnp.exp2((scores - top) * SCALE).astype(BF16)
            own_weights = jnp.exp2((own - top) * SCALE).astype(BF16)
            both = jnp.dot(weights, values_ref[...], preferred_element_type=F32)
            both += jnp.dot(
                own_weights, own_values_ref[: (b + 1) * block, :], preferred_element_type=F32
            )
            out_ref[rows, lanes] = (both[:, :HD] / both[:, HD:]).astype(BF16)
        return 0

    lax.fori_loop(0, HEADS, one_head, 0)


def attend(halves, q_sum, inv_norm, cosine, sine, w_query, keys, values, own_keys, own_values):
    return pl.pallas_call(
        attend_kernel,
        out_shape=shape((ROWS, QW), BF16),
        in_specs=[VMEM] * 8 + [HBM] + [VMEM] * 4,
        out_specs=VMEM,
        scratch_shapes=[
            pltpu.VMEM((2, FEAT, QW), BF16),
            pltpu.VMEM((HEADS, ROWS, HD), BF16),
            pltpu.SemaphoreType.DMA((2,)),
        ],
        compiler_params=params(28),
        cost_estimate=cost(2 * ROWS * (4 * 2560 * 512 + 2 * FEAT * QW), 8 * MIB),
        name="attend",
    )(*halves, q_sum, inv_norm, cosine, sine, w_query, keys, values, own_keys, own_values)


def place_kernel(table_ref, received_ref, out_ref):
    height = out_ref.shape[0]
    base = pl.program_id(0) * height
    for i in range(height):
        source = table_ref[PLACE, base + i]
        page = received_ref[jnp.maximum(source - 1, 0)]
        out_ref[i] = jnp.where(source > 0, page, jnp.zeros_like(page))


def place_pages(table, received):
    height = 8
    return pl.pallas_call(
        place_kernel,
        grid=(SLOTS // height,),
        out_shape=shape((SLOTS, 2 * PAGE, HD), BF16),
        in_specs=[SMEM, VMEM],
        out_specs=pl.BlockSpec((height, 2 * PAGE, HD), lambda i: (i, 0, 0)),
        compiler_params=params(8),
        cost_estimate=cost(0, 2 * MIB),
        name="place_pages",
    )(table, received)


def shift(values, step):
    pairs = [(i, ((i // 2 + step) % 4) * 2 + i % 2) for i in range(8)]
    return lax.ppermute(values, "tp", pairs)


def swap(values):
    return lax.ppermute(values, "tp", [(i, i ^ 1) for i in range(8)])


def rope_tables(row_count, offset):
    half_dim = HD // 2
    frequency = 500000.0 ** (-(jnp.arange(half_dim, dtype=F32) * (2.0 / HD)))
    place = (offset + jnp.arange(row_count, dtype=jnp.int32)).astype(F32)
    angles = place[:, None] * frequency[None, :]
    cosine, sine = jnp.cos(angles), jnp.sin(angles)
    return jnp.concatenate([cosine, cosine], 1), jnp.concatenate([-sine, sine], 1)


def exchange(values):
    return lax.all_to_all(values, "pool", split_axis=0, concat_axis=0, tiled=True)


def body(hidden, w_query, w_keyval, store, page_owner, page_slot, new_owner):
    half = ROWS // 2
    ahead, behind = shift(hidden, 1), shift(hidden, -1)
    table = make_table(page_owner, page_slot, new_owner)
    pages = exchange(gather_pages(table, store.reshape(64, 2 * PAGE, HD)))
    cosine, sine = rope_tables(ROWS, PAGES * PAGE)
    top, bottom = shift(ahead[:half], 1), shift(behind[half:], -1)
    blocks = (hidden, swap(hidden), ahead, swap(ahead), behind, swap(behind))
    q_sum, kv_sum, squares = project_early(blocks, w_query, w_keyval)
    keys, values = split_pages(table, pages)
    halves = (top, bottom, swap(top), swap(bottom))
    own_keys, own_values, inv_norm, send = project_keyval(
        table, halves, kv_sum, squares, cosine, sine, w_keyval
    )
    received = exchange(send)
    attended = attend(
        halves, q_sum, inv_norm, cosine, sine, w_query, keys, values, own_keys, own_values
    )
    placed = place_pages(table, received)
    return attended, placed.reshape(SLOTS, 1, PAGE, 2, HD)


def solution(mesh):
    in_specs = (
        P("pool", "tp"),
        P(None, "tp"),
        P(None, "tp"),
        P("pool", "tp", None, None, None),
        P(),
        P(),
        P(),
    )
    out_specs = (P("pool", "tp"), P("pool", "tp", None, None, None))
    return jax.shard_map(body, mesh=mesh, in_specs=in_specs, out_specs=out_specs, check_vma=False)
```

```python
import functools
import math

import jax
import jax.numpy as jnp
from jax import lax
from jax.experimental import pallas as pl
from jax.experimental.pallas import tpu as pltpu
from jax.sharding import PartitionSpec as P

D = 8192
HD = 128
PAGE = 64
CAP = 4
PUSH_CAP = 2
HEADS = 4
FEAT = 1024
QW = 512
KVW = 256
POOL = 16
PAGES = 32
NEW_PAGES = 8
SLOTS = 32
ROWS = 512
TAKE, PUSH, PLACE = 16, 17, 18
MIB = 1024 * 1024
SCALE = math.log2(math.e) / math.sqrt(HD)
F32 = jnp.float32
BF16 = jnp.bfloat16
ANY = pl.BlockSpec(memory_space=pl.ANY)
HBM = pl.BlockSpec(memory_space=pltpu.HBM)
VMEM = pl.BlockSpec(memory_space=pltpu.VMEM)
SMEM = pl.BlockSpec(memory_space=pltpu.SMEM)


def params(mib):
    return pltpu.CompilerParams(vmem_limit_bytes=mib * MIB)


def cost(flops, nbytes):
    return pl.CostEstimate(flops=flops, bytes_accessed=nbytes, transcendentals=0)


def hbm(array):
    return pltpu.with_memory_space_constraint(array, pltpu.HBM)


def shape(dims, dtype):
    return jax.ShapeDtypeStruct(dims, dtype)


def ranks_of(owners, lanes):
    ranks = jnp.zeros_like(owners)
    for j in range(owners.shape[1]):
        ranks += ((owners == owners[:, j : j + 1]) & (lanes > j)).astype(jnp.int32)
    return ranks


def table_kernel(page_owner_ref, page_slot_ref, new_owner_ref, out_ref):
    me = lax.axis_index("pool")
    out_ref[...] = jnp.zeros_like(out_ref)
    owners, slots = page_owner_ref[...], page_slot_ref[...]
    lanes = lax.broadcasted_iota(jnp.int32, owners.shape, 1)
    rows = lax.broadcasted_iota(jnp.int32, owners.shape, 0)
    ranks = ranks_of(owners, lanes)
    for k in range(CAP):
        chosen = jnp.where((owners == me) & (ranks == k), slots, 0)
        out_ref[:POOL, k : k + 1] = jnp.sum(chosen, axis=1, keepdims=True)
    mine = jnp.where(rows == me, owners * CAP + ranks, 0)
    out_ref[TAKE : TAKE + 1, :PAGES] = jnp.sum(mine, axis=0, keepdims=True)
    targets = new_owner_ref[...]
    target_lanes = lax.broadcasted_iota(jnp.int32, targets.shape, 1)
    target_rows = lax.broadcasted_iota(jnp.int32, targets.shape, 0)
    ranks = ranks_of(targets, target_lanes)
    mine = jnp.where(target_rows == me, targets * PUSH_CAP + ranks, 0)
    out_ref[PUSH : PUSH + 1, :NEW_PAGES] = jnp.sum(mine, axis=0, keepdims=True)
    kept = (targets == me).astype(jnp.int32)
    slot = jnp.zeros_like(targets)
    for j in range(NEW_PAGES):
        slot += jnp.where(target_lanes > j, kept[:, j : j + 1], 0)
    in_row = jnp.sum(kept, axis=1, keepdims=True)
    for r in range(POOL):
        slot += jnp.where(target_rows > r, in_row[r : r + 1, :], 0)
    source = jnp.zeros((POOL, SLOTS), jnp.int32)
    slot_lanes = lax.broadcasted_iota(jnp.int32, source.shape, 1)
    slot_rows = lax.broadcasted_iota(jnp.int32, source.shape, 0)
    for j in range(NEW_PAGES):
        hit = (kept[:, j : j + 1] > 0) & (slot[:, j : j + 1] == slot_lanes)
        source += jnp.where(hit, slot_rows * PUSH_CAP + ranks[:, j : j + 1] + 1, 0)
    out_ref[PLACE : PLACE + 1, :SLOTS] = jnp.sum(source, axis=0, keepdims=True)


def make_table(page_owner, page_slot, new_owner):
    return pl.pallas_call(
        table_kernel,
        out_shape=shape((24, HD), jnp.int32),
        in_specs=[VMEM] * 3,
        out_specs=VMEM,
        compiler_params=params(4),
        cost_estimate=cost(0, 16384),
        name="make_table",
    )(page_owner, page_slot, new_owner)


def gather_kernel(table_ref, store_ref, out_ref):
    def one(index, _):
        out_ref[index] = store_ref[table_ref[index >> 2, index & 3]]
        return 0

    lax.fori_loop(0, POOL * CAP, one, 0, unroll=8)


def gather_pages(table, store):
    return pl.pallas_call(
        gather_kernel,
        out_shape=shape((POOL * CAP, 2 * PAGE, HD), BF16),
        in_specs=[SMEM, VMEM],
        out_specs=VMEM,
        compiler_params=params(8),
        cost_estimate=cost(0, 4 * MIB),
        name="gather_pages",
    )(table, store)


def split_kernel(table_ref, pages_ref, keys_ref, values_ref):
    row = lax.broadcasted_iota(jnp.int32, (2 * PAGE, 2 * PAGE), 0)
    column = lax.broadcasted_iota(jnp.int32, (2 * PAGE, 2 * PAGE), 1)
    wanted = jnp.where(row < PAGE, 2 * row, 2 * (row - PAGE) + 1)
    picker = (column == wanted).astype(BF16)
    values_ref[:, HD:] = jnp.ones((PAGES * PAGE, HD), BF16)
    for page in range(PAGES):
        both = jnp.dot(picker, pages_ref[table_ref[TAKE, page]], preferred_element_type=F32)
        rows = pl.ds(page * PAGE, PAGE)
        keys_ref[rows, :] = both[:PAGE].astype(BF16)
        values_ref[rows, :HD] = both[PAGE:].astype(BF16)


def split_pages(table, pages):
    return pl.pallas_call(
        split_kernel,
        out_shape=[
            shape((PAGES * PAGE, HD), BF16),
            shape((PAGES * PAGE, 2 * HD), BF16),
        ],
        in_specs=[SMEM, VMEM],
        out_specs=[VMEM, VMEM],
        compiler_params=params(8),
        cost_estimate=cost(2 * 2048 * 128 * 256, 4 * MIB),
        name="split_pages",
    )(table, pages)


def block_index(z_step, other_core):
    index = lax.axis_index("tp")
    z = lax.rem(index // 2 + z_step, 4)
    core = lax.rem(index, 2)
    return 2 * z + (1 - core if other_core else core)


def squares_of(rows):
    wide = rows.astype(F32)
    total = None
    for lane in range(0, FEAT, HD):
        part = wide[:, lane : lane + HD]
        total = part * part if total is None else total + part * part
    return total


def weight_copies(refs, buffers, sems, blocks):
    copies = []
    for i, (z_step, other) in enumerate(blocks):
        rows = pl.ds(pl.multiple_of(block_index(z_step, other) * FEAT, FEAT), FEAT)
        copies.append(
            [
                pltpu.make_async_copy(ref.at[rows, :], buffer.at[i], sems.at[len(refs) * i + j])
                for j, (ref, buffer) in enumerate(zip(refs, buffers))
            ]
        )
    for group in copies:
        for copy in group:
            copy.start()
    return copies


EARLY = ((0, True), (3, False), (3, True), (1, False), (1, True), (0, False))
LATE = ((2, False), (2, True))
TILE = 128


def early_kernel(*refs):
    count = len(EARLY)
    sources = (refs[0:1], refs[1:3], refs[3:5], refs[5:7], refs[7:9], None)
    hidden_ref, wq_ref, wkv_ref = refs[9:12]
    q_ref, kv_ref, sq_ref, late_q, late_kv, x_buf, wq_buf, wkv_buf, sems, late_sems, x_sem = refs[12:]
    x_copy = pltpu.make_async_copy(hidden_ref, x_buf, x_sem)
    copies = weight_copies((wq_ref, wkv_ref), (wq_buf, wkv_buf), sems, EARLY)
    x_copy.start()
    late = weight_copies((wq_ref, wkv_ref), (late_q, late_kv), late_sems, LATE)
    for i in range(count):
        copies[i][0].wait()
        copies[i][1].wait()
        if i == count - 1:
            x_copy.wait()
        group = sources[i] or (x_buf,)
        for r in range(0, ROWS, TILE):
            height = ROWS // len(group)
            start = r % height
            x = group[r // height][start : start + TILE, :]
            rows = slice(r, r + TILE)
            q_part = jnp.dot(x, wq_buf[i], preferred_element_type=F32)
            kv_part = jnp.dot(x, wkv_buf[i], preferred_element_type=F32)
            sq_part = squares_of(x)
            if i == 0:
                q_ref[rows, :] = q_part
                kv_ref[rows, :] = kv_part
                sq_ref[rows, :] = sq_part
            else:
                q_ref[rows, :] += q_part
                kv_ref[rows, :] += kv_part
                sq_ref[rows, :] += sq_part
    for group in late:
        for copy in group:
            copy.wait()


def project_early(arrays, hidden, w_query, w_keyval):
    count = len(EARLY)
    return pl.pallas_call(
        early_kernel,
        out_shape=[
            shape((ROWS, QW), F32),
            shape((ROWS, KVW), F32),
            shape((ROWS, HD), F32),
            shape((2, FEAT, QW), BF16),
            shape((2, FEAT, KVW), BF16),
        ],
        in_specs=[VMEM] * len(arrays) + [HBM] * 3,
        out_specs=[VMEM] * 5,
        scratch_shapes=[
            pltpu.VMEM((ROWS, FEAT), BF16),
            pltpu.VMEM((count, FEAT, QW), BF16),
            pltpu.VMEM((count, FEAT, KVW), BF16),
            pltpu.SemaphoreType.DMA((2 * count,)),
            pltpu.SemaphoreType.DMA((4,)),
            pltpu.SemaphoreType.DMA,
        ],
        compiler_params=params(16),
        cost_estimate=cost(
            2 * ROWS * count * FEAT * (QW + KVW), count * FEAT * (QW + KVW + ROWS) * 2
        ),
        name="project_early",
    )(*arrays, hbm(hidden), hbm(w_query), hbm(w_keyval))


def after_kernel(*refs):
    pass


def after(token, *arrays):
    count = len(arrays)
    return pl.pallas_call(
        after_kernel,
        out_shape=[shape(x.shape, x.dtype) for x in arrays],
        in_specs=[ANY] * (count + 1),
        out_specs=[ANY] * count,
        input_output_aliases={i + 1: i for i in range(count)},
        compiler_params=params(1),
        cost_estimate=cost(0, 1024),
        name="after",
    )(token, *arrays)


def turn(values, cosine, sine):
    return values * cosine + pltpu.roll(values, HD // 2, 1) * sine


def late_kernel(table_ref, *refs):
    x_refs = (refs[0:2], refs[2:4])
    q_in, kv_in, sq_in, late_q, late_kv, cos_ref, sin_ref = refs[4:11]
    q_ref, keys_ref, values_ref, send_ref = refs[11:]
    row = lax.broadcasted_iota(jnp.int32, (2 * PAGE, 2 * PAGE), 0)
    column = lax.broadcasted_iota(jnp.int32, (2 * PAGE, 2 * PAGE), 1)
    picker = (column == (row >> 1) + (row & 1) * PAGE).astype(BF16)
    half = ROWS // 2
    for r in range(0, ROWS, TILE):
        rows = slice(r, r + TILE)
        start = r % half
        x = [x_refs[i][r // half][start : start + TILE, :] for i in range(2)]
        squares = sq_in[rows, :] + squares_of(x[0]) + squares_of(x[1])
        mean = jnp.sum(squares, axis=1, keepdims=True) / D
        inv_norm = jnp.broadcast_to(lax.rsqrt(mean + 1e-05), (TILE, HD))
        kv_sum = kv_in[rows, :]
        q_sum = q_in[rows, :]
        for i in range(2):
            kv_sum += jnp.dot(x[i], late_kv[i], preferred_element_type=F32)
            q_sum += jnp.dot(x[i], late_q[i], preferred_element_type=F32)
        cosine, sine = cos_ref[rows, :], sin_ref[rows, :]
        for head in range(HEADS):
            part = q_sum[:, head * HD : (head + 1) * HD] * inv_norm
            q_ref[head, rows, :] = turn(part, cosine, sine).astype(BF16)
        keys = turn(kv_sum[:, :HD] * inv_norm, cosine, sine).astype(BF16)
        values = (kv_sum[:, HD:] * inv_norm).astype(BF16)
        keys_ref[rows, :] = keys
        values_ref[rows, :HD] = values
        values_ref[rows, HD:] = jnp.ones((TILE, HD), BF16)
        for p in range(0, TILE, PAGE):
            both = jnp.concatenate([keys[p : p + PAGE], values[p : p + PAGE]], axis=0)
            mixed = jnp.dot(picker, both, preferred_element_type=F32).astype(BF16)
            send_ref[table_ref[PUSH, (r + p) // PAGE]] = mixed


def project_late(table, halves, sums, late_weights, cosine, sine):
    return pl.pallas_call(
        late_kernel,
        out_shape=[
            pltpu.HBM((HEADS, ROWS, HD), BF16),
            pltpu.HBM((ROWS, HD), BF16),
            pltpu.HBM((ROWS, 2 * HD), BF16),
            pltpu.HBM((POOL * PUSH_CAP, 2 * PAGE, HD), BF16),
        ],
        in_specs=[SMEM] + [VMEM] * 11,
        out_specs=[VMEM] * 4,
        compiler_params=params(12),
        cost_estimate=cost(2 * ROWS * 2 * FEAT * (QW + KVW), 2 * FEAT * (QW + KVW + ROWS) * 2),
        name="project_late",
    )(table, *halves, *sums, *late_weights, cosine, sine)


def dot_nt(a, b):
    return lax.dot_general(a, b, (((1,), (1,)), ((), ())), preferred_element_type=F32)


def attend_kernel(q_ref, own_keys_ref, own_values_ref, keys_ref, values_ref, out_ref, *scratch):
    q_buf, own_keys, own_values, sems = scratch
    copies = [
        pltpu.make_async_copy(source, target, sems.at[i])
        for i, (source, target) in enumerate(
            ((q_ref, q_buf), (own_keys_ref, own_keys), (own_values_ref, own_values))
        )
    ]
    for copy in copies:
        copy.start()
    for copy in copies:
        copy.wait()
    block = 256
    allowed = lax.broadcasted_iota(jnp.int32, (block, block), 0) >= lax.broadcasted_iota(
        jnp.int32, (block, block), 1
    )
    for head in range(HEADS):
        lanes = slice(head * HD, (head + 1) * HD)
        for b in range(ROWS // block):
            rows = slice(b * block, (b + 1) * block)
            queries = q_buf[head, rows, :]
            scores = dot_nt(queries, keys_ref[...])
            own = dot_nt(queries, own_keys[: (b + 1) * block, :])
            last = jnp.where(allowed, own[:, b * block :], -1e30)
            own = last if b == 0 else jnp.concatenate([own[:, : b * block], last], axis=1)
            top = jnp.maximum(
                jnp.max(scores, axis=1, keepdims=True), jnp.max(own, axis=1, keepdims=True)
            )
            weights = jnp.exp2((scores - top) * SCALE).astype(BF16)
            own_weights = jnp.exp2((own - top) * SCALE).astype(BF16)
            both = jnp.dot(weights, values_ref[...], preferred_element_type=F32)
            both += jnp.dot(
                own_weights, own_values[: (b + 1) * block, :], preferred_element_type=F32
            )
            out_ref[rows, lanes] = (both[:, :HD] / both[:, HD:]).astype(BF16)


def attend(queries, own_keys, own_values, keys, values):
    return pl.pallas_call(
        attend_kernel,
        out_shape=shape((ROWS, QW), BF16),
        in_specs=[HBM] * 3 + [VMEM] * 2,
        out_specs=VMEM,
        scratch_shapes=[
            pltpu.VMEM((HEADS, ROWS, HD), BF16),
            pltpu.VMEM((ROWS, HD), BF16),
            pltpu.VMEM((ROWS, 2 * HD), BF16),
            pltpu.SemaphoreType.DMA((3,)),
        ],
        compiler_params=params(40),
        cost_estimate=cost(2 * ROWS * 4 * 2560 * 512, 8 * MIB),
        name="attend",
    )(hbm(queries), hbm(own_keys), hbm(own_values), keys, values)


def place_kernel(table_ref, received_ref, out_ref):
    height = out_ref.shape[0]
    base = pl.program_id(0) * height
    for i in range(height):
        source = table_ref[PLACE, base + i]
        page = received_ref[jnp.maximum(source - 1, 0)]
        out_ref[i] = jnp.where(source > 0, page, jnp.zeros_like(page))


def place_pages(table, received):
    height = 8
    return pl.pallas_call(
        place_kernel,
        grid=(SLOTS // height,),
        out_shape=shape((SLOTS, 2 * PAGE, HD), BF16),
        in_specs=[SMEM, VMEM],
        out_specs=pl.BlockSpec((height, 2 * PAGE, HD), lambda i: (i, 0, 0)),
        compiler_params=params(8),
        cost_estimate=cost(0, 2 * MIB),
        name="place_pages",
    )(table, received)


def shift(values, step):
    pairs = [(i, ((i // 2 + step) % 4) * 2 + i % 2) for i in range(8)]
    return lax.ppermute(values, "tp", pairs)


def swap(values):
    return lax.ppermute(values, "tp", [(i, i ^ 1) for i in range(8)])


def rope_tables(row_count, offset):
    half_dim = HD // 2
    frequency = 500000.0 ** (-(jnp.arange(half_dim, dtype=F32) * (2.0 / HD)))
    place = (offset + jnp.arange(row_count, dtype=jnp.int32)).astype(F32)
    angles = place[:, None] * frequency[None, :]
    cosine, sine = jnp.cos(angles), jnp.sin(angles)
    return jnp.concatenate([cosine, cosine], 1), jnp.concatenate([-sine, sine], 1)


def exchange(values):
    return lax.all_to_all(values, "pool", split_axis=0, concat_axis=0, tiled=True)


def body(hidden, w_query, w_keyval, store, page_owner, page_slot, new_owner):
    half = ROWS // 2
    upper, lower = hidden[:half], hidden[half:]
    ahead_upper, behind_lower = shift(upper, 1), shift(lower, -1)
    ahead_lower, behind_upper = shift(lower, 1), shift(upper, -1)
    sibling = swap(hidden)
    table = make_table(page_owner, page_slot, new_owner)
    pages = exchange(gather_pages(table, store.reshape(64, 2 * PAGE, HD)))
    cosine, sine = rope_tables(ROWS, PAGES * PAGE)
    far = (shift(ahead_upper, 1), shift(behind_lower, -1))
    ahead, behind = (ahead_upper, ahead_lower), (behind_upper, behind_lower)
    arrays = (
        sibling,
        *ahead,
        *[swap(x) for x in ahead],
        *behind,
        *[swap(x) for x in behind],
    )
    early = project_early(arrays, hidden, w_query, w_keyval)
    far = after(early[2], *far)
    halves = (*far, *[swap(x) for x in far])
    queries, own_keys, own_values, send = project_late(
        table, halves, early[:3], early[3:], cosine, sine
    )
    received = exchange(send)
    keys, values = split_pages(table, pages)
    attended = attend(queries, own_keys, own_values, keys, values)
    placed = place_pages(table, received)
    return attended, placed.reshape(SLOTS, 1, PAGE, 2, HD)


def solution(mesh):
    in_specs = (
        P("pool", "tp"),
        P(None, "tp"),
        P(None, "tp"),
        P("pool", "tp", None, None, None),
        P(),
        P(),
        P(),
    )
    out_specs = (P("pool", "tp"), P("pool", "tp", None, None, None))
    return jax.shard_map(body, mesh=mesh, in_specs=in_specs, out_specs=out_specs, check_vma=False)
```

```python
import functools
import math

import jax
import jax.numpy as jnp
from jax import lax
from jax.experimental import pallas as pl
from jax.experimental.pallas import tpu as pltpu
from jax.sharding import PartitionSpec as P

D = 8192
HD = 128
PAGE = 64
CAP = 4
PUSH_CAP = 2
HEADS = 4
FEAT = 1024
QW = 512
KVW = 256
POOL = 16
PAGES = 32
NEW_PAGES = 8
SLOTS = 32
ROWS = 512
TAKE, PUSH, PLACE = 16, 17, 18
MIB = 1024 * 1024
SCALE = math.log2(math.e) / math.sqrt(HD)
F32 = jnp.float32
BF16 = jnp.bfloat16
ANY = pl.BlockSpec(memory_space=pl.ANY)
HBM = pl.BlockSpec(memory_space=pltpu.HBM)
VMEM = pl.BlockSpec(memory_space=pltpu.VMEM)
SMEM = pl.BlockSpec(memory_space=pltpu.SMEM)


def params(mib):
    return pltpu.CompilerParams(vmem_limit_bytes=mib * MIB)


def cost(flops, nbytes):
    return pl.CostEstimate(flops=flops, bytes_accessed=nbytes, transcendentals=0)


def hbm(array):
    return pltpu.with_memory_space_constraint(array, pltpu.HBM)


def shape(dims, dtype):
    return jax.ShapeDtypeStruct(dims, dtype)


def ranks_of(owners, lanes):
    ranks = jnp.zeros_like(owners)
    for j in range(owners.shape[1]):
        ranks += ((owners == owners[:, j : j + 1]) & (lanes > j)).astype(jnp.int32)
    return ranks


def table_kernel(page_owner_ref, page_slot_ref, new_owner_ref, out_ref):
    me = lax.axis_index("pool")
    out_ref[...] = jnp.zeros_like(out_ref)
    owners, slots = page_owner_ref[...], page_slot_ref[...]
    lanes = lax.broadcasted_iota(jnp.int32, owners.shape, 1)
    rows = lax.broadcasted_iota(jnp.int32, owners.shape, 0)
    ranks = ranks_of(owners, lanes)
    for k in range(CAP):
        chosen = jnp.where((owners == me) & (ranks == k), slots, 0)
        out_ref[:POOL, k : k + 1] = jnp.sum(chosen, axis=1, keepdims=True)
    mine = jnp.where(rows == me, owners * CAP + ranks, 0)
    out_ref[TAKE : TAKE + 1, :PAGES] = jnp.sum(mine, axis=0, keepdims=True)
    targets = new_owner_ref[...]
    target_lanes = lax.broadcasted_iota(jnp.int32, targets.shape, 1)
    target_rows = lax.broadcasted_iota(jnp.int32, targets.shape, 0)
    ranks = ranks_of(targets, target_lanes)
    mine = jnp.where(target_rows == me, targets * PUSH_CAP + ranks, 0)
    out_ref[PUSH : PUSH + 1, :NEW_PAGES] = jnp.sum(mine, axis=0, keepdims=True)
    kept = (targets == me).astype(jnp.int32)
    slot = jnp.zeros_like(targets)
    for j in range(NEW_PAGES):
        slot += jnp.where(target_lanes > j, kept[:, j : j + 1], 0)
    in_row = jnp.sum(kept, axis=1, keepdims=True)
    for r in range(POOL):
        slot += jnp.where(target_rows > r, in_row[r : r + 1, :], 0)
    source = jnp.zeros((POOL, SLOTS), jnp.int32)
    slot_lanes = lax.broadcasted_iota(jnp.int32, source.shape, 1)
    slot_rows = lax.broadcasted_iota(jnp.int32, source.shape, 0)
    for j in range(NEW_PAGES):
        hit = (kept[:, j : j + 1] > 0) & (slot[:, j : j + 1] == slot_lanes)
        source += jnp.where(hit, slot_rows * PUSH_CAP + ranks[:, j : j + 1] + 1, 0)
    out_ref[PLACE : PLACE + 1, :SLOTS] = jnp.sum(source, axis=0, keepdims=True)


def make_table(page_owner, page_slot, new_owner):
    return pl.pallas_call(
        table_kernel,
        out_shape=shape((24, HD), jnp.int32),
        in_specs=[VMEM] * 3,
        out_specs=VMEM,
        compiler_params=params(4),
        cost_estimate=cost(0, 16384),
        name="make_table",
    )(page_owner, page_slot, new_owner)


def gather_kernel(table_ref, store_ref, out_ref):
    def one(index, _):
        out_ref[index] = store_ref[table_ref[index >> 2, index & 3]]
        return 0

    lax.fori_loop(0, POOL * CAP, one, 0, unroll=8)


def gather_pages(table, store):
    return pl.pallas_call(
        gather_kernel,
        out_shape=shape((POOL * CAP, 2 * PAGE, HD), BF16),
        in_specs=[SMEM, VMEM],
        out_specs=VMEM,
        compiler_params=params(8),
        cost_estimate=cost(0, 4 * MIB),
        name="gather_pages",
    )(table, store)


def split_kernel(table_ref, pages_ref, keys_ref, values_ref):
    row = lax.broadcasted_iota(jnp.int32, (2 * PAGE, 2 * PAGE), 0)
    column = lax.broadcasted_iota(jnp.int32, (2 * PAGE, 2 * PAGE), 1)
    wanted = jnp.where(row < PAGE, 2 * row, 2 * (row - PAGE) + 1)
    picker = (column == wanted).astype(BF16)
    values_ref[:, HD:] = jnp.ones((PAGES * PAGE, HD), BF16)
    for page in range(PAGES):
        both = jnp.dot(picker, pages_ref[table_ref[TAKE, page]], preferred_element_type=F32)
        rows = pl.ds(page * PAGE, PAGE)
        keys_ref[rows, :] = both[:PAGE].astype(BF16)
        values_ref[rows, :HD] = both[PAGE:].astype(BF16)


def split_pages(table, pages):
    return pl.pallas_call(
        split_kernel,
        out_shape=[
            shape((PAGES * PAGE, HD), BF16),
            shape((PAGES * PAGE, 2 * HD), BF16),
        ],
        in_specs=[SMEM, VMEM],
        out_specs=[VMEM, VMEM],
        compiler_params=params(8),
        cost_estimate=cost(2 * 2048 * 128 * 256, 4 * MIB),
        name="split_pages",
    )(table, pages)


def block_index(steps, other_core):
    index = lax.axis_index("tp")
    core = lax.rem(index, 2)
    if other_core:
        core = 1 - core
    z = lax.rem(index // 2 + jnp.where(core == 0, steps[0], steps[1]), 4)
    return 2 * z + core


def squares_of(rows):
    wide = rows.astype(F32)
    total = None
    for lane in range(0, FEAT, HD):
        part = wide[:, lane : lane + HD]
        total = part * part if total is None else total + part * part
    return total


def weight_copies(refs, buffers, sems, blocks):
    copies = []
    for i, (steps, other) in enumerate(blocks):
        rows = pl.ds(pl.multiple_of(block_index(steps, other) * FEAT, FEAT), FEAT)
        copies.append(
            [
                pltpu.make_async_copy(ref.at[rows, :], buffer.at[i], sems.at[len(refs) * i + j])
                for j, (ref, buffer) in enumerate(zip(refs, buffers))
            ]
        )
    for group in copies:
        for copy in group:
            copy.start()
    return copies


OWN, NEAR, BACK, FAR = (0, 0), (3, 1), (1, 3), (2, 2)
EARLY = ((OWN, True), (NEAR, False), (NEAR, True), (BACK, False), (BACK, True), (OWN, False))
LATE = ((FAR, False), (FAR, True))
TILE = 128


def early_kernel(*refs):
    count = len(EARLY)
    hidden_ref, wq_ref, wkv_ref = refs[5:8]
    q_ref, kv_ref, sq_ref, late_q, late_kv, x_buf, wq_buf, wkv_buf, sems, late_sems, x_sem = refs[8:]
    sources = (*refs[:5], x_buf)
    x_copy = pltpu.make_async_copy(hidden_ref, x_buf, x_sem)
    copies = weight_copies((wq_ref, wkv_ref), (wq_buf, wkv_buf), sems, EARLY)
    x_copy.start()
    late = weight_copies((wq_ref, wkv_ref), (late_q, late_kv), late_sems, LATE)
    for i in range(count):
        copies[i][0].wait()
        copies[i][1].wait()
        if i == count - 1:
            x_copy.wait()
        for r in range(0, ROWS, TILE):
            rows = slice(r, r + TILE)
            x = sources[i][rows, :]
            q_part = jnp.dot(x, wq_buf[i], preferred_element_type=F32)
            kv_part = jnp.dot(x, wkv_buf[i], preferred_element_type=F32)
            sq_part = squares_of(x)
            if i == 0:
                q_ref[rows, :] = q_part
                kv_ref[rows, :] = kv_part
                sq_ref[rows, :] = sq_part
            else:
                q_ref[rows, :] += q_part
                kv_ref[rows, :] += kv_part
                sq_ref[rows, :] += sq_part
    for group in late:
        for copy in group:
            copy.wait()


def project_early(arrays, hidden, w_query, w_keyval):
    count = len(EARLY)
    return pl.pallas_call(
        early_kernel,
        out_shape=[
            shape((ROWS, QW), F32),
            shape((ROWS, KVW), F32),
            shape((ROWS, HD), F32),
            shape((2, FEAT, QW), BF16),
            shape((2, FEAT, KVW), BF16),
        ],
        in_specs=[VMEM] * len(arrays) + [HBM] * 3,
        out_specs=[VMEM] * 5,
        scratch_shapes=[
            pltpu.VMEM((ROWS, FEAT), BF16),
            pltpu.VMEM((count, FEAT, QW), BF16),
            pltpu.VMEM((count, FEAT, KVW), BF16),
            pltpu.SemaphoreType.DMA((2 * count,)),
            pltpu.SemaphoreType.DMA((4,)),
            pltpu.SemaphoreType.DMA,
        ],
        compiler_params=params(16),
        cost_estimate=cost(0, 1),
        name="project_early",
    )(*arrays, hbm(hidden), hbm(w_query), hbm(w_keyval))


def after_kernel(*refs):
    pass


def after(tokens, *arrays):
    count, skip = len(arrays), len(tokens)
    return pl.pallas_call(
        after_kernel,
        out_shape=[shape(x.shape, x.dtype) for x in arrays],
        in_specs=[ANY] * (count + skip),
        out_specs=[ANY] * count,
        input_output_aliases={i + skip: i for i in range(count)},
        compiler_params=params(1),
        cost_estimate=cost(0, 1024),
        name="after",
    )(*tokens, *arrays)


def turn(values, cosine, sine):
    return values * cosine + pltpu.roll(values, HD // 2, 1) * sine


def late_kernel(table_ref, *refs):
    x_refs = refs[:2]
    q_in, kv_in, sq_in, late_q, late_kv, cos_ref, sin_ref = refs[2:9]
    q_ref, keys_ref, values_ref, send_ref = refs[9:]
    row = lax.broadcasted_iota(jnp.int32, (2 * PAGE, 2 * PAGE), 0)
    column = lax.broadcasted_iota(jnp.int32, (2 * PAGE, 2 * PAGE), 1)
    picker = (column == (row >> 1) + (row & 1) * PAGE).astype(BF16)
    for r in range(0, ROWS, TILE):
        rows = slice(r, r + TILE)
        x = [ref[rows, :] for ref in x_refs]
        squares = sq_in[rows, :] + squares_of(x[0]) + squares_of(x[1])
        mean = jnp.sum(squares, axis=1, keepdims=True) / D
        inv_norm = jnp.broadcast_to(lax.rsqrt(mean + 1e-05), (TILE, HD))
        kv_sum = kv_in[rows, :]
        q_sum = q_in[rows, :]
        for i in range(2):
            kv_sum += jnp.dot(x[i], late_kv[i], preferred_element_type=F32)
            q_sum += jnp.dot(x[i], late_q[i], preferred_element_type=F32)
        cosine, sine = cos_ref[rows, :], sin_ref[rows, :]
        for head in range(HEADS):
            part = q_sum[:, head * HD : (head + 1) * HD] * inv_norm
            q_ref[head, rows, :] = turn(part, cosine, sine).astype(BF16)
        keys = turn(kv_sum[:, :HD] * inv_norm, cosine, sine).astype(BF16)
        values = (kv_sum[:, HD:] * inv_norm).astype(BF16)
        keys_ref[rows, :] = keys
        values_ref[rows, :HD] = values
        values_ref[rows, HD:] = jnp.ones((TILE, HD), BF16)
        for p in range(0, TILE, PAGE):
            both = jnp.concatenate([keys[p : p + PAGE], values[p : p + PAGE]], axis=0)
            mixed = jnp.dot(picker, both, preferred_element_type=F32).astype(BF16)
            send_ref[table_ref[PUSH, (r + p) // PAGE]] = mixed


def project_late(table, blocks, sums, late_weights, cosine, sine):
    return pl.pallas_call(
        late_kernel,
        out_shape=[
            pltpu.HBM((HEADS, ROWS, HD), BF16),
            pltpu.HBM((ROWS, HD), BF16),
            pltpu.HBM((ROWS, 2 * HD), BF16),
            pltpu.HBM((POOL * PUSH_CAP, 2 * PAGE, HD), BF16),
        ],
        in_specs=[SMEM] + [VMEM] * 9,
        out_specs=[VMEM] * 4,
        compiler_params=params(12),
        cost_estimate=cost(0, 1),
        name="project_late",
    )(table, *blocks, *sums, *late_weights, cosine, sine)


def dot_nt(a, b):
    return lax.dot_general(a, b, (((1,), (1,)), ((), ())), preferred_element_type=F32)


def attend_kernel(q_ref, own_keys_ref, own_values_ref, keys_ref, values_ref, out_ref, *scratch):
    q_buf, own_keys, own_values, sems = scratch
    copies = [
        pltpu.make_async_copy(source, target, sems.at[i])
        for i, (source, target) in enumerate(
            ((q_ref, q_buf), (own_keys_ref, own_keys), (own_values_ref, own_values))
        )
    ]
    for copy in copies:
        copy.start()
    for copy in copies:
        copy.wait()
    block = 256
    allowed = lax.broadcasted_iota(jnp.int32, (block, block), 0) >= lax.broadcasted_iota(
        jnp.int32, (block, block), 1
    )
    for head in range(HEADS):
        lanes = slice(head * HD, (head + 1) * HD)
        for b in range(ROWS // block):
            rows = slice(b * block, (b + 1) * block)
            queries = q_buf[head, rows, :]
            own = dot_nt(queries, own_keys[: (b + 1) * block, :])
            diagonal = jnp.where(allowed, own[:, b * block :], -1e30)
            parts = [(diagonal, own_values[rows, :])]
            if b:
                parts.append((own[:, : b * block], own_values[: b * block, :]))
            parts.append((dot_nt(queries, keys_ref[...]), values_ref[...]))
            tops = [jnp.max(scores, axis=1, keepdims=True) for scores, _ in parts]
            top = functools.reduce(jnp.maximum, tops)
            both = jnp.zeros((block, 2 * HD), F32)
            for scores, held in parts:
                weights = jnp.exp2((scores - top) * SCALE).astype(BF16)
                both += jnp.dot(weights, held, preferred_element_type=F32)
            out_ref[rows, lanes] = (both[:, :HD] / both[:, HD:]).astype(BF16)


def attend(queries, own_keys, own_values, keys, values):
    return pl.pallas_call(
        attend_kernel,
        out_shape=shape((ROWS, QW), BF16),
        in_specs=[HBM] * 3 + [VMEM] * 2,
        out_specs=VMEM,
        scratch_shapes=[
            pltpu.VMEM((HEADS, ROWS, HD), BF16),
            pltpu.VMEM((ROWS, HD), BF16),
            pltpu.VMEM((ROWS, 2 * HD), BF16),
            pltpu.SemaphoreType.DMA((3,)),
        ],
        compiler_params=params(40),
        cost_estimate=cost(2 * ROWS * 4 * 2560 * 512, 8 * MIB),
        name="attend",
    )(hbm(queries), hbm(own_keys), hbm(own_values), keys, values)


def place_kernel(table_ref, received_ref, out_ref, buffer, sems):
    group = 4
    copies = []
    for i in range(SLOTS):
        source = table_ref[PLACE, i]
        page = received_ref[jnp.maximum(source - 1, 0)]
        buffer[i] = jnp.where(source > 0, page, jnp.zeros_like(page))
        if i % group == group - 1:
            slots = pl.ds(i + 1 - group, group)
            copy = pltpu.make_async_copy(
                buffer.at[slots], out_ref.at[slots], sems.at[i // group]
            )
            copy.start()
            copies.append(copy)
    for copy in copies:
        copy.wait()


def place_pages(table, received):
    return pl.pallas_call(
        place_kernel,
        out_shape=pltpu.HBM((SLOTS, 2 * PAGE, HD), BF16),
        in_specs=[SMEM, VMEM],
        out_specs=HBM,
        scratch_shapes=[
            pltpu.VMEM((SLOTS, 2 * PAGE, HD), BF16),
            pltpu.SemaphoreType.DMA((SLOTS // 4,)),
        ],
        compiler_params=params(8),
        cost_estimate=cost(0, 2 * MIB),
        name="place_pages",
    )(table, received)


def shift(values, steps):
    pairs = [(i, ((i // 2 + steps[i % 2]) % 4) * 2 + i % 2) for i in range(8)]
    return lax.ppermute(values, "tp", pairs)


def swap(values):
    return lax.ppermute(values, "tp", [(i, i ^ 1) for i in range(8)])


def rope_tables(row_count, offset):
    half_dim = HD // 2
    frequency = 500000.0 ** (-(jnp.arange(half_dim, dtype=F32) * (2.0 / HD)))
    place = (offset + jnp.arange(row_count, dtype=jnp.int32)).astype(F32)
    angles = place[:, None] * frequency[None, :]
    cosine, sine = jnp.cos(angles), jnp.sin(angles)
    return jnp.concatenate([cosine, cosine], 1), jnp.concatenate([-sine, sine], 1)


def exchange(values):
    return lax.all_to_all(values, "pool", split_axis=0, concat_axis=0, tiled=True)


def body(hidden, w_query, w_keyval, store, page_owner, page_slot, new_owner):
    near, back = shift(hidden, (1, -1)), shift(hidden, (-1, 1))
    far = shift(near, (1, -1))
    table = make_table(page_owner, page_slot, new_owner)
    pages = exchange(gather_pages(table, store.reshape(64, 2 * PAGE, HD)))
    cosine, sine = rope_tables(ROWS, PAGES * PAGE)
    arrays = (swap(hidden), near, swap(near), back, swap(back))
    early = project_early(arrays, hidden, w_query, w_keyval)
    (far,) = after((early[2], pages), far)
    queries, own_keys, own_values, send = project_late(
        table, (far, swap(far)), early[:3], early[3:], cosine, sine
    )
    received = exchange(send)
    keys, values = split_pages(table, pages)
    attended = attend(queries, own_keys, own_values, keys, values)
    placed = place_pages(table, received)
    return attended, placed.reshape(SLOTS, 1, PAGE, 2, HD)


def solution(mesh):
    in_specs = (
        P("pool", "tp"),
        P(None, "tp"),
        P(None, "tp"),
        P("pool", "tp", None, None, None),
        P(),
        P(),
        P(),
    )
    out_specs = (P("pool", "tp"), P("pool", "tp", None, None, None))
    return jax.shard_map(body, mesh=mesh, in_specs=in_specs, out_specs=out_specs, check_vma=False)
```

```python
import functools
import math

import jax
import jax.numpy as jnp
from jax import lax
from jax.experimental import pallas as pl
from jax.experimental.pallas import tpu as pltpu
from jax.sharding import PartitionSpec as P

D = 8192
HD = 128
PAGE = 64
CAP = 4
PUSH_CAP = 2
HEADS = 4
FEAT = 1024
QW = 512
KVW = 256
POOL = 16
PAGES = 32
NEW_PAGES = 8
SLOTS = 32
ROWS = 512
PUSH, TAKE, PLACE = 4, 16, 17
MIB = 1024 * 1024
SCALE = math.log2(math.e) / math.sqrt(HD)
PIN = 30_000_000_000
F32 = jnp.float32
BF16 = jnp.bfloat16
ANY = pl.BlockSpec(memory_space=pl.ANY)
HBM = pl.BlockSpec(memory_space=pltpu.HBM)
VMEM = pl.BlockSpec(memory_space=pltpu.VMEM)
SMEM = pl.BlockSpec(memory_space=pltpu.SMEM)


def params(mib):
    return pltpu.CompilerParams(vmem_limit_bytes=mib * MIB)


def cost(flops, nbytes):
    return pl.CostEstimate(flops=flops, bytes_accessed=nbytes, transcendentals=0)


def hbm(array):
    return pltpu.with_memory_space_constraint(array, pltpu.HBM)


def shape(dims, dtype):
    return jax.ShapeDtypeStruct(dims, dtype)


def fill_table(owners, slots, targets, out_ref):
    me = lax.axis_index("pool")
    out_ref[...] = jnp.zeros_like(out_ref)
    lanes = lax.broadcasted_iota(jnp.int32, owners.shape, 1)
    rows = lax.broadcasted_iota(jnp.int32, owners.shape, 0)
    ranks = jnp.zeros_like(owners)
    for j in range(PAGES):
        ranks += ((owners == owners[:, j : j + 1]) & (lanes > j)).astype(jnp.int32)
    for k in range(CAP):
        chosen = jnp.where((owners == me) & (ranks == k), slots, 0)
        out_ref[:POOL, k : k + 1] = jnp.sum(chosen, axis=1, keepdims=True)
    mine = jnp.where(rows == me, owners * CAP + ranks, 0)
    out_ref[TAKE : TAKE + 1, :PAGES] = jnp.sum(mine, axis=0, keepdims=True)
    lanes = lax.broadcasted_iota(jnp.int32, targets.shape, 1)
    rows = lax.broadcasted_iota(jnp.int32, targets.shape, 0)
    kept = (targets == me).astype(jnp.int32)
    ranks = jnp.zeros_like(targets)
    slot = jnp.zeros_like(targets)
    for j in range(NEW_PAGES):
        later = rows > j
        ranks += ((targets == targets[j : j + 1, :]) & later).astype(jnp.int32)
        slot += jnp.where(later, kept[j : j + 1, :], 0)
    mine = jnp.where(lanes == me, targets * PUSH_CAP + ranks, 0)
    out_ref[:NEW_PAGES, PUSH : PUSH + 1] = jnp.sum(mine, axis=1, keepdims=True)
    of_request = jnp.sum(kept, axis=0, keepdims=True)
    for r in range(POOL):
        slot += jnp.where(lanes > r, of_request[:, r : r + 1], 0)
    source = jnp.zeros((NEW_PAGES, SLOTS), jnp.int32)
    slot_lanes = lax.broadcasted_iota(jnp.int32, source.shape, 1)
    for r in range(POOL):
        hit = (kept[:, r : r + 1] > 0) & (slot[:, r : r + 1] == slot_lanes)
        source += jnp.where(hit, r * PUSH_CAP + ranks[:, r : r + 1] + 1, 0)
    out_ref[PLACE : PLACE + 1, :SLOTS] = jnp.sum(source, axis=0, keepdims=True)


def prelude_kernel(owner_in, slot_in, target_in, store_in, table_ref, out_ref, *scratch):
    owner_ref, slot_ref, target_ref, store_ref, index_ref, sems, page_sems = scratch
    pairs = (
        (owner_in, owner_ref),
        (slot_in, slot_ref),
        (target_in, target_ref),
        (store_in, store_ref),
    )
    copies = [pltpu.make_async_copy(x, y, sems.at[i]) for i, (x, y) in enumerate(pairs)]
    for copy in copies:
        copy.start()
    for copy in copies[:3]:
        copy.wait()
    fill_table(owner_ref[...], slot_ref[...], target_ref[...], table_ref)
    indices = pltpu.make_async_copy(table_ref, index_ref, sems.at[4])
    indices.start()
    indices.wait()
    copies[3].wait()
    pages = [
        pltpu.make_async_copy(
            store_ref.at[index_ref[i // CAP, i % CAP]], out_ref.at[i], page_sems.at[i]
        )
        for i in range(POOL * CAP)
    ]
    for page in pages:
        page.start()
    for page in pages:
        page.wait()


def prelude(page_owner, page_slot, new_owner, store):
    return pl.pallas_call(
        prelude_kernel,
        out_shape=[
            shape((24, HD), jnp.int32),
            pltpu.HBM((POOL * CAP, 2 * PAGE, HD), BF16),
        ],
        in_specs=[HBM] * 4,
        out_specs=[VMEM, HBM],
        scratch_shapes=[
            pltpu.VMEM((POOL, PAGES), jnp.int32),
            pltpu.VMEM((POOL, PAGES), jnp.int32),
            pltpu.VMEM((NEW_PAGES, POOL), jnp.int32),
            pltpu.VMEM(store.shape, BF16),
            pltpu.SMEM((24, HD), jnp.int32),
            pltpu.SemaphoreType.DMA((5,)),
            pltpu.SemaphoreType.DMA((POOL * CAP,)),
        ],
        compiler_params=params(8),
        cost_estimate=cost(0, 1),
        name="prelude",
    )(hbm(page_owner), hbm(page_slot), hbm(new_owner.T), hbm(store))


def split_kernel(table_ref, pages_ref, keys_ref, values_ref):
    row = lax.broadcasted_iota(jnp.int32, (2 * PAGE, 2 * PAGE), 0)
    column = lax.broadcasted_iota(jnp.int32, (2 * PAGE, 2 * PAGE), 1)
    wanted = jnp.where(row < PAGE, 2 * row, 2 * (row - PAGE) + 1)
    picker = (column == wanted).astype(BF16)
    values_ref[:, HD:] = jnp.ones((PAGES * PAGE, HD), BF16)
    for page in range(PAGES):
        both = jnp.dot(picker, pages_ref[table_ref[TAKE, page]], preferred_element_type=F32)
        rows = pl.ds(page * PAGE, PAGE)
        keys_ref[rows, :] = both[:PAGE].astype(BF16)
        values_ref[rows, :HD] = both[PAGE:].astype(BF16)


def split_pages(table, pages):
    return pl.pallas_call(
        split_kernel,
        out_shape=[
            shape((PAGES * PAGE, HD), BF16),
            shape((PAGES * PAGE, 2 * HD), BF16),
        ],
        in_specs=[SMEM, VMEM],
        out_specs=[VMEM, VMEM],
        compiler_params=params(8),
        cost_estimate=cost(2 * 2048 * 128 * 256, 4 * MIB),
        name="split_pages",
    )(table, pages)


def block_index(steps, other_core):
    index = lax.axis_index("tp")
    core = lax.rem(index, 2)
    if other_core:
        core = 1 - core
    z = lax.rem(index // 2 + jnp.where(core == 0, steps[0], steps[1]), 4)
    return 2 * z + core


def squares_of(rows):
    wide = rows.astype(F32)
    total = None
    for lane in range(0, FEAT, HD):
        part = wide[:, lane : lane + HD]
        total = part * part if total is None else total + part * part
    return total


def weight_copies(refs, buffers, sems, blocks):
    copies = []
    for i, (steps, other) in enumerate(blocks):
        rows = pl.ds(pl.multiple_of(block_index(steps, other) * FEAT, FEAT), FEAT)
        copies.append(
            [
                pltpu.make_async_copy(ref.at[rows, :], buffer.at[i], sems.at[len(refs) * i + j])
                for j, (ref, buffer) in enumerate(zip(refs, buffers))
            ]
        )
    for group in copies:
        for copy in group:
            copy.start()
    return copies


OWN, NEAR, BACK, FAR = (0, 0), (3, 1), (1, 3), (2, 2)
EARLY = ((OWN, True), (NEAR, True), (BACK, True), (OWN, False), (NEAR, False), (BACK, False))
LATE = ((FAR, False), (FAR, True))
TILE = 128


def early_kernel(*refs):
    count = len(EARLY)
    wq_ref, wkv_ref = refs[6:8]
    q_ref, kv_ref, sq_ref, x_buf, wq_buf, wkv_buf, sems, x_sems = refs[8:]
    x_copies = [pltpu.make_async_copy(refs[3 + i], x_buf.at[i], x_sems.at[i]) for i in range(3)]
    copies = weight_copies((wq_ref, wkv_ref), (wq_buf, wkv_buf), sems, EARLY)
    for copy in x_copies:
        copy.start()
    for i in range(count):
        copies[i][0].wait()
        copies[i][1].wait()
        if i >= 3:
            x_copies[i - 3].wait()
        for r in range(0, ROWS, TILE):
            rows = slice(r, r + TILE)
            x = refs[i][rows, :] if i < 3 else x_buf[i - 3, rows, :]
            q_part = jnp.dot(x, wq_buf[i], preferred_element_type=F32)
            kv_part = jnp.dot(x, wkv_buf[i], preferred_element_type=F32)
            sq_part = squares_of(x)
            if i == 0:
                q_ref[rows, :] = q_part
                kv_ref[rows, :] = kv_part
                sq_ref[rows, :] = sq_part
            else:
                q_ref[rows, :] += q_part
                kv_ref[rows, :] += kv_part
                sq_ref[rows, :] += sq_part


def project_early(swapped, direct, w_query, w_keyval):
    count = len(EARLY)
    return pl.pallas_call(
        early_kernel,
        out_shape=[
            pltpu.HBM((ROWS, QW), F32),
            pltpu.HBM((ROWS, KVW), F32),
            pltpu.HBM((ROWS, HD), F32),
        ],
        in_specs=[VMEM] * 3 + [HBM] * 5,
        out_specs=[VMEM] * 3,
        scratch_shapes=[
            pltpu.VMEM((3, ROWS, FEAT), BF16),
            pltpu.VMEM((count, FEAT, QW), BF16),
            pltpu.VMEM((count, FEAT, KVW), BF16),
            pltpu.SemaphoreType.DMA((2 * count,)),
            pltpu.SemaphoreType.DMA((3,)),
        ],
        compiler_params=params(16),
        cost_estimate=cost(0, 1),
        name="project_early",
    )(*swapped, *[hbm(x) for x in (*direct, w_query, w_keyval)])


def after_kernel(*refs):
    pass


def after(tokens, *arrays, flops=0):
    count, skip = len(arrays), len(tokens)
    return pl.pallas_call(
        after_kernel,
        out_shape=[shape(x.shape, x.dtype) for x in arrays],
        in_specs=[HBM] * skip + [ANY] * count,
        out_specs=[ANY] * count,
        input_output_aliases={i + skip: i for i in range(count)},
        compiler_params=params(1),
        cost_estimate=cost(flops, 1),
        name="after",
    )(*[hbm(token) for token in tokens], *arrays)


def turn(values, cosine, sine):
    return values * cosine + pltpu.roll(values, HD // 2, 1) * sine


def late_kernel(table_ref, *refs):
    x_refs = refs[:2]
    q_in, kv_in, sq_in, cos_ref, sin_ref, wq_ref, wkv_ref, _ = refs[2:10]
    q_out, keys_out, values_out, send_out = refs[10:14]
    wq_buf, wkv_buf, q_buf, keys_buf, values_buf, page_buf, w_sems, sems, page_sems = refs[14:]
    weights = weight_copies((wq_ref, wkv_ref), (wq_buf, wkv_buf), w_sems, LATE)
    row = lax.broadcasted_iota(jnp.int32, (2 * PAGE, 2 * PAGE), 0)
    column = lax.broadcasted_iota(jnp.int32, (2 * PAGE, 2 * PAGE), 1)
    picker = (column == (row >> 1) + (row & 1) * PAGE).astype(BF16)
    values_buf[:, HD:] = jnp.ones((ROWS, HD), BF16)
    inv_norms = []
    for r in range(0, ROWS, TILE):
        rows = slice(r, r + TILE)
        squares = sq_in[rows, :] + squares_of(x_refs[0][rows, :]) + squares_of(x_refs[1][rows, :])
        mean = jnp.sum(squares, axis=1, keepdims=True) / D
        inv_norms.append(jnp.broadcast_to(lax.rsqrt(mean + 1e-05), (TILE, HD)))
    copies = []
    for group in weights:
        for copy in group:
            copy.wait()
    for r in range(0, ROWS, TILE):
        rows = slice(r, r + TILE)
        inv_norm = inv_norms[r // TILE]
        kv_sum = kv_in[rows, :]
        q_sum = q_in[rows, :]
        for i in range(2):
            x = x_refs[i][rows, :]
            kv_sum += jnp.dot(x, wkv_buf[i], preferred_element_type=F32)
            q_sum += jnp.dot(x, wq_buf[i], preferred_element_type=F32)
        cosine, sine = cos_ref[rows, :], sin_ref[rows, :]
        keys = turn(kv_sum[:, :HD] * inv_norm, cosine, sine).astype(BF16)
        values = (kv_sum[:, HD:] * inv_norm).astype(BF16)
        keys_buf[rows, :] = keys
        values_buf[rows, :HD] = values
        for p in range(0, TILE, PAGE):
            page = (r + p) // PAGE
            both = jnp.concatenate([keys[p : p + PAGE], values[p : p + PAGE]], axis=0)
            page_buf[page] = jnp.dot(picker, both, preferred_element_type=F32).astype(BF16)
            target = send_out.at[table_ref[page, PUSH]]
            copies.append(pltpu.make_async_copy(page_buf.at[page], target, page_sems.at[page]))
            copies[-1].start()
        for head in range(HEADS):
            part = q_sum[:, head * HD : (head + 1) * HD] * inv_norm
            q_buf[head, rows, :] = turn(part, cosine, sine).astype(BF16)
        span = pl.ds(r, TILE)
        results = (
            (q_buf.at[:, span, :], q_out.at[:, span, :]),
            (keys_buf.at[span, :], keys_out.at[span, :]),
            (values_buf.at[span, :], values_out.at[span, :]),
        )
        for i, (source, target) in enumerate(results):
            copies.append(pltpu.make_async_copy(source, target, sems.at[3 * (r // TILE) + i]))
            copies[-1].start()
    for copy in copies:
        copy.wait()


def project_late(table, blocks, sums, cosine, sine, w_query, w_keyval, token):
    results = [(HEADS, ROWS, HD), (ROWS, HD), (ROWS, 2 * HD)]
    return pl.pallas_call(
        late_kernel,
        out_shape=[pltpu.HBM(x, BF16) for x in results]
        + [pltpu.HBM((POOL * PUSH_CAP, 2 * PAGE, HD), BF16)],
        in_specs=[SMEM] + [VMEM] * 7 + [HBM] * 2 + [ANY],
        out_specs=[HBM] * 4,
        scratch_shapes=[
            pltpu.VMEM((2, FEAT, QW), BF16),
            pltpu.VMEM((2, FEAT, KVW), BF16),
            *[pltpu.VMEM(x, BF16) for x in results],
            pltpu.VMEM((NEW_PAGES, 2 * PAGE, HD), BF16),
            pltpu.SemaphoreType.DMA((4,)),
            pltpu.SemaphoreType.DMA((3 * ROWS // TILE,)),
            pltpu.SemaphoreType.DMA((NEW_PAGES,)),
        ],
        compiler_params=params(16),
        cost_estimate=cost(0, 1),
        name="project_late",
    )(table, *blocks, *sums, cosine, sine, hbm(w_query), hbm(w_keyval), token)


def dot_nt(a, b):
    return lax.dot_general(a, b, (((1,), (1,)), ((), ())), preferred_element_type=F32)


def attend_kernel(q_ref, own_keys_ref, own_values_ref, keys_ref, values_ref, out_ref, *scratch):
    q_buf, own_keys, own_values, sems = scratch
    copies = [
        pltpu.make_async_copy(source, target, sems.at[i])
        for i, (source, target) in enumerate(
            ((q_ref, q_buf), (own_keys_ref, own_keys), (own_values_ref, own_values))
        )
    ]
    for copy in copies:
        copy.start()
    for copy in copies:
        copy.wait()
    block = 256
    allowed = lax.broadcasted_iota(jnp.int32, (block, block), 0) >= lax.broadcasted_iota(
        jnp.int32, (block, block), 1
    )
    for head in range(HEADS):
        lanes = slice(head * HD, (head + 1) * HD)
        for b in range(ROWS // block):
            rows = slice(b * block, (b + 1) * block)
            queries = q_buf[head, rows, :]
            own = dot_nt(queries, own_keys[: (b + 1) * block, :])
            diagonal = jnp.where(allowed, own[:, b * block :], -1e30)
            parts = [(diagonal, own_values[rows, :])]
            if b:
                parts.append((own[:, : b * block], own_values[: b * block, :]))
            parts.append((dot_nt(queries, keys_ref[...]), values_ref[...]))
            tops = [jnp.max(scores, axis=1, keepdims=True) for scores, _ in parts]
            top = functools.reduce(jnp.maximum, tops)
            both = jnp.zeros((block, 2 * HD), F32)
            for scores, held in parts:
                weights = jnp.exp2((scores - top) * SCALE).astype(BF16)
                both += jnp.dot(weights, held, preferred_element_type=F32)
            out_ref[rows, lanes] = (both[:, :HD] / both[:, HD:]).astype(BF16)


def attend(queries, own_keys, own_values, keys, values):
    return pl.pallas_call(
        attend_kernel,
        out_shape=shape((ROWS, QW), BF16),
        in_specs=[HBM] * 3 + [VMEM] * 2,
        out_specs=VMEM,
        scratch_shapes=[
            pltpu.VMEM((HEADS, ROWS, HD), BF16),
            pltpu.VMEM((ROWS, HD), BF16),
            pltpu.VMEM((ROWS, 2 * HD), BF16),
            pltpu.SemaphoreType.DMA((3,)),
        ],
        compiler_params=params(40),
        cost_estimate=cost(2 * ROWS * 4 * 2560 * 512, 8 * MIB),
        name="attend",
    )(hbm(queries), hbm(own_keys), hbm(own_values), keys, values)


def place_kernel(table_ref, received_ref, out_ref, buffer, sems):
    group = 4
    copies = []
    for i in range(SLOTS):
        source = table_ref[PLACE, i]
        page = received_ref[jnp.maximum(source - 1, 0)]
        buffer[i] = jnp.where(source > 0, page, jnp.zeros_like(page))
        if i % group == group - 1:
            slots = pl.ds(i + 1 - group, group)
            copy = pltpu.make_async_copy(
                buffer.at[slots], out_ref.at[slots], sems.at[i // group]
            )
            copy.start()
            copies.append(copy)
    for copy in copies:
        copy.wait()


def place_pages(table, received):
    return pl.pallas_call(
        place_kernel,
        out_shape=pltpu.HBM((SLOTS, 2 * PAGE, HD), BF16),
        in_specs=[SMEM, VMEM],
        out_specs=HBM,
        scratch_shapes=[
            pltpu.VMEM((SLOTS, 2 * PAGE, HD), BF16),
            pltpu.SemaphoreType.DMA((SLOTS // 4,)),
        ],
        compiler_params=params(8),
        cost_estimate=cost(0, 2 * MIB),
        name="place_pages",
    )(table, received)


def shift(values, steps):
    pairs = [(i, ((i // 2 + steps[i % 2]) % 4) * 2 + i % 2) for i in range(8)]
    return lax.ppermute(values, "tp", pairs)


def swap(values):
    return lax.ppermute(values, "tp", [(i, i ^ 1) for i in range(8)])


def rope_tables(row_count, offset):
    half_dim = HD // 2
    frequency = 500000.0 ** (-(jnp.arange(half_dim, dtype=F32) * (2.0 / HD)))
    place = (offset + jnp.arange(row_count, dtype=jnp.int32)).astype(F32)
    angles = place[:, None] * frequency[None, :]
    cosine, sine = jnp.cos(angles), jnp.sin(angles)
    return jnp.concatenate([cosine, cosine], 1), jnp.concatenate([-sine, sine], 1)


def exchange(values):
    return lax.all_to_all(values, "pool", split_axis=0, concat_axis=0, tiled=True)


def body(hidden, w_query, w_keyval, store, page_owner, page_slot, new_owner):
    near, back = shift(hidden, (1, -1)), shift(hidden, (-1, 1))
    far = shift(near, (1, -1))
    table, packed = prelude(page_owner, page_slot, new_owner, store.reshape(64, 2 * PAGE, HD))
    (pages,) = after((), exchange(packed), flops=PIN)
    cosine, sine = rope_tables(ROWS, PAGES * PAGE)
    direct = (hidden, near, back)
    sums = project_early([swap(x) for x in direct], direct, w_query, w_keyval)
    (far,) = after((sums[2],), far)
    queries, own_keys, own_values, send = project_late(
        table, (far, swap(far)), sums, cosine, sine, w_query, w_keyval, pages
    )
    received = exchange(send)
    keys, values = split_pages(table, pages)
    attended = attend(queries, own_keys, own_values, keys, values)
    placed = place_pages(table, received)
    return attended, placed.reshape(SLOTS, 1, PAGE, 2, HD)


def solution(mesh):
    in_specs = (
        P("pool", "tp"),
        P(None, "tp"),
        P(None, "tp"),
        P("pool", "tp", None, None, None),
        P(),
        P(),
        P(),
    )
    out_specs = (P("pool", "tp"), P("pool", "tp", None, None, None))
    return jax.shard_map(body, mesh=mesh, in_specs=in_specs, out_specs=out_specs, check_vma=False)
```

```python
import functools
import math

import jax
import jax.numpy as jnp
from jax import lax
from jax.experimental import pallas as pl
from jax.experimental.pallas import tpu as pltpu
from jax.sharding import PartitionSpec as P

D = 8192
HD = 128
PAGE = 64
CAP = 4
PUSH_CAP = 2
HEADS = 4
FEAT = 1024
QW = 512
KVW = 256
POOL = 16
PAGES = 32
NEW_PAGES = 8
SLOTS = 32
ROWS = 512
PUSH, TAKE, PLACE = 4, 16, 17
MIB = 1024 * 1024
SCALE = math.log2(math.e) / math.sqrt(HD)
HIDES = 20_000_000_000
F32 = jnp.float32
BF16 = jnp.bfloat16
ANY = pl.BlockSpec(memory_space=pl.ANY)
HBM = pl.BlockSpec(memory_space=pltpu.HBM)
VMEM = pl.BlockSpec(memory_space=pltpu.VMEM)
SMEM = pl.BlockSpec(memory_space=pltpu.SMEM)


def params(mib):
    return pltpu.CompilerParams(vmem_limit_bytes=mib * MIB)


def cost(flops, nbytes):
    return pl.CostEstimate(flops=flops, bytes_accessed=nbytes, transcendentals=0)


def hbm(array):
    return pltpu.with_memory_space_constraint(array, pltpu.HBM)


def shape(dims, dtype):
    return jax.ShapeDtypeStruct(dims, dtype)


def fill_table(owners, slots, targets, out_ref):
    me = lax.axis_index("pool")
    out_ref[...] = jnp.zeros_like(out_ref)
    lanes = lax.broadcasted_iota(jnp.int32, owners.shape, 1)
    rows = lax.broadcasted_iota(jnp.int32, owners.shape, 0)
    ranks = jnp.zeros_like(owners)
    for j in range(PAGES):
        ranks += ((owners == owners[:, j : j + 1]) & (lanes > j)).astype(jnp.int32)
    for k in range(CAP):
        chosen = jnp.where((owners == me) & (ranks == k), slots, 0)
        out_ref[:POOL, k : k + 1] = jnp.sum(chosen, axis=1, keepdims=True)
    mine = jnp.where(rows == me, owners * CAP + ranks, 0)
    out_ref[TAKE : TAKE + 1, :PAGES] = jnp.sum(mine, axis=0, keepdims=True)
    lanes = lax.broadcasted_iota(jnp.int32, targets.shape, 1)
    rows = lax.broadcasted_iota(jnp.int32, targets.shape, 0)
    kept = (targets == me).astype(jnp.int32)
    ranks = jnp.zeros_like(targets)
    slot = jnp.zeros_like(targets)
    for j in range(NEW_PAGES):
        later = rows > j
        ranks += ((targets == targets[j : j + 1, :]) & later).astype(jnp.int32)
        slot += jnp.where(later, kept[j : j + 1, :], 0)
    mine = jnp.where(lanes == me, targets * PUSH_CAP + ranks, 0)
    out_ref[:NEW_PAGES, PUSH : PUSH + 1] = jnp.sum(mine, axis=1, keepdims=True)
    of_request = jnp.sum(kept, axis=0, keepdims=True)
    for r in range(POOL):
        slot += jnp.where(lanes > r, of_request[:, r : r + 1], 0)
    source = jnp.zeros((NEW_PAGES, SLOTS), jnp.int32)
    slot_lanes = lax.broadcasted_iota(jnp.int32, source.shape, 1)
    for r in range(POOL):
        hit = (kept[:, r : r + 1] > 0) & (slot[:, r : r + 1] == slot_lanes)
        source += jnp.where(hit, r * PUSH_CAP + ranks[:, r : r + 1] + 1, 0)
    out_ref[PLACE : PLACE + 1, :SLOTS] = jnp.sum(source, axis=0, keepdims=True)


def prelude_kernel(owner_in, slot_in, target_in, store_in, table_ref, out_ref, *scratch):
    owner_ref, slot_ref, target_ref, store_ref, index_ref, sems, page_sems = scratch
    pairs = (
        (owner_in, owner_ref),
        (slot_in, slot_ref),
        (target_in, target_ref),
        (store_in, store_ref),
    )
    copies = [pltpu.make_async_copy(x, y, sems.at[i]) for i, (x, y) in enumerate(pairs)]
    for copy in copies:
        copy.start()
    for copy in copies[:3]:
        copy.wait()
    fill_table(owner_ref[...], slot_ref[...], target_ref[...], table_ref)
    indices = pltpu.make_async_copy(table_ref, index_ref, sems.at[4])
    indices.start()
    indices.wait()
    copies[3].wait()
    pages = [
        pltpu.make_async_copy(
            store_ref.at[index_ref[i // CAP, i % CAP]], out_ref.at[i], page_sems.at[i]
        )
        for i in range(POOL * CAP)
    ]
    for page in pages:
        page.start()
    for page in pages:
        page.wait()


def prelude(page_owner, page_slot, new_owner, store):
    return pl.pallas_call(
        prelude_kernel,
        out_shape=[
            shape((24, HD), jnp.int32),
            pltpu.HBM((POOL * CAP, 2 * PAGE, HD), BF16),
        ],
        in_specs=[HBM] * 4,
        out_specs=[VMEM, HBM],
        scratch_shapes=[
            pltpu.VMEM((POOL, PAGES), jnp.int32),
            pltpu.VMEM((POOL, PAGES), jnp.int32),
            pltpu.VMEM((NEW_PAGES, POOL), jnp.int32),
            pltpu.VMEM(store.shape, BF16),
            pltpu.SMEM((24, HD), jnp.int32),
            pltpu.SemaphoreType.DMA((5,)),
            pltpu.SemaphoreType.DMA((POOL * CAP,)),
        ],
        compiler_params=params(8),
        cost_estimate=cost(0, 1),
        name="prelude",
    )(hbm(page_owner), hbm(page_slot), hbm(new_owner.T), hbm(store))


def split_kernel(table_ref, pages_ref, keys_ref, values_ref):
    row = lax.broadcasted_iota(jnp.int32, (2 * PAGE, 2 * PAGE), 0)
    column = lax.broadcasted_iota(jnp.int32, (2 * PAGE, 2 * PAGE), 1)
    wanted = jnp.where(row < PAGE, 2 * row, 2 * (row - PAGE) + 1)
    picker = (column == wanted).astype(BF16)
    values_ref[:, HD:] = jnp.ones((PAGES * PAGE, HD), BF16)
    for page in range(PAGES):
        both = jnp.dot(picker, pages_ref[table_ref[TAKE, page]], preferred_element_type=F32)
        rows = pl.ds(page * PAGE, PAGE)
        keys_ref[rows, :] = both[:PAGE].astype(BF16)
        values_ref[rows, :HD] = both[PAGE:].astype(BF16)


def split_pages(table, pages):
    return pl.pallas_call(
        split_kernel,
        out_shape=[
            shape((PAGES * PAGE, HD), BF16),
            shape((PAGES * PAGE, 2 * HD), BF16),
        ],
        in_specs=[SMEM, VMEM],
        out_specs=[VMEM, VMEM],
        compiler_params=params(8),
        cost_estimate=cost(2 * 2048 * 128 * 256, 4 * MIB),
        name="split_pages",
    )(table, pages)


def block_index(steps, other_core):
    index = lax.axis_index("tp")
    core = lax.rem(index, 2)
    if other_core:
        core = 1 - core
    z = lax.rem(index // 2 + jnp.where(core == 0, steps[0], steps[1]), 4)
    return 2 * z + core


def squares_of(rows):
    wide = rows.astype(F32)
    total = None
    for lane in range(0, FEAT, HD):
        part = wide[:, lane : lane + HD]
        total = part * part if total is None else total + part * part
    return total


def weight_copies(refs, buffers, sems, blocks):
    copies = []
    for i, (steps, other) in enumerate(blocks):
        rows = pl.ds(pl.multiple_of(block_index(steps, other) * FEAT, FEAT), FEAT)
        copies.append(
            [
                pltpu.make_async_copy(ref.at[rows, :], buffer.at[i], sems.at[len(refs) * i + j])
                for j, (ref, buffer) in enumerate(zip(refs, buffers))
            ]
        )
    for group in copies:
        for copy in group:
            copy.start()
    return copies


OWN, NEAR, BACK, FAR = (0, 0), (3, 1), (1, 3), (2, 2)
TILE = 128


def project_kernel(blocks, held, has_sums, tokens, ahead, *refs):
    count = len(blocks)
    x_refs, refs = refs[:count], refs[count:]
    wq_ref, wkv_ref, refs = refs[0], refs[1], refs[2:]
    before, refs = (refs[:3], refs[3:]) if has_sums else (None, refs)
    refs = refs[tokens:]
    sums, refs = refs[:3], refs[3:]
    fetched, refs = (refs[:2], refs[2:]) if ahead else (None, refs)
    x_buf, wq_buf, wkv_buf, sems, x_sems, ahead_sems = refs
    copies = weight_copies((wq_ref, wkv_ref), (wq_buf, wkv_buf), sems, blocks)
    x_copies = {}
    for i in range(held, count):
        x_copies[i] = pltpu.make_async_copy(x_refs[i], x_buf.at[i - held], x_sems.at[i - held])
        x_copies[i].start()
    later = weight_copies((wq_ref, wkv_ref), fetched, ahead_sems, ahead) if ahead else []
    for i in range(count):
        copies[i][0].wait()
        copies[i][1].wait()
        if i in x_copies:
            x_copies[i].wait()
        for r in range(0, ROWS, TILE):
            rows = slice(r, r + TILE)
            x = x_refs[i][rows, :] if i < held else x_buf[i - held, rows, :]
            parts = (
                jnp.dot(x, wq_buf[i], preferred_element_type=F32),
                jnp.dot(x, wkv_buf[i], preferred_element_type=F32),
                squares_of(x),
            )
            for j, part in enumerate(parts):
                if i > 0:
                    sums[j][rows, :] += part
                elif has_sums:
                    sums[j][rows, :] = before[j][rows, :] + part
                else:
                    sums[j][rows, :] = part
    for group in later:
        for copy in group:
            copy.wait()


def project(blocks, held, direct, w_query, w_keyval, sums=(), ahead=(), tokens=(), flops=0):
    count = len(blocks)
    shapes = [shape((ROWS, w), F32) for w in (QW, KVW, HD)]
    if ahead:
        shapes += [shape((len(ahead), FEAT, w), BF16) for w in (QW, KVW)]
    return pl.pallas_call(
        functools.partial(project_kernel, blocks, len(held), bool(sums), len(tokens), ahead),
        out_shape=shapes,
        in_specs=[VMEM] * len(held)
        + [HBM] * (len(direct) + 2)
        + [VMEM] * len(sums)
        + [ANY] * len(tokens),
        out_specs=[VMEM] * len(shapes),
        scratch_shapes=[
            pltpu.VMEM((max(len(direct), 1), ROWS, FEAT), BF16),
            pltpu.VMEM((count, FEAT, QW), BF16),
            pltpu.VMEM((count, FEAT, KVW), BF16),
            pltpu.SemaphoreType.DMA((2 * count,)),
            pltpu.SemaphoreType.DMA((max(len(direct), 1),)),
            pltpu.SemaphoreType.DMA((max(2 * len(ahead), 1),)),
        ],
        compiler_params=params(24),
        cost_estimate=cost(flops, 1),
        name="project",
    )(*held, *[hbm(x) for x in (*direct, w_query, w_keyval)], *sums, *tokens)


def after_kernel(*refs):
    pass


def after(tokens, *arrays, flops=0):
    count, skip = len(arrays), len(tokens)
    return pl.pallas_call(
        after_kernel,
        out_shape=[shape(x.shape, x.dtype) for x in arrays],
        in_specs=[ANY] * (count + skip),
        out_specs=[ANY] * count,
        input_output_aliases={i + skip: i for i in range(count)},
        compiler_params=params(1),
        cost_estimate=cost(flops, 1),
        name="after",
    )(*tokens, *arrays)


def turn(values, cosine, sine):
    return values * cosine + pltpu.roll(values, HD // 2, 1) * sine


def late_kernel(table_ref, x_ref, q_in, kv_in, sq_in, wq_ref, wkv_ref, cos_ref, sin_ref, *refs):
    q_out, keys_out, values_out, send_out = refs[:4]
    q_buf, keys_buf, values_buf, page_buf, sems, page_sems = refs[4:]
    row = lax.broadcasted_iota(jnp.int32, (2 * PAGE, 2 * PAGE), 0)
    column = lax.broadcasted_iota(jnp.int32, (2 * PAGE, 2 * PAGE), 1)
    picker = (column == (row >> 1) + (row & 1) * PAGE).astype(BF16)
    values_buf[:, HD:] = jnp.ones((ROWS, HD), BF16)
    copies = []
    for r in range(0, ROWS, TILE):
        rows = slice(r, r + TILE)
        x = x_ref[rows, :]
        kv_sum = kv_in[rows, :] + jnp.dot(x, wkv_ref[0], preferred_element_type=F32)
        q_sum = q_in[rows, :] + jnp.dot(x, wq_ref[0], preferred_element_type=F32)
        squares = sq_in[rows, :] + squares_of(x)
        mean = jnp.sum(squares, axis=1, keepdims=True) / D
        inv_norm = jnp.broadcast_to(lax.rsqrt(mean + 1e-05), (TILE, HD))
        cosine, sine = cos_ref[rows, :], sin_ref[rows, :]
        keys = turn(kv_sum[:, :HD] * inv_norm, cosine, sine).astype(BF16)
        values = (kv_sum[:, HD:] * inv_norm).astype(BF16)
        keys_buf[rows, :] = keys
        values_buf[rows, :HD] = values
        for p in range(0, TILE, PAGE):
            page = (r + p) // PAGE
            both = jnp.concatenate([keys[p : p + PAGE], values[p : p + PAGE]], axis=0)
            page_buf[page] = jnp.dot(picker, both, preferred_element_type=F32).astype(BF16)
            target = send_out.at[table_ref[page, PUSH]]
            copies.append(pltpu.make_async_copy(page_buf.at[page], target, page_sems.at[page]))
            copies[-1].start()
        for head in range(HEADS):
            part = q_sum[:, head * HD : (head + 1) * HD] * inv_norm
            q_buf[head, rows, :] = turn(part, cosine, sine).astype(BF16)
        span = pl.ds(r, TILE)
        results = (
            (q_buf.at[:, span, :], q_out.at[:, span, :]),
            (keys_buf.at[span, :], keys_out.at[span, :]),
            (values_buf.at[span, :], values_out.at[span, :]),
        )
        for i, (source, target) in enumerate(results):
            copies.append(pltpu.make_async_copy(source, target, sems.at[3 * (r // TILE) + i]))
            copies[-1].start()
    for copy in copies:
        copy.wait()


def project_late(table, block, sums, cosine, sine):
    results = [(HEADS, ROWS, HD), (ROWS, HD), (ROWS, 2 * HD)]
    return pl.pallas_call(
        late_kernel,
        out_shape=[pltpu.HBM(x, BF16) for x in results]
        + [pltpu.HBM((POOL * PUSH_CAP, 2 * PAGE, HD), BF16)],
        in_specs=[SMEM] + [VMEM] * 8,
        out_specs=[HBM] * 4,
        scratch_shapes=[
            *[pltpu.VMEM(x, BF16) for x in results],
            pltpu.VMEM((NEW_PAGES, 2 * PAGE, HD), BF16),
            pltpu.SemaphoreType.DMA((3 * ROWS // TILE,)),
            pltpu.SemaphoreType.DMA((NEW_PAGES,)),
        ],
        compiler_params=params(16),
        cost_estimate=cost(0, 1),
        name="project_late",
    )(table, block, *sums, cosine, sine)


def dot_nt(a, b):
    return lax.dot_general(a, b, (((1,), (1,)), ((), ())), preferred_element_type=F32)


def attend_kernel(q_ref, own_keys_ref, own_values_ref, keys_ref, values_ref, out_ref, *scratch):
    q_buf, own_keys, own_values, sems = scratch
    copies = [
        pltpu.make_async_copy(source, target, sems.at[i])
        for i, (source, target) in enumerate(
            ((q_ref, q_buf), (own_keys_ref, own_keys), (own_values_ref, own_values))
        )
    ]
    for copy in copies:
        copy.start()
    for copy in copies:
        copy.wait()
    block = 256
    allowed = lax.broadcasted_iota(jnp.int32, (block, block), 0) >= lax.broadcasted_iota(
        jnp.int32, (block, block), 1
    )
    for head in range(HEADS):
        lanes = slice(head * HD, (head + 1) * HD)
        for b in range(ROWS // block):
            rows = slice(b * block, (b + 1) * block)
            queries = q_buf[head, rows, :]
            own = dot_nt(queries, own_keys[: (b + 1) * block, :])
            diagonal = jnp.where(allowed, own[:, b * block :], -1e30)
            parts = [(diagonal, own_values[rows, :])]
            if b:
                parts.append((own[:, : b * block], own_values[: b * block, :]))
            parts.append((dot_nt(queries, keys_ref[...]), values_ref[...]))
            tops = [jnp.max(scores, axis=1, keepdims=True) for scores, _ in parts]
            top = functools.reduce(jnp.maximum, tops)
            both = jnp.zeros((block, 2 * HD), F32)
            for scores, held in parts:
                weights = jnp.exp2((scores - top) * SCALE).astype(BF16)
                both += jnp.dot(weights, held, preferred_element_type=F32)
            out_ref[rows, lanes] = (both[:, :HD] / both[:, HD:]).astype(BF16)


def attend(queries, own_keys, own_values, keys, values):
    return pl.pallas_call(
        attend_kernel,
        out_shape=shape((ROWS, QW), BF16),
        in_specs=[HBM] * 3 + [VMEM] * 2,
        out_specs=VMEM,
        scratch_shapes=[
            pltpu.VMEM((HEADS, ROWS, HD), BF16),
            pltpu.VMEM((ROWS, HD), BF16),
            pltpu.VMEM((ROWS, 2 * HD), BF16),
            pltpu.SemaphoreType.DMA((3,)),
        ],
        compiler_params=params(40),
        cost_estimate=cost(2 * ROWS * 4 * 2560 * 512, 8 * MIB),
        name="attend",
    )(hbm(queries), hbm(own_keys), hbm(own_values), keys, values)


def place_kernel(table_ref, received_ref, out_ref, buffer, sems):
    group = 4
    copies = []
    for i in range(SLOTS):
        source = table_ref[PLACE, i]
        page = received_ref[jnp.maximum(source - 1, 0)]
        buffer[i] = jnp.where(source > 0, page, jnp.zeros_like(page))
        if i % group == group - 1:
            slots = pl.ds(i + 1 - group, group)
            copy = pltpu.make_async_copy(
                buffer.at[slots], out_ref.at[slots], sems.at[i // group]
            )
            copy.start()
            copies.append(copy)
    for copy in copies:
        copy.wait()


def place_pages(table, received):
    return pl.pallas_call(
        place_kernel,
        out_shape=pltpu.HBM((SLOTS, 2 * PAGE, HD), BF16),
        in_specs=[SMEM, VMEM],
        out_specs=HBM,
        scratch_shapes=[
            pltpu.VMEM((SLOTS, 2 * PAGE, HD), BF16),
            pltpu.SemaphoreType.DMA((SLOTS // 4,)),
        ],
        compiler_params=params(8),
        cost_estimate=cost(0, 2 * MIB),
        name="place_pages",
    )(table, received)


def shift(values, steps):
    pairs = [(i, ((i // 2 + steps[i % 2]) % 4) * 2 + i % 2) for i in range(8)]
    return lax.ppermute(values, "tp", pairs)


def swap(values):
    return lax.ppermute(values, "tp", [(i, i ^ 1) for i in range(8)])


def rope_tables(row_count, offset):
    half_dim = HD // 2
    frequency = 500000.0 ** (-(jnp.arange(half_dim, dtype=F32) * (2.0 / HD)))
    place = (offset + jnp.arange(row_count, dtype=jnp.int32)).astype(F32)
    angles = place[:, None] * frequency[None, :]
    cosine, sine = jnp.cos(angles), jnp.sin(angles)
    return jnp.concatenate([cosine, cosine], 1), jnp.concatenate([-sine, sine], 1)


def exchange(values):
    return lax.all_to_all(values, "pool", split_axis=0, concat_axis=0, tiled=True)


def body(hidden, w_query, w_keyval, store, page_owner, page_slot, new_owner):
    near, back = shift(hidden, (1, -1)), shift(hidden, (-1, 1))
    far = shift(near, (1, -1))
    table, packed = prelude(page_owner, page_slot, new_owner, store.reshape(64, 2 * PAGE, HD))
    pages = exchange(packed)
    cosine, sine = rope_tables(ROWS, PAGES * PAGE)
    weights = (w_query, w_keyval)
    blocks = ((OWN, True), (OWN, False), (NEAR, False), (BACK, False))
    tables = (cosine, sine)
    sums = project(
        blocks, [swap(hidden)], [hidden, near, back], *weights, tokens=tables, flops=HIDES
    )
    blocks = ((NEAR, True), (BACK, True))
    sums = project(blocks, [swap(near), swap(back)], [], *weights, sums)
    (far,) = after((sums[2],), far)
    other = swap(far)
    sums = project(((FAR, False),), [far], [], *weights, sums, ((FAR, True),))
    queries, own_keys, own_values, send = project_late(table, other, sums, cosine, sine)
    received = exchange(send)
    keys, values = split_pages(table, pages)
    attended = attend(queries, own_keys, own_values, keys, values)
    placed = place_pages(table, received)
    return attended, placed.reshape(SLOTS, 1, PAGE, 2, HD)


def solution(mesh):
    in_specs = (
        P("pool", "tp"),
        P(None, "tp"),
        P(None, "tp"),
        P("pool", "tp", None, None, None),
        P(),
        P(),
        P(),
    )
    out_specs = (P("pool", "tp"), P("pool", "tp", None, None, None))
    return jax.shard_map(body, mesh=mesh, in_specs=in_specs, out_specs=out_specs, check_vma=False)
```

```python
import functools
import math

import jax
import jax.numpy as jnp
from jax import lax
from jax.experimental import pallas as pl
from jax.experimental.pallas import tpu as pltpu
from jax.sharding import PartitionSpec as P

D = 8192
HD = 128
PAGE = 64
CAP = 4
PUSH_CAP = 2
HEADS = 4
FEAT = 1024
QW = 512
KVW = 256
POOL = 16
PAGES = 32
NEW_PAGES = 8
SLOTS = 32
ROWS = 512
PUSH, TAKE, PLACE = 4, 16, 17
MIB = 1024 * 1024
SCALE = math.log2(math.e) / math.sqrt(HD)
HIDES = 20_000_000_000
F32 = jnp.float32
BF16 = jnp.bfloat16
ANY = pl.BlockSpec(memory_space=pl.ANY)
HBM = pl.BlockSpec(memory_space=pltpu.HBM)
VMEM = pl.BlockSpec(memory_space=pltpu.VMEM)
SMEM = pl.BlockSpec(memory_space=pltpu.SMEM)


def params(mib):
    return pltpu.CompilerParams(vmem_limit_bytes=mib * MIB)


def cost(flops, nbytes):
    return pl.CostEstimate(flops=flops, bytes_accessed=nbytes, transcendentals=0)


def hbm(array):
    return pltpu.with_memory_space_constraint(array, pltpu.HBM)


def shape(dims, dtype):
    return jax.ShapeDtypeStruct(dims, dtype)


def fill_table(owners, slots, targets, out_ref):
    me = lax.axis_index("pool")
    out_ref[...] = jnp.zeros_like(out_ref)
    lanes = lax.broadcasted_iota(jnp.int32, owners.shape, 1)
    rows = lax.broadcasted_iota(jnp.int32, owners.shape, 0)
    ranks = jnp.zeros_like(owners)
    for j in range(PAGES):
        ranks += ((owners == owners[:, j : j + 1]) & (lanes > j)).astype(jnp.int32)
    for k in range(CAP):
        chosen = jnp.where((owners == me) & (ranks == k), slots, 0)
        out_ref[:POOL, k : k + 1] = jnp.sum(chosen, axis=1, keepdims=True)
    mine = jnp.where(rows == me, owners * CAP + ranks, 0)
    out_ref[TAKE : TAKE + 1, :PAGES] = jnp.sum(mine, axis=0, keepdims=True)
    lanes = lax.broadcasted_iota(jnp.int32, targets.shape, 1)
    rows = lax.broadcasted_iota(jnp.int32, targets.shape, 0)
    kept = (targets == me).astype(jnp.int32)
    ranks = jnp.zeros_like(targets)
    slot = jnp.zeros_like(targets)
    for j in range(NEW_PAGES):
        later = rows > j
        ranks += ((targets == targets[j : j + 1, :]) & later).astype(jnp.int32)
        slot += jnp.where(later, kept[j : j + 1, :], 0)
    mine = jnp.where(lanes == me, targets * PUSH_CAP + ranks, 0)
    out_ref[:NEW_PAGES, PUSH : PUSH + 1] = jnp.sum(mine, axis=1, keepdims=True)
    of_request = jnp.sum(kept, axis=0, keepdims=True)
    for r in range(POOL):
        slot += jnp.where(lanes > r, of_request[:, r : r + 1], 0)
    source = jnp.zeros((NEW_PAGES, SLOTS), jnp.int32)
    slot_lanes = lax.broadcasted_iota(jnp.int32, source.shape, 1)
    for r in range(POOL):
        hit = (kept[:, r : r + 1] > 0) & (slot[:, r : r + 1] == slot_lanes)
        source += jnp.where(hit, r * PUSH_CAP + ranks[:, r : r + 1] + 1, 0)
    out_ref[PLACE : PLACE + 1, :SLOTS] = jnp.sum(source, axis=0, keepdims=True)


def prelude_kernel(*refs):
    owner_in, slot_in, target_in, store_in, hidden_in, table_ref, out_ref, hidden_out = refs[:8]
    owner_ref, slot_ref, target_ref, store_ref, hidden_ref, index_ref, sems, page_sems = refs[8:]
    pairs = (
        (owner_in, owner_ref),
        (slot_in, slot_ref),
        (target_in, target_ref),
        (store_in, store_ref),
        (hidden_in, hidden_ref),
    )
    copies = [pltpu.make_async_copy(x, y, sems.at[i]) for i, (x, y) in enumerate(pairs)]
    for copy in copies:
        copy.start()
    for copy in copies[:3]:
        copy.wait()
    fill_table(owner_ref[...], slot_ref[...], target_ref[...], table_ref)
    indices = pltpu.make_async_copy(table_ref, index_ref, sems.at[5])
    indices.start()
    copies[4].wait()
    hidden_copy = pltpu.make_async_copy(hidden_ref, hidden_out, sems.at[6])
    hidden_copy.start()
    indices.wait()
    copies[3].wait()
    pages = [
        pltpu.make_async_copy(
            store_ref.at[index_ref[i // CAP, i % CAP]], out_ref.at[i], page_sems.at[i]
        )
        for i in range(POOL * CAP)
    ]
    for page in pages:
        page.start()
    for page in pages:
        page.wait()
    hidden_copy.wait()


def prelude(page_owner, page_slot, new_owner, store, hidden):
    return pl.pallas_call(
        prelude_kernel,
        out_shape=[
            shape((24, HD), jnp.int32),
            pltpu.HBM((POOL * CAP, 2 * PAGE, HD), BF16),
            pltpu.HBM(hidden.shape, BF16),
        ],
        in_specs=[HBM] * 5,
        out_specs=[VMEM, HBM, HBM],
        scratch_shapes=[
            pltpu.VMEM((POOL, PAGES), jnp.int32),
            pltpu.VMEM((POOL, PAGES), jnp.int32),
            pltpu.VMEM((NEW_PAGES, POOL), jnp.int32),
            pltpu.VMEM(store.shape, BF16),
            pltpu.VMEM(hidden.shape, BF16),
            pltpu.SMEM((24, HD), jnp.int32),
            pltpu.SemaphoreType.DMA((7,)),
            pltpu.SemaphoreType.DMA((POOL * CAP,)),
        ],
        compiler_params=params(8),
        cost_estimate=cost(0, 1),
        name="prelude",
    )(*[hbm(x) for x in (page_owner, page_slot, new_owner.T, store, hidden)])


def split_kernel(table_ref, pages_ref, keys_ref, values_ref):
    row = lax.broadcasted_iota(jnp.int32, (2 * PAGE, 2 * PAGE), 0)
    column = lax.broadcasted_iota(jnp.int32, (2 * PAGE, 2 * PAGE), 1)
    wanted = jnp.where(row < PAGE, 2 * row, 2 * (row - PAGE) + 1)
    picker = (column == wanted).astype(BF16)
    values_ref[:, HD:] = jnp.ones((PAGES * PAGE, HD), BF16)
    for page in range(PAGES):
        both = jnp.dot(picker, pages_ref[table_ref[TAKE, page]], preferred_element_type=F32)
        rows = pl.ds(page * PAGE, PAGE)
        keys_ref[rows, :] = both[:PAGE].astype(BF16)
        values_ref[rows, :HD] = both[PAGE:].astype(BF16)


def split_pages(table, pages):
    return pl.pallas_call(
        split_kernel,
        out_shape=[
            shape((PAGES * PAGE, HD), BF16),
            shape((PAGES * PAGE, 2 * HD), BF16),
        ],
        in_specs=[SMEM, VMEM],
        out_specs=[VMEM, VMEM],
        compiler_params=params(8),
        cost_estimate=cost(2 * 2048 * 128 * 256, 4 * MIB),
        name="split_pages",
    )(table, pages)


def block_index(steps, other_core):
    index = lax.axis_index("tp")
    core = lax.rem(index, 2)
    if other_core:
        core = 1 - core
    z = lax.rem(index // 2 + jnp.where(core == 0, steps[0], steps[1]), 4)
    return 2 * z + core


def squares_of(rows):
    wide = rows.astype(F32)
    total = None
    for lane in range(0, FEAT, HD):
        part = wide[:, lane : lane + HD]
        total = part * part if total is None else total + part * part
    return total


def weight_copies(refs, buffers, sems, blocks):
    copies = []
    for i, (steps, other) in enumerate(blocks):
        rows = pl.ds(pl.multiple_of(block_index(steps, other) * FEAT, FEAT), FEAT)
        copies.append(
            [
                pltpu.make_async_copy(ref.at[rows, :], buffer.at[i], sems.at[len(refs) * i + j])
                for j, (ref, buffer) in enumerate(zip(refs, buffers))
            ]
        )
    for group in copies:
        for copy in group:
            copy.start()
    return copies


OWN, NEAR, BACK, FAR = (0, 0), (3, 1), (1, 3), (2, 2)
TILE = 128


def project_kernel(blocks, held, has_sums, tokens, ahead, *refs):
    count = len(blocks)
    x_refs, refs = refs[:count], refs[count:]
    wq_ref, wkv_ref, refs = refs[0], refs[1], refs[2:]
    before, refs = (refs[:3], refs[3:]) if has_sums else (None, refs)
    refs = refs[tokens:]
    sums, refs = refs[:3], refs[3:]
    fetched, refs = (refs[:2], refs[2:]) if ahead else (None, refs)
    x_buf, wq_buf, wkv_buf, sems, x_sems, ahead_sems = refs
    copies = weight_copies((wq_ref, wkv_ref), (wq_buf, wkv_buf), sems, blocks)
    x_copies = {}
    for i in range(held, count):
        x_copies[i] = pltpu.make_async_copy(x_refs[i], x_buf.at[i - held], x_sems.at[i - held])
        x_copies[i].start()
    later = weight_copies((wq_ref, wkv_ref), fetched, ahead_sems, ahead) if ahead else []
    for i in range(count):
        copies[i][0].wait()
        copies[i][1].wait()
        if i in x_copies:
            x_copies[i].wait()
        for r in range(0, ROWS, TILE):
            rows = slice(r, r + TILE)
            x = x_refs[i][rows, :] if i < held else x_buf[i - held, rows, :]
            parts = (
                jnp.dot(x, wq_buf[i], preferred_element_type=F32),
                jnp.dot(x, wkv_buf[i], preferred_element_type=F32),
                squares_of(x),
            )
            for j, part in enumerate(parts):
                if i > 0:
                    sums[j][rows, :] += part
                elif has_sums:
                    sums[j][rows, :] = before[j][rows, :] + part
                else:
                    sums[j][rows, :] = part
    for group in later:
        for copy in group:
            copy.wait()


def project(blocks, held, direct, w_query, w_keyval, sums=(), ahead=(), tokens=(), flops=0):
    count = len(blocks)
    shapes = [shape((ROWS, w), F32) for w in (QW, KVW, HD)]
    if ahead:
        shapes += [shape((len(ahead), FEAT, w), BF16) for w in (QW, KVW)]
    return pl.pallas_call(
        functools.partial(project_kernel, blocks, len(held), bool(sums), len(tokens), ahead),
        out_shape=shapes,
        in_specs=[VMEM] * len(held)
        + [HBM] * (len(direct) + 2)
        + [VMEM] * len(sums)
        + [ANY] * len(tokens),
        out_specs=[VMEM] * len(shapes),
        scratch_shapes=[
            pltpu.VMEM((max(len(direct), 1), ROWS, FEAT), BF16),
            pltpu.VMEM((count, FEAT, QW), BF16),
            pltpu.VMEM((count, FEAT, KVW), BF16),
            pltpu.SemaphoreType.DMA((2 * count,)),
            pltpu.SemaphoreType.DMA((max(len(direct), 1),)),
            pltpu.SemaphoreType.DMA((max(2 * len(ahead), 1),)),
        ],
        compiler_params=params(24),
        cost_estimate=cost(flops, 1),
        name="project",
    )(*held, *[hbm(x) for x in (*direct, w_query, w_keyval)], *sums, *tokens)


def far_kernel(x_ref, wq_ref, wkv_ref, *refs):
    before, sums = refs[:3], refs[3:]
    for r in range(0, ROWS, TILE):
        rows = slice(r, r + TILE)
        x = x_ref[rows, :]
        sums[0][rows, :] = before[0][rows, :] + jnp.dot(x, wq_ref[0], preferred_element_type=F32)
        sums[1][rows, :] = before[1][rows, :] + jnp.dot(x, wkv_ref[0], preferred_element_type=F32)
        sums[2][rows, :] = before[2][rows, :] + squares_of(x)


def project_far(block, weights, sums):
    return pl.pallas_call(
        far_kernel,
        out_shape=[shape((ROWS, w), F32) for w in (QW, KVW, HD)],
        in_specs=[VMEM] * 6,
        out_specs=[VMEM] * 3,
        compiler_params=params(16),
        cost_estimate=cost(0, 1),
        name="project_far",
    )(block, *weights, *sums)


def after_kernel(*refs):
    pass


def after(tokens, *arrays, flops=0):
    count, skip = len(arrays), len(tokens)
    return pl.pallas_call(
        after_kernel,
        out_shape=[shape(x.shape, x.dtype) for x in arrays],
        in_specs=[ANY] * (count + skip),
        out_specs=[ANY] * count,
        input_output_aliases={i + skip: i for i in range(count)},
        compiler_params=params(1),
        cost_estimate=cost(flops, 1),
        name="after",
    )(*tokens, *arrays)


def turn(values, cosine, sine):
    return values * cosine + pltpu.roll(values, HD // 2, 1) * sine


def late_kernel(table_ref, x_ref, q_in, kv_in, sq_in, wq_ref, wkv_ref, cos_ref, sin_ref, *refs):
    q_out, keys_out, values_out, send_out = refs[:4]
    q_buf, keys_buf, values_buf, page_buf, index_ref, index_sem, sems, page_sems = refs[4:]
    indices = pltpu.make_async_copy(table_ref, index_ref, index_sem)
    indices.start()
    row = lax.broadcasted_iota(jnp.int32, (2 * PAGE, 2 * PAGE), 0)
    column = lax.broadcasted_iota(jnp.int32, (2 * PAGE, 2 * PAGE), 1)
    picker = (column == (row >> 1) + (row & 1) * PAGE).astype(BF16)
    values_buf[:, HD:] = jnp.ones((ROWS, HD), BF16)
    copies = []
    for r in range(0, ROWS, TILE):
        rows = slice(r, r + TILE)
        x = x_ref[rows, :]
        kv_sum = kv_in[rows, :] + jnp.dot(x, wkv_ref[1], preferred_element_type=F32)
        q_sum = q_in[rows, :] + jnp.dot(x, wq_ref[1], preferred_element_type=F32)
        squares = sq_in[rows, :] + squares_of(x)
        mean = jnp.sum(squares, axis=1, keepdims=True) / D
        inv_norm = jnp.broadcast_to(lax.rsqrt(mean + 1e-05), (TILE, HD))
        cosine, sine = cos_ref[rows, :], sin_ref[rows, :]
        keys = turn(kv_sum[:, :HD] * inv_norm, cosine, sine).astype(BF16)
        values = (kv_sum[:, HD:] * inv_norm).astype(BF16)
        keys_buf[rows, :] = keys
        values_buf[rows, :HD] = values
        if r == 0:
            indices.wait()
        for p in range(0, TILE, PAGE):
            page = (r + p) // PAGE
            both = jnp.concatenate([keys[p : p + PAGE], values[p : p + PAGE]], axis=0)
            page_buf[page] = jnp.dot(picker, both, preferred_element_type=F32).astype(BF16)
            target = send_out.at[index_ref[page, PUSH]]
            copies.append(pltpu.make_async_copy(page_buf.at[page], target, page_sems.at[page]))
            copies[-1].start()
        for head in range(HEADS):
            part = q_sum[:, head * HD : (head + 1) * HD] * inv_norm
            q_buf[head, rows, :] = turn(part, cosine, sine).astype(BF16)
        span = pl.ds(r, TILE)
        results = (
            (q_buf.at[:, span, :], q_out.at[:, span, :]),
            (keys_buf.at[span, :], keys_out.at[span, :]),
            (values_buf.at[span, :], values_out.at[span, :]),
        )
        for i, (source, target) in enumerate(results):
            copies.append(pltpu.make_async_copy(source, target, sems.at[3 * (r // TILE) + i]))
            copies[-1].start()
    for copy in copies:
        copy.wait()


def project_late(table, block, sums, weights, cosine, sine):
    results = [(HEADS, ROWS, HD), (ROWS, HD), (ROWS, 2 * HD)]
    return pl.pallas_call(
        late_kernel,
        out_shape=[pltpu.HBM(x, BF16) for x in results]
        + [pltpu.HBM((POOL * PUSH_CAP, 2 * PAGE, HD), BF16)],
        in_specs=[VMEM] * 9,
        out_specs=[HBM] * 4,
        scratch_shapes=[
            *[pltpu.VMEM(x, BF16) for x in results],
            pltpu.VMEM((NEW_PAGES, 2 * PAGE, HD), BF16),
            pltpu.SMEM((24, HD), jnp.int32),
            pltpu.SemaphoreType.DMA,
            pltpu.SemaphoreType.DMA((3 * ROWS // TILE,)),
            pltpu.SemaphoreType.DMA((NEW_PAGES,)),
        ],
        compiler_params=params(16),
        cost_estimate=cost(0, 1),
        name="project_late",
    )(table, block, *sums, *weights, cosine, sine)


def dot_nt(a, b):
    return lax.dot_general(a, b, (((1,), (1,)), ((), ())), preferred_element_type=F32)


def attend_kernel(q_ref, own_keys_ref, own_values_ref, keys_ref, values_ref, out_ref, *scratch):
    q_buf, own_keys, own_values, sems = scratch
    copies = [
        pltpu.make_async_copy(source, target, sems.at[i])
        for i, (source, target) in enumerate(
            ((q_ref, q_buf), (own_keys_ref, own_keys), (own_values_ref, own_values))
        )
    ]
    for copy in copies:
        copy.start()
    for copy in copies:
        copy.wait()
    block = 256
    allowed = lax.broadcasted_iota(jnp.int32, (block, block), 0) >= lax.broadcasted_iota(
        jnp.int32, (block, block), 1
    )
    for head in range(HEADS):
        lanes = slice(head * HD, (head + 1) * HD)
        for b in range(ROWS // block):
            rows = slice(b * block, (b + 1) * block)
            queries = q_buf[head, rows, :]
            own = dot_nt(queries, own_keys[: (b + 1) * block, :])
            diagonal = jnp.where(allowed, own[:, b * block :], -1e30)
            parts = [(diagonal, own_values[rows, :])]
            if b:
                parts.append((own[:, : b * block], own_values[: b * block, :]))
            parts.append((dot_nt(queries, keys_ref[...]), values_ref[...]))
            tops = [jnp.max(scores, axis=1, keepdims=True) for scores, _ in parts]
            top = functools.reduce(jnp.maximum, tops)
            both = jnp.zeros((block, 2 * HD), F32)
            for scores, held in parts:
                weights = jnp.exp2((scores - top) * SCALE).astype(BF16)
                both += jnp.dot(weights, held, preferred_element_type=F32)
            out_ref[rows, lanes] = (both[:, :HD] / both[:, HD:]).astype(BF16)


def attend(queries, own_keys, own_values, keys, values):
    return pl.pallas_call(
        attend_kernel,
        out_shape=shape((ROWS, QW), BF16),
        in_specs=[HBM] * 3 + [VMEM] * 2,
        out_specs=VMEM,
        scratch_shapes=[
            pltpu.VMEM((HEADS, ROWS, HD), BF16),
            pltpu.VMEM((ROWS, HD), BF16),
            pltpu.VMEM((ROWS, 2 * HD), BF16),
            pltpu.SemaphoreType.DMA((3,)),
        ],
        compiler_params=params(40),
        cost_estimate=cost(2 * ROWS * 4 * 2560 * 512, 8 * MIB),
        name="attend",
    )(hbm(queries), hbm(own_keys), hbm(own_values), keys, values)


def place_kernel(table_ref, received_ref, out_ref, buffer, sems):
    group = 4
    copies = []
    for i in range(SLOTS):
        source = table_ref[PLACE, i]
        page = received_ref[jnp.maximum(source - 1, 0)]
        buffer[i] = jnp.where(source > 0, page, jnp.zeros_like(page))
        if i % group == group - 1:
            slots = pl.ds(i + 1 - group, group)
            copy = pltpu.make_async_copy(
                buffer.at[slots], out_ref.at[slots], sems.at[i // group]
            )
            copy.start()
            copies.append(copy)
    for copy in copies:
        copy.wait()


def place_pages(table, received):
    return pl.pallas_call(
        place_kernel,
        out_shape=pltpu.HBM((SLOTS, 2 * PAGE, HD), BF16),
        in_specs=[SMEM, VMEM],
        out_specs=HBM,
        scratch_shapes=[
            pltpu.VMEM((SLOTS, 2 * PAGE, HD), BF16),
            pltpu.SemaphoreType.DMA((SLOTS // 4,)),
        ],
        compiler_params=params(8),
        cost_estimate=cost(0, 2 * MIB),
        name="place_pages",
    )(table, received)


def shift(values, steps):
    pairs = [(i, ((i // 2 + steps[i % 2]) % 4) * 2 + i % 2) for i in range(8)]
    return lax.ppermute(values, "tp", pairs)


def swap(values):
    return lax.ppermute(values, "tp", [(i, i ^ 1) for i in range(8)])


def rope_tables(row_count, offset):
    half_dim = HD // 2
    frequency = 500000.0 ** (-(jnp.arange(half_dim, dtype=F32) * (2.0 / HD)))
    place = (offset + jnp.arange(row_count, dtype=jnp.int32)).astype(F32)
    angles = place[:, None] * frequency[None, :]
    cosine, sine = jnp.cos(angles), jnp.sin(angles)
    return jnp.concatenate([cosine, cosine], 1), jnp.concatenate([-sine, sine], 1)


def exchange(values):
    return lax.all_to_all(values, "pool", split_axis=0, concat_axis=0, tiled=True)


def body(hidden, w_query, w_keyval, store, page_owner, page_slot, new_owner):
    near = shift(hidden, (1, -1))
    table, packed, again = prelude(
        page_owner, page_slot, new_owner, store.reshape(64, 2 * PAGE, HD), hidden
    )
    pages = exchange(packed)
    back = shift(again, (-1, 1))
    tables = rope_tables(ROWS, PAGES * PAGE)
    weights = (w_query, w_keyval)
    blocks = ((OWN, True), (OWN, False))
    sums = project(blocks, [swap(hidden)], [hidden], *weights, tokens=tables)
    (near,) = after((sums[2],), near)
    far = shift(near, (1, -1))
    blocks = ((NEAR, False), (BACK, False))
    sums = project(blocks, [], [near, back], *weights, sums, flops=HIDES)
    blocks, ahead = ((NEAR, True), (BACK, True)), ((FAR, False), (FAR, True))
    held = [swap(near), swap(back)]
    *sums, last_q, last_kv = project(blocks, held, [], *weights, sums, ahead)
    (far,) = after((sums[2],), far)
    other = swap(far)
    sums = project_far(far, (last_q, last_kv), sums)
    queries, own_keys, own_values, send = project_late(
        table, other, sums, (last_q, last_kv), *tables
    )
    received = exchange(send)
    keys, values = split_pages(table, pages)
    attended = attend(queries, own_keys, own_values, keys, values)
    placed = place_pages(table, received)
    return attended, placed.reshape(SLOTS, 1, PAGE, 2, HD)


def solution(mesh):
    in_specs = (
        P("pool", "tp"),
        P(None, "tp"),
        P(None, "tp"),
        P("pool", "tp", None, None, None),
        P(),
        P(),
        P(),
    )
    out_specs = (P("pool", "tp"), P("pool", "tp", None, None, None))
    return jax.shard_map(body, mesh=mesh, in_specs=in_specs, out_specs=out_specs, check_vma=False)
```

```python
import functools
import math

import jax
import jax.numpy as jnp
from jax import lax
from jax.experimental import pallas as pl
from jax.experimental.pallas import tpu as pltpu
from jax.sharding import PartitionSpec as P

D = 8192
HD = 128
PAGE = 64
CAP = 4
PUSH_CAP = 2
HEADS = 4
FEAT = 1024
QW = 512
KVW = 256
POOL = 16
PAGES = 32
NEW_PAGES = 8
SLOTS = 32
ROWS = 512
PUSH, TAKE, PLACE = 4, 16, 17
MIB = 1024 * 1024
SCALE = math.log2(math.e) / math.sqrt(HD)
HIDES = 20_000_000_000
F32 = jnp.float32
BF16 = jnp.bfloat16
ANY = pl.BlockSpec(memory_space=pl.ANY)
HBM = pl.BlockSpec(memory_space=pltpu.HBM)
VMEM = pl.BlockSpec(memory_space=pltpu.VMEM)
SMEM = pl.BlockSpec(memory_space=pltpu.SMEM)


def params(mib):
    return pltpu.CompilerParams(vmem_limit_bytes=mib * MIB)


def cost(flops, nbytes):
    return pl.CostEstimate(flops=flops, bytes_accessed=nbytes, transcendentals=0)


def hbm(array):
    return pltpu.with_memory_space_constraint(array, pltpu.HBM)


def shape(dims, dtype):
    return jax.ShapeDtypeStruct(dims, dtype)


def fill_table(owners, slots, targets, out_ref):
    me = lax.axis_index("pool")
    out_ref[...] = jnp.zeros_like(out_ref)
    lanes = lax.broadcasted_iota(jnp.int32, owners.shape, 1)
    rows = lax.broadcasted_iota(jnp.int32, owners.shape, 0)
    ranks = jnp.zeros_like(owners)
    for j in range(PAGES):
        ranks += ((owners == owners[:, j : j + 1]) & (lanes > j)).astype(jnp.int32)
    for k in range(CAP):
        chosen = jnp.where((owners == me) & (ranks == k), slots, 0)
        out_ref[:POOL, k : k + 1] = jnp.sum(chosen, axis=1, keepdims=True)
    mine = jnp.where(rows == me, owners * CAP + ranks, 0)
    out_ref[TAKE : TAKE + 1, :PAGES] = jnp.sum(mine, axis=0, keepdims=True)
    lanes = lax.broadcasted_iota(jnp.int32, targets.shape, 1)
    rows = lax.broadcasted_iota(jnp.int32, targets.shape, 0)
    kept = (targets == me).astype(jnp.int32)
    ranks = jnp.zeros_like(targets)
    slot = jnp.zeros_like(targets)
    for j in range(NEW_PAGES):
        later = rows > j
        ranks += ((targets == targets[j : j + 1, :]) & later).astype(jnp.int32)
        slot += jnp.where(later, kept[j : j + 1, :], 0)
    mine = jnp.where(lanes == me, targets * PUSH_CAP + ranks, 0)
    out_ref[:NEW_PAGES, PUSH : PUSH + 1] = jnp.sum(mine, axis=1, keepdims=True)
    of_request = jnp.sum(kept, axis=0, keepdims=True)
    for r in range(POOL):
        slot += jnp.where(lanes > r, of_request[:, r : r + 1], 0)
    source = jnp.zeros((NEW_PAGES, SLOTS), jnp.int32)
    slot_lanes = lax.broadcasted_iota(jnp.int32, source.shape, 1)
    for r in range(POOL):
        hit = (kept[:, r : r + 1] > 0) & (slot[:, r : r + 1] == slot_lanes)
        source += jnp.where(hit, r * PUSH_CAP + ranks[:, r : r + 1] + 1, 0)
    out_ref[PLACE : PLACE + 1, :SLOTS] = jnp.sum(source, axis=0, keepdims=True)


def prelude_kernel(*refs):
    owner_in, slot_in, target_in, store_in, hidden_in, table_ref, out_ref, hidden_out = refs[:8]
    owner_ref, slot_ref, target_ref, store_ref, hidden_ref, index_ref, sems, page_sems = refs[8:]
    pairs = (
        (owner_in, owner_ref),
        (slot_in, slot_ref),
        (target_in, target_ref),
        (store_in, store_ref),
        (hidden_in, hidden_ref),
    )
    copies = [pltpu.make_async_copy(x, y, sems.at[i]) for i, (x, y) in enumerate(pairs)]
    for copy in copies:
        copy.start()
    for copy in copies[:3]:
        copy.wait()
    fill_table(owner_ref[...], slot_ref[...], target_ref[...], table_ref)
    indices = pltpu.make_async_copy(table_ref, index_ref, sems.at[5])
    indices.start()
    copies[4].wait()
    hidden_copy = pltpu.make_async_copy(hidden_ref, hidden_out, sems.at[6])
    hidden_copy.start()
    indices.wait()
    copies[3].wait()
    pages = [
        pltpu.make_async_copy(
            store_ref.at[index_ref[i // CAP, i % CAP]], out_ref.at[i], page_sems.at[i]
        )
        for i in range(POOL * CAP)
    ]
    for page in pages:
        page.start()
    for page in pages:
        page.wait()
    hidden_copy.wait()


def prelude(page_owner, page_slot, new_owner, store, hidden):
    return pl.pallas_call(
        prelude_kernel,
        out_shape=[
            shape((24, HD), jnp.int32),
            pltpu.HBM((POOL * CAP, 2 * PAGE, HD), BF16),
            pltpu.HBM(hidden.shape, BF16),
        ],
        in_specs=[HBM] * 5,
        out_specs=[VMEM, HBM, HBM],
        scratch_shapes=[
            pltpu.VMEM((POOL, PAGES), jnp.int32),
            pltpu.VMEM((POOL, PAGES), jnp.int32),
            pltpu.VMEM((NEW_PAGES, POOL), jnp.int32),
            pltpu.VMEM(store.shape, BF16),
            pltpu.VMEM(hidden.shape, BF16),
            pltpu.SMEM((24, HD), jnp.int32),
            pltpu.SemaphoreType.DMA((7,)),
            pltpu.SemaphoreType.DMA((POOL * CAP,)),
        ],
        compiler_params=params(8),
        cost_estimate=cost(0, 1),
        name="prelude",
    )(*[hbm(x) for x in (page_owner, page_slot, new_owner.T, store, hidden)])


def block_index(steps, other_core):
    index = lax.axis_index("tp")
    core = lax.rem(index, 2)
    if other_core:
        core = 1 - core
    z = lax.rem(index // 2 + jnp.where(core == 0, steps[0], steps[1]), 4)
    return 2 * z + core


def squares_of(rows):
    wide = rows.astype(F32)
    total = None
    for lane in range(0, FEAT, HD):
        part = wide[:, lane : lane + HD]
        total = part * part if total is None else total + part * part
    return total


def weight_copies(refs, buffers, sems, blocks):
    copies = []
    for i, (steps, other) in enumerate(blocks):
        rows = pl.ds(pl.multiple_of(block_index(steps, other) * FEAT, FEAT), FEAT)
        copies.append(
            [
                pltpu.make_async_copy(ref.at[rows, :], buffer.at[i], sems.at[len(refs) * i + j])
                for j, (ref, buffer) in enumerate(zip(refs, buffers))
            ]
        )
    for group in copies:
        for copy in group:
            copy.start()
    return copies


OWN, NEAR, BACK, FAR = (0, 0), (3, 1), (1, 3), (2, 2)
TILE = 128


def project_kernel(blocks, held, has_sums, tokens, ahead, *refs):
    count = len(blocks)
    x_refs, refs = refs[:count], refs[count:]
    wq_ref, wkv_ref, refs = refs[0], refs[1], refs[2:]
    before, refs = (refs[:3], refs[3:]) if has_sums else (None, refs)
    refs = refs[tokens:]
    sums, refs = refs[:3], refs[3:]
    fetched, refs = (refs[:2], refs[2:]) if ahead else (None, refs)
    x_buf, wq_buf, wkv_buf, sems, x_sems, ahead_sems = refs
    copies = weight_copies((wq_ref, wkv_ref), (wq_buf, wkv_buf), sems, blocks)
    x_copies = {}
    for i in range(held, count):
        x_copies[i] = pltpu.make_async_copy(x_refs[i], x_buf.at[i - held], x_sems.at[i - held])
        x_copies[i].start()
    later = weight_copies((wq_ref, wkv_ref), fetched, ahead_sems, ahead) if ahead else []
    for i in range(count):
        copies[i][0].wait()
        copies[i][1].wait()
        if i in x_copies:
            x_copies[i].wait()
        for r in range(0, ROWS, TILE):
            rows = slice(r, r + TILE)
            x = x_refs[i][rows, :] if i < held else x_buf[i - held, rows, :]
            parts = (
                jnp.dot(x, wq_buf[i], preferred_element_type=F32),
                jnp.dot(x, wkv_buf[i], preferred_element_type=F32),
                squares_of(x),
            )
            for j, part in enumerate(parts):
                if i > 0:
                    sums[j][rows, :] += part
                elif has_sums:
                    sums[j][rows, :] = before[j][rows, :] + part
                else:
                    sums[j][rows, :] = part
    for group in later:
        for copy in group:
            copy.wait()


def project(blocks, held, direct, w_query, w_keyval, sums=(), ahead=(), tokens=(), flops=0):
    count = len(blocks)
    shapes = [shape((ROWS, w), F32) for w in (QW, KVW, HD)]
    if ahead:
        shapes += [shape((len(ahead), FEAT, w), BF16) for w in (QW, KVW)]
    return pl.pallas_call(
        functools.partial(project_kernel, blocks, len(held), bool(sums), len(tokens), ahead),
        out_shape=shapes,
        in_specs=[VMEM] * len(held)
        + [HBM] * (len(direct) + 2)
        + [VMEM] * len(sums)
        + [ANY] * len(tokens),
        out_specs=[VMEM] * len(shapes),
        scratch_shapes=[
            pltpu.VMEM((max(len(direct), 1), ROWS, FEAT), BF16),
            pltpu.VMEM((count, FEAT, QW), BF16),
            pltpu.VMEM((count, FEAT, KVW), BF16),
            pltpu.SemaphoreType.DMA((2 * count,)),
            pltpu.SemaphoreType.DMA((max(len(direct), 1),)),
            pltpu.SemaphoreType.DMA((max(2 * len(ahead), 1),)),
        ],
        compiler_params=params(24),
        cost_estimate=cost(flops, 1),
        name="project",
    )(*held, *[hbm(x) for x in (*direct, w_query, w_keyval)], *sums, *tokens)


def far_kernel(x_ref, wq_ref, wkv_ref, *refs):
    before, sums = refs[:3], refs[3:]
    for r in range(0, ROWS, TILE):
        rows = slice(r, r + TILE)
        x = x_ref[rows, :]
        sums[0][rows, :] = before[0][rows, :] + jnp.dot(x, wq_ref[0], preferred_element_type=F32)
        sums[1][rows, :] = before[1][rows, :] + jnp.dot(x, wkv_ref[0], preferred_element_type=F32)
        sums[2][rows, :] = before[2][rows, :] + squares_of(x)


def project_far(block, weights, sums):
    return pl.pallas_call(
        far_kernel,
        out_shape=[pltpu.HBM((ROWS, QW), F32)] + [shape((ROWS, w), F32) for w in (KVW, HD)],
        in_specs=[VMEM] * 6,
        out_specs=[VMEM] * 3,
        compiler_params=params(16),
        cost_estimate=cost(0, 1),
        name="project_far",
    )(block, *weights, *sums)


def after_kernel(*refs):
    pass


def after(tokens, *arrays, flops=0):
    count, skip = len(arrays), len(tokens)
    return pl.pallas_call(
        after_kernel,
        out_shape=[shape(x.shape, x.dtype) for x in arrays],
        in_specs=[ANY] * (count + skip),
        out_specs=[ANY] * count,
        input_output_aliases={i + skip: i for i in range(count)},
        compiler_params=params(1),
        cost_estimate=cost(flops, 1),
        name="after",
    )(*tokens, *arrays)


def turn(values, cosine, sine):
    return values * cosine + pltpu.roll(values, HD // 2, 1) * sine


def keyval_kernel(table_ref, x_ref, kv_in, sq_in, wkv_ref, cos_ref, sin_ref, *refs):
    keys_out, values_out, inv_out, x_out, send_out = refs[:5]
    keys_buf, values_buf, inv_buf, page_buf, index_ref, sems, page_sems = refs[5:]
    indices = pltpu.make_async_copy(table_ref, index_ref, sems.at[0])
    indices.start()
    copies = [pltpu.make_async_copy(x_ref, x_out, sems.at[1])]
    copies[0].start()
    row = lax.broadcasted_iota(jnp.int32, (2 * PAGE, 2 * PAGE), 0)
    column = lax.broadcasted_iota(jnp.int32, (2 * PAGE, 2 * PAGE), 1)
    picker = (column == (row >> 1) + (row & 1) * PAGE).astype(BF16)
    values_buf[:, HD:] = jnp.ones((ROWS, HD), BF16)
    for r in range(0, ROWS, TILE):
        rows = slice(r, r + TILE)
        x = x_ref[rows, :]
        kv_sum = kv_in[rows, :] + jnp.dot(x, wkv_ref[1], preferred_element_type=F32)
        squares = sq_in[rows, :] + squares_of(x)
        mean = jnp.sum(squares, axis=1, keepdims=True) / D
        inv_norm = jnp.broadcast_to(lax.rsqrt(mean + 1e-05), (TILE, HD))
        inv_buf[rows, :] = inv_norm
        keys = turn(kv_sum[:, :HD] * inv_norm, cos_ref[rows, :], sin_ref[rows, :]).astype(BF16)
        values = (kv_sum[:, HD:] * inv_norm).astype(BF16)
        keys_buf[rows, :] = keys
        values_buf[rows, :HD] = values
        if r == 0:
            indices.wait()
        for p in range(0, TILE, PAGE):
            page = (r + p) // PAGE
            both = jnp.concatenate([keys[p : p + PAGE], values[p : p + PAGE]], axis=0)
            page_buf[page] = jnp.dot(picker, both, preferred_element_type=F32).astype(BF16)
            target = send_out.at[index_ref[page, PUSH]]
            copies.append(pltpu.make_async_copy(page_buf.at[page], target, page_sems.at[page]))
            copies[-1].start()
    results = ((keys_buf, keys_out), (values_buf, values_out), (inv_buf, inv_out))
    for i, (source, target) in enumerate(results):
        copies.append(pltpu.make_async_copy(source, target, sems.at[2 + i]))
        copies[-1].start()
    for copy in copies:
        copy.wait()


def project_keyval(table, block, sums, weights, cosine, sine):
    kept = [((ROWS, HD), BF16), ((ROWS, 2 * HD), BF16), ((ROWS, HD), F32)]
    sent = (POOL * PUSH_CAP, 2 * PAGE, HD)
    return pl.pallas_call(
        keyval_kernel,
        out_shape=[pltpu.HBM(*x) for x in (*kept, ((ROWS, FEAT), BF16), (sent, BF16))],
        in_specs=[VMEM] * 7,
        out_specs=[HBM] * 5,
        scratch_shapes=[
            *[pltpu.VMEM(*x) for x in kept],
            pltpu.VMEM((NEW_PAGES, 2 * PAGE, HD), BF16),
            pltpu.SMEM((24, HD), jnp.int32),
            pltpu.SemaphoreType.DMA((5,)),
            pltpu.SemaphoreType.DMA((NEW_PAGES,)),
        ],
        compiler_params=params(16),
        cost_estimate=cost(0, 1),
        name="project_keyval",
    )(table, block, *sums, weights, cosine, sine)


def dot_nt(a, b):
    return lax.dot_general(a, b, (((1,), (1,)), ((), ())), preferred_element_type=F32)


def attend_kernel(table_ref, pages_ref, *refs):
    sources, wq_ref, out_ref, refs = refs[:7], refs[7], refs[8], refs[9:]
    targets, wq_buf, index_ref, q_buf, keys, values, sems = refs[:7], *refs[7:]
    q_sum, x, inv_norm, cosine, sine, own_keys, own_values = targets
    indices = pltpu.make_async_copy(table_ref, index_ref, sems.at[8])
    indices.start()
    copies = [pltpu.make_async_copy(a, b, sems.at[i]) for i, (a, b) in enumerate(zip(sources, targets))]
    rows = pl.ds(pl.multiple_of(block_index(FAR, True) * FEAT, FEAT), FEAT)
    copies.insert(0, pltpu.make_async_copy(wq_ref.at[rows, :], wq_buf, sems.at[7]))
    for copy in copies:
        copy.start()
    row = lax.broadcasted_iota(jnp.int32, (2 * PAGE, 2 * PAGE), 0)
    column = lax.broadcasted_iota(jnp.int32, (2 * PAGE, 2 * PAGE), 1)
    wanted = jnp.where(row < PAGE, 2 * row, 2 * (row - PAGE) + 1)
    picker = (column == wanted).astype(BF16)
    values[:, HD:] = jnp.ones((PAGES * PAGE, HD), BF16)
    indices.wait()
    for page in range(PAGES):
        both = jnp.dot(picker, pages_ref[index_ref[TAKE, page]], preferred_element_type=F32)
        rows = slice(page * PAGE, (page + 1) * PAGE)
        keys[rows, :] = both[:PAGE].astype(BF16)
        values[rows, :HD] = both[PAGE:].astype(BF16)
    for copy in copies:
        copy.wait()
    for r in range(0, ROWS, TILE):
        rows = slice(r, r + TILE)
        total = q_sum[rows, :] + jnp.dot(x[rows, :], wq_buf[...], preferred_element_type=F32)
        for head in range(HEADS):
            part = total[:, head * HD : (head + 1) * HD] * inv_norm[rows, :]
            q_buf[head, rows, :] = turn(part, cosine[rows, :], sine[rows, :]).astype(BF16)
    block = 256
    allowed = lax.broadcasted_iota(jnp.int32, (block, block), 0) >= lax.broadcasted_iota(
        jnp.int32, (block, block), 1
    )
    for head in range(HEADS):
        lanes = slice(head * HD, (head + 1) * HD)
        for b in range(ROWS // block):
            rows = slice(b * block, (b + 1) * block)
            queries = q_buf[head, rows, :]
            own = dot_nt(queries, own_keys[: (b + 1) * block, :])
            diagonal = jnp.where(allowed, own[:, b * block :], -1e30)
            parts = [(diagonal, own_values[rows, :])]
            if b:
                parts.append((own[:, : b * block], own_values[: b * block, :]))
            parts.append((dot_nt(queries, keys[...]), values[...]))
            tops = [jnp.max(scores, axis=1, keepdims=True) for scores, _ in parts]
            top = functools.reduce(jnp.maximum, tops)
            both = jnp.zeros((block, 2 * HD), F32)
            for scores, held in parts:
                weights = jnp.exp2((scores - top) * SCALE).astype(BF16)
                both += jnp.dot(weights, held, preferred_element_type=F32)
            out_ref[rows, lanes] = (both[:, :HD] / both[:, HD:]).astype(BF16)


def attend(table, pages, sources, w_query):
    return pl.pallas_call(
        attend_kernel,
        out_shape=shape((ROWS, QW), BF16),
        in_specs=[VMEM] * 2 + [HBM] * (len(sources) + 1),
        out_specs=VMEM,
        scratch_shapes=[
            *[pltpu.VMEM(x.shape, x.dtype) for x in sources],
            pltpu.VMEM((FEAT, QW), BF16),
            pltpu.SMEM((24, HD), jnp.int32),
            pltpu.VMEM((HEADS, ROWS, HD), BF16),
            pltpu.VMEM((PAGES * PAGE, HD), BF16),
            pltpu.VMEM((PAGES * PAGE, 2 * HD), BF16),
            pltpu.SemaphoreType.DMA((9,)),
        ],
        compiler_params=params(40),
        cost_estimate=cost(2 * ROWS * 4 * 2560 * 512, 8 * MIB),
        name="attend",
    )(table, pages, *[hbm(x) for x in (*sources, w_query)])


def place_kernel(table_ref, received_ref, out_ref, buffer, sems):
    group = 4
    copies = []
    for i in range(SLOTS):
        source = table_ref[PLACE, i]
        page = received_ref[jnp.maximum(source - 1, 0)]
        buffer[i] = jnp.where(source > 0, page, jnp.zeros_like(page))
        if i % group == group - 1:
            slots = pl.ds(i + 1 - group, group)
            copy = pltpu.make_async_copy(
                buffer.at[slots], out_ref.at[slots], sems.at[i // group]
            )
            copy.start()
            copies.append(copy)
    for copy in copies:
        copy.wait()


def place_pages(table, received):
    return pl.pallas_call(
        place_kernel,
        out_shape=pltpu.HBM((SLOTS, 2 * PAGE, HD), BF16),
        in_specs=[SMEM, VMEM],
        out_specs=HBM,
        scratch_shapes=[
            pltpu.VMEM((SLOTS, 2 * PAGE, HD), BF16),
            pltpu.SemaphoreType.DMA((SLOTS // 4,)),
        ],
        compiler_params=params(8),
        cost_estimate=cost(0, 2 * MIB),
        name="place_pages",
    )(table, received)


def shift(values, steps):
    pairs = [(i, ((i // 2 + steps[i % 2]) % 4) * 2 + i % 2) for i in range(8)]
    return lax.ppermute(values, "tp", pairs)


def swap(values):
    return lax.ppermute(values, "tp", [(i, i ^ 1) for i in range(8)])


def rope_tables(row_count, offset):
    half_dim = HD // 2
    frequency = 500000.0 ** (-(jnp.arange(half_dim, dtype=F32) * (2.0 / HD)))
    place = (offset + jnp.arange(row_count, dtype=jnp.int32)).astype(F32)
    angles = place[:, None] * frequency[None, :]
    cosine, sine = jnp.cos(angles), jnp.sin(angles)
    return jnp.concatenate([cosine, cosine], 1), jnp.concatenate([-sine, sine], 1)


def exchange(values):
    return lax.all_to_all(values, "pool", split_axis=0, concat_axis=0, tiled=True)


def body(hidden, w_query, w_keyval, store, page_owner, page_slot, new_owner):
    near = shift(hidden, (1, -1))
    table, packed, again = prelude(
        page_owner, page_slot, new_owner, store.reshape(64, 2 * PAGE, HD), hidden
    )
    pages = exchange(packed)
    back = shift(again, (-1, 1))
    tables = rope_tables(ROWS, PAGES * PAGE)
    weights = (w_query, w_keyval)
    blocks = ((OWN, True), (OWN, False))
    sums = project(blocks, [swap(hidden)], [hidden], *weights, tokens=tables, flops=HIDES)
    (near,) = after((sums[2],), near)
    far = shift(near, (1, -1))
    blocks = ((NEAR, False), (BACK, False))
    sums = project(blocks, [near, back], [], *weights, sums, flops=HIDES)
    blocks, ahead = ((NEAR, True), (BACK, True)), ((FAR, False), (FAR, True))
    held = [swap(near), swap(back)]
    *sums, last_q, last_kv = project(blocks, held, [], *weights, sums, ahead)
    (far,) = after((sums[2],), far)
    other = swap(far)
    sums = project_far(far, (last_q, last_kv), sums)
    own_keys, own_values, inv_norm, other, send = project_keyval(
        table, other, sums[1:], last_kv, *tables
    )
    received = exchange(send)
    sources = (sums[0], other, inv_norm, *tables, own_keys, own_values)
    attended = attend(table, pages, sources, w_query)
    placed = place_pages(table, received)
    return attended, placed.reshape(SLOTS, 1, PAGE, 2, HD)


def solution(mesh):
    in_specs = (
        P("pool", "tp"),
        P(None, "tp"),
        P(None, "tp"),
        P("pool", "tp", None, None, None),
        P(),
        P(),
        P(),
    )
    out_specs = (P("pool", "tp"), P("pool", "tp", None, None, None))
    return jax.shard_map(body, mesh=mesh, in_specs=in_specs, out_specs=out_specs, check_vma=False)
```

```python
import functools
import math

import jax
import jax.numpy as jnp
from jax import lax
from jax.experimental import pallas as pl
from jax.experimental.pallas import tpu as pltpu
from jax.sharding import PartitionSpec as P

D = 8192
HD = 128
PAGE = 64
CAP = 4
PUSH_CAP = 2
HEADS = 4
FEAT = 1024
QW = 512
KVW = 256
POOL = 16
PAGES = 32
NEW_PAGES = 8
SLOTS = 32
ROWS = 512
PUSH, TAKE, PLACE = 4, 16, 17
MIB = 1024 * 1024
SCALE = math.log2(math.e) / math.sqrt(HD)
HIDES = 20_000_000_000
F32 = jnp.float32
BF16 = jnp.bfloat16
ANY = pl.BlockSpec(memory_space=pl.ANY)
HBM = pl.BlockSpec(memory_space=pltpu.HBM)
VMEM = pl.BlockSpec(memory_space=pltpu.VMEM)
SMEM = pl.BlockSpec(memory_space=pltpu.SMEM)


def params(mib):
    return pltpu.CompilerParams(vmem_limit_bytes=mib * MIB)


def cost(flops, nbytes):
    return pl.CostEstimate(flops=flops, bytes_accessed=nbytes, transcendentals=0)


def hbm(array):
    return pltpu.with_memory_space_constraint(array, pltpu.HBM)


def shape(dims, dtype):
    return jax.ShapeDtypeStruct(dims, dtype)


def fill_table(owners, slots, targets, out_ref):
    me = lax.axis_index("pool")
    out_ref[...] = jnp.zeros_like(out_ref)
    lanes = lax.broadcasted_iota(jnp.int32, owners.shape, 1)
    rows = lax.broadcasted_iota(jnp.int32, owners.shape, 0)
    ranks = jnp.zeros_like(owners)
    for j in range(PAGES):
        ranks += ((owners == owners[:, j : j + 1]) & (lanes > j)).astype(jnp.int32)
    for k in range(CAP):
        chosen = jnp.where((owners == me) & (ranks == k), slots, 0)
        out_ref[:POOL, k : k + 1] = jnp.sum(chosen, axis=1, keepdims=True)
    mine = jnp.where(rows == me, owners * CAP + ranks, 0)
    out_ref[TAKE : TAKE + 1, :PAGES] = jnp.sum(mine, axis=0, keepdims=True)
    lanes = lax.broadcasted_iota(jnp.int32, targets.shape, 1)
    rows = lax.broadcasted_iota(jnp.int32, targets.shape, 0)
    kept = (targets == me).astype(jnp.int32)
    ranks = jnp.zeros_like(targets)
    slot = jnp.zeros_like(targets)
    for j in range(NEW_PAGES):
        later = rows > j
        ranks += ((targets == targets[j : j + 1, :]) & later).astype(jnp.int32)
        slot += jnp.where(later, kept[j : j + 1, :], 0)
    mine = jnp.where(lanes == me, targets * PUSH_CAP + ranks, 0)
    out_ref[:NEW_PAGES, PUSH : PUSH + 1] = jnp.sum(mine, axis=1, keepdims=True)
    of_request = jnp.sum(kept, axis=0, keepdims=True)
    for r in range(POOL):
        slot += jnp.where(lanes > r, of_request[:, r : r + 1], 0)
    source = jnp.zeros((NEW_PAGES, SLOTS), jnp.int32)
    slot_lanes = lax.broadcasted_iota(jnp.int32, source.shape, 1)
    for r in range(POOL):
        hit = (kept[:, r : r + 1] > 0) & (slot[:, r : r + 1] == slot_lanes)
        source += jnp.where(hit, r * PUSH_CAP + ranks[:, r : r + 1] + 1, 0)
    out_ref[PLACE : PLACE + 1, :SLOTS] = jnp.sum(source, axis=0, keepdims=True)


def prelude_kernel(*refs):
    owner_in, slot_in, target_in, store_in, hidden_in, table_ref, out_ref, hidden_out = refs[:8]
    owner_ref, slot_ref, target_ref, store_ref, hidden_ref, index_ref, sems, page_sems = refs[8:]
    pairs = (
        (owner_in, owner_ref),
        (slot_in, slot_ref),
        (target_in, target_ref),
        (store_in, store_ref),
        (hidden_in, hidden_ref),
    )
    copies = [pltpu.make_async_copy(x, y, sems.at[i]) for i, (x, y) in enumerate(pairs)]
    for copy in copies:
        copy.start()
    for copy in copies[:3]:
        copy.wait()
    fill_table(owner_ref[...], slot_ref[...], target_ref[...], table_ref)
    indices = pltpu.make_async_copy(table_ref, index_ref, sems.at[5])
    indices.start()
    copies[4].wait()
    hidden_copy = pltpu.make_async_copy(hidden_ref, hidden_out, sems.at[6])
    hidden_copy.start()
    indices.wait()
    copies[3].wait()
    pages = [
        pltpu.make_async_copy(
            store_ref.at[index_ref[i // CAP, i % CAP]], out_ref.at[i], page_sems.at[i]
        )
        for i in range(POOL * CAP)
    ]
    for page in pages:
        page.start()
    for page in pages:
        page.wait()
    hidden_copy.wait()


def prelude(page_owner, page_slot, new_owner, store, hidden):
    return pl.pallas_call(
        prelude_kernel,
        out_shape=[
            shape((24, HD), jnp.int32),
            pltpu.HBM((POOL * CAP, 2 * PAGE, HD), BF16),
            pltpu.HBM(hidden.shape, BF16),
        ],
        in_specs=[HBM] * 5,
        out_specs=[VMEM, HBM, HBM],
        scratch_shapes=[
            pltpu.VMEM((POOL, PAGES), jnp.int32),
            pltpu.VMEM((POOL, PAGES), jnp.int32),
            pltpu.VMEM((NEW_PAGES, POOL), jnp.int32),
            pltpu.VMEM(store.shape, BF16),
            pltpu.VMEM(hidden.shape, BF16),
            pltpu.SMEM((24, HD), jnp.int32),
            pltpu.SemaphoreType.DMA((7,)),
            pltpu.SemaphoreType.DMA((POOL * CAP,)),
        ],
        compiler_params=params(8),
        cost_estimate=cost(0, 1),
        name="prelude",
    )(*[hbm(x) for x in (page_owner, page_slot, new_owner.T, store, hidden)])


def block_index(steps, other_core):
    index = lax.axis_index("tp")
    core = lax.rem(index, 2)
    if other_core:
        core = 1 - core
    z = lax.rem(index // 2 + jnp.where(core == 0, steps[0], steps[1]), 4)
    return 2 * z + core


def squares_of(rows):
    wide = rows.astype(F32)
    total = None
    for lane in range(0, FEAT, HD):
        part = wide[:, lane : lane + HD]
        total = part * part if total is None else total + part * part
    return total


def weight_copies(refs, buffers, sems, blocks):
    copies = []
    for i, (steps, other) in enumerate(blocks):
        rows = pl.ds(pl.multiple_of(block_index(steps, other) * FEAT, FEAT), FEAT)
        copies.append(
            [
                pltpu.make_async_copy(ref.at[rows, :], buffer.at[i], sems.at[len(refs) * i + j])
                for j, (ref, buffer) in enumerate(zip(refs, buffers))
            ]
        )
    for group in copies:
        for copy in group:
            copy.start()
    return copies


OWN, NEAR, BACK, FAR = (0, 0), (3, 1), (1, 3), (2, 2)
TILE = 128


def project_kernel(blocks, held, has_sums, tokens, ahead, *refs):
    count = len(blocks)
    x_refs, refs = refs[:count], refs[count:]
    wq_ref, wkv_ref, refs = refs[0], refs[1], refs[2:]
    before, refs = (refs[:3], refs[3:]) if has_sums else (None, refs)
    refs = refs[tokens:]
    sums, refs = refs[:3], refs[3:]
    fetched, refs = (refs[:2], refs[2:]) if ahead else (None, refs)
    x_buf, wq_buf, wkv_buf, sems, x_sems, ahead_sems = refs
    copies = weight_copies((wq_ref, wkv_ref), (wq_buf, wkv_buf), sems, blocks)
    x_copies = {}
    for i in range(held, count):
        x_copies[i] = pltpu.make_async_copy(x_refs[i], x_buf.at[i - held], x_sems.at[i - held])
        x_copies[i].start()
    later = weight_copies((wq_ref, wkv_ref), fetched, ahead_sems, ahead) if ahead else []
    for i in range(count):
        copies[i][0].wait()
        copies[i][1].wait()
        if i in x_copies:
            x_copies[i].wait()
        for r in range(0, ROWS, TILE):
            rows = slice(r, r + TILE)
            x = x_refs[i][rows, :] if i < held else x_buf[i - held, rows, :]
            parts = (
                jnp.dot(x, wq_buf[i], preferred_element_type=F32),
                jnp.dot(x, wkv_buf[i], preferred_element_type=F32),
                squares_of(x),
            )
            for j, part in enumerate(parts):
                if i > 0:
                    sums[j][rows, :] += part
                elif has_sums:
                    sums[j][rows, :] = before[j][rows, :] + part
                else:
                    sums[j][rows, :] = part
    for group in later:
        for copy in group:
            copy.wait()


def project(blocks, held, direct, w_query, w_keyval, sums=(), ahead=(), tokens=(), flops=0):
    count = len(blocks)
    shapes = [shape((ROWS, w), F32) for w in (QW, KVW, HD)]
    if ahead:
        shapes += [shape((len(ahead), FEAT, w), BF16) for w in (QW, KVW)]
    return pl.pallas_call(
        functools.partial(project_kernel, blocks, len(held), bool(sums), len(tokens), ahead),
        out_shape=shapes,
        in_specs=[VMEM] * len(held)
        + [HBM] * (len(direct) + 2)
        + [VMEM] * len(sums)
        + [ANY] * len(tokens),
        out_specs=[VMEM] * len(shapes),
        scratch_shapes=[
            pltpu.VMEM((max(len(direct), 1), ROWS, FEAT), BF16),
            pltpu.VMEM((count, FEAT, QW), BF16),
            pltpu.VMEM((count, FEAT, KVW), BF16),
            pltpu.SemaphoreType.DMA((2 * count,)),
            pltpu.SemaphoreType.DMA((max(len(direct), 1),)),
            pltpu.SemaphoreType.DMA((max(2 * len(ahead), 1),)),
        ],
        compiler_params=params(24),
        cost_estimate=cost(flops, 1),
        name="project",
    )(*held, *[hbm(x) for x in (*direct, w_query, w_keyval)], *sums, *tokens)


def far_kernel(x_ref, wq_ref, wkv_ref, *refs):
    before, sums = refs[:3], refs[3:]
    for r in range(0, ROWS, TILE):
        rows = slice(r, r + TILE)
        x = x_ref[rows, :]
        sums[0][rows, :] = before[0][rows, :] + jnp.dot(x, wq_ref[0], preferred_element_type=F32)
        sums[1][rows, :] = before[1][rows, :] + jnp.dot(x, wkv_ref[0], preferred_element_type=F32)
        sums[2][rows, :] = before[2][rows, :] + squares_of(x)


def project_far(block, weights, sums):
    return pl.pallas_call(
        far_kernel,
        out_shape=[pltpu.HBM((ROWS, QW), F32)] + [shape((ROWS, w), F32) for w in (KVW, HD)],
        in_specs=[VMEM] * 6,
        out_specs=[VMEM] * 3,
        compiler_params=params(16),
        cost_estimate=cost(0, 1),
        name="project_far",
    )(block, *weights, *sums)


def after_kernel(*refs):
    pass


def after(tokens, *arrays, flops=0):
    count, skip = len(arrays), len(tokens)
    return pl.pallas_call(
        after_kernel,
        out_shape=[shape(x.shape, x.dtype) for x in arrays],
        in_specs=[ANY] * (count + skip),
        out_specs=[ANY] * count,
        input_output_aliases={i + skip: i for i in range(count)},
        compiler_params=params(1),
        cost_estimate=cost(flops, 1),
        name="after",
    )(*tokens, *arrays)


def turn(values, cosine, sine):
    return values * cosine + pltpu.roll(values, HD // 2, 1) * sine


def keyval_kernel(table_ref, x_ref, kv_in, sq_in, wkv_ref, cos_ref, sin_ref, *refs):
    keys_out, values_out, inv_out, x_out, send_out = refs[:5]
    keys_buf, values_buf, inv_buf, page_buf, index_ref, sems, page_sems = refs[5:]
    indices = pltpu.make_async_copy(table_ref, index_ref, sems.at[0])
    indices.start()
    copies = [pltpu.make_async_copy(x_ref, x_out, sems.at[1])]
    copies[0].start()
    row = lax.broadcasted_iota(jnp.int32, (2 * PAGE, 2 * PAGE), 0)
    column = lax.broadcasted_iota(jnp.int32, (2 * PAGE, 2 * PAGE), 1)
    picker = (column == (row >> 1) + (row & 1) * PAGE).astype(BF16)
    values_buf[:, HD:] = jnp.ones((ROWS, HD), BF16)
    for r in range(0, ROWS, TILE):
        rows = slice(r, r + TILE)
        x = x_ref[rows, :]
        kv_sum = kv_in[rows, :] + jnp.dot(x, wkv_ref[1], preferred_element_type=F32)
        squares = sq_in[rows, :] + squares_of(x)
        mean = jnp.sum(squares, axis=1, keepdims=True) / D
        inv_norm = jnp.broadcast_to(lax.rsqrt(mean + 1e-05), (TILE, HD))
        inv_buf[rows, :] = inv_norm
        keys = turn(kv_sum[:, :HD] * inv_norm, cos_ref[rows, :], sin_ref[rows, :]).astype(BF16)
        values = (kv_sum[:, HD:] * inv_norm).astype(BF16)
        keys_buf[rows, :] = keys
        values_buf[rows, :HD] = values
        if r == 0:
            indices.wait()
        for p in range(0, TILE, PAGE):
            page = (r + p) // PAGE
            both = jnp.concatenate([keys[p : p + PAGE], values[p : p + PAGE]], axis=0)
            page_buf[page] = jnp.dot(picker, both, preferred_element_type=F32).astype(BF16)
            target = send_out.at[index_ref[page, PUSH]]
            copies.append(pltpu.make_async_copy(page_buf.at[page], target, page_sems.at[page]))
            copies[-1].start()
    results = ((keys_buf, keys_out), (values_buf, values_out), (inv_buf, inv_out))
    for i, (source, target) in enumerate(results):
        copies.append(pltpu.make_async_copy(source, target, sems.at[2 + i]))
        copies[-1].start()
    for copy in copies:
        copy.wait()


def project_keyval(table, block, sums, weights, cosine, sine):
    kept = [((ROWS, HD), BF16), ((ROWS, 2 * HD), BF16), ((ROWS, HD), F32)]
    sent = (POOL * PUSH_CAP, 2 * PAGE, HD)
    return pl.pallas_call(
        keyval_kernel,
        out_shape=[pltpu.HBM(*x) for x in (*kept, ((ROWS, FEAT), BF16), (sent, BF16))],
        in_specs=[VMEM] * 7,
        out_specs=[HBM] * 5,
        scratch_shapes=[
            *[pltpu.VMEM(*x) for x in kept],
            pltpu.VMEM((NEW_PAGES, 2 * PAGE, HD), BF16),
            pltpu.SMEM((24, HD), jnp.int32),
            pltpu.SemaphoreType.DMA((5,)),
            pltpu.SemaphoreType.DMA((NEW_PAGES,)),
        ],
        compiler_params=params(16),
        cost_estimate=cost(0, 1),
        name="project_keyval",
    )(table, block, *sums, weights, cosine, sine)


def dot_nt(a, b):
    return lax.dot_general(a, b, (((1,), (1,)), ((), ())), preferred_element_type=F32)


def attend_kernel(table_ref, pages_ref, *refs):
    sources, wq_ref, out_ref, refs = refs[:7], refs[7], refs[8], refs[9:]
    targets, wq_buf, index_ref, q_buf, keys, values, sems = refs[:7], *refs[7:]
    q_sum, x, inv_norm, cosine, sine, own_keys, own_values = targets
    indices = pltpu.make_async_copy(table_ref, index_ref, sems.at[8])
    indices.start()
    copies = [pltpu.make_async_copy(a, b, sems.at[i]) for i, (a, b) in enumerate(zip(sources, targets))]
    rows = pl.ds(pl.multiple_of(block_index(FAR, True) * FEAT, FEAT), FEAT)
    copies.insert(0, pltpu.make_async_copy(wq_ref.at[rows, :], wq_buf, sems.at[7]))
    for copy in copies:
        copy.start()
    row = lax.broadcasted_iota(jnp.int32, (2 * PAGE, 2 * PAGE), 0)
    column = lax.broadcasted_iota(jnp.int32, (2 * PAGE, 2 * PAGE), 1)
    wanted = jnp.where(row < PAGE, 2 * row, 2 * (row - PAGE) + 1)
    picker = (column == wanted).astype(BF16)
    values[:, HD:] = jnp.ones((PAGES * PAGE, HD), BF16)
    indices.wait()
    for page in range(PAGES):
        both = jnp.dot(picker, pages_ref[index_ref[TAKE, page]], preferred_element_type=F32)
        rows = slice(page * PAGE, (page + 1) * PAGE)
        keys[rows, :] = both[:PAGE].astype(BF16)
        values[rows, :HD] = both[PAGE:].astype(BF16)
    for copy in copies:
        copy.wait()
    for r in range(0, ROWS, TILE):
        rows = slice(r, r + TILE)
        total = q_sum[rows, :] + jnp.dot(x[rows, :], wq_buf[...], preferred_element_type=F32)
        for head in range(HEADS):
            part = total[:, head * HD : (head + 1) * HD] * inv_norm[rows, :]
            q_buf[head, rows, :] = turn(part, cosine[rows, :], sine[rows, :]).astype(BF16)
    block = 256
    allowed = lax.broadcasted_iota(jnp.int32, (block, block), 0) >= lax.broadcasted_iota(
        jnp.int32, (block, block), 1
    )
    for head in range(HEADS):
        lanes = slice(head * HD, (head + 1) * HD)
        for b in range(ROWS // block):
            rows = slice(b * block, (b + 1) * block)
            queries = q_buf[head, rows, :]
            own = dot_nt(queries, own_keys[: (b + 1) * block, :])
            diagonal = jnp.where(allowed, own[:, b * block :], -1e30)
            parts = [(diagonal, own_values[rows, :])]
            if b:
                parts.append((own[:, : b * block], own_values[: b * block, :]))
            parts.append((dot_nt(queries, keys[...]), values[...]))
            tops = [jnp.max(scores, axis=1, keepdims=True) for scores, _ in parts]
            top = functools.reduce(jnp.maximum, tops)
            both = jnp.zeros((block, 2 * HD), F32)
            for scores, held in parts:
                weights = jnp.exp2((scores - top) * SCALE).astype(BF16)
                both += jnp.dot(weights, held, preferred_element_type=F32)
            out_ref[rows, lanes] = (both[:, :HD] / both[:, HD:]).astype(BF16)


def attend(table, pages, sources, w_query):
    return pl.pallas_call(
        attend_kernel,
        out_shape=shape((ROWS, QW), BF16),
        in_specs=[VMEM] * 2 + [HBM] * (len(sources) + 1),
        out_specs=VMEM,
        scratch_shapes=[
            *[pltpu.VMEM(x.shape, x.dtype) for x in sources],
            pltpu.VMEM((FEAT, QW), BF16),
            pltpu.SMEM((24, HD), jnp.int32),
            pltpu.VMEM((HEADS, ROWS, HD), BF16),
            pltpu.VMEM((PAGES * PAGE, HD), BF16),
            pltpu.VMEM((PAGES * PAGE, 2 * HD), BF16),
            pltpu.SemaphoreType.DMA((9,)),
        ],
        compiler_params=params(40),
        cost_estimate=cost(2 * ROWS * 4 * 2560 * 512, 8 * MIB),
        name="attend",
    )(table, pages, *[hbm(x) for x in (*sources, w_query)])


def place_kernel(table_ref, received_ref, out_ref, buffer, index_ref, index_sem, sems):
    indices = pltpu.make_async_copy(table_ref, index_ref, index_sem)
    indices.start()
    indices.wait()
    group = 4
    copies = []
    for i in range(SLOTS):
        source = index_ref[PLACE, i]
        page = received_ref[jnp.maximum(source - 1, 0)]
        buffer[i] = jnp.where(source > 0, page, jnp.zeros_like(page))
        if i % group == group - 1:
            slots = pl.ds(i + 1 - group, group)
            copy = pltpu.make_async_copy(
                buffer.at[slots], out_ref.at[slots], sems.at[i // group]
            )
            copy.start()
            copies.append(copy)
    for copy in copies:
        copy.wait()


def place_pages(table, received):
    return pl.pallas_call(
        place_kernel,
        out_shape=pltpu.HBM((SLOTS, 2 * PAGE, HD), BF16),
        in_specs=[VMEM, VMEM],
        out_specs=HBM,
        scratch_shapes=[
            pltpu.VMEM((SLOTS, 2 * PAGE, HD), BF16),
            pltpu.SMEM((24, HD), jnp.int32),
            pltpu.SemaphoreType.DMA,
            pltpu.SemaphoreType.DMA((SLOTS // 4,)),
        ],
        compiler_params=params(8),
        cost_estimate=cost(0, 2 * MIB),
        name="place_pages",
    )(table, received)


def shift(values, steps):
    pairs = [(i, ((i // 2 + steps[i % 2]) % 4) * 2 + i % 2) for i in range(8)]
    return lax.ppermute(values, "tp", pairs)


def swap(values):
    return lax.ppermute(values, "tp", [(i, i ^ 1) for i in range(8)])


def rope_tables(row_count, offset):
    half_dim = HD // 2
    frequency = 500000.0 ** (-(jnp.arange(half_dim, dtype=F32) * (2.0 / HD)))
    place = (offset + jnp.arange(row_count, dtype=jnp.int32)).astype(F32)
    angles = place[:, None] * frequency[None, :]
    cosine, sine = jnp.cos(angles), jnp.sin(angles)
    return jnp.concatenate([cosine, cosine], 1), jnp.concatenate([-sine, sine], 1)


def exchange(values):
    return lax.all_to_all(values, "pool", split_axis=0, concat_axis=0, tiled=True)


def body(hidden, w_query, w_keyval, store, page_owner, page_slot, new_owner):
    near = shift(hidden, (1, -1))
    table, packed, again = prelude(
        page_owner, page_slot, new_owner, store.reshape(64, 2 * PAGE, HD), hidden
    )
    pages = exchange(packed)
    back = shift(again, (-1, 1))
    tables = rope_tables(ROWS, PAGES * PAGE)
    weights = (w_query, w_keyval)
    blocks = ((OWN, True), (OWN, False))
    sums = project(blocks, [swap(hidden)], [hidden], *weights, tokens=tables)
    (near,) = after((sums[2],), near)
    far = shift(near, (1, -1))
    blocks = ((NEAR, False), (BACK, False))
    sums = project(blocks, [near, back], [], *weights, sums, flops=HIDES)
    blocks, ahead = ((NEAR, True), (BACK, True)), ((FAR, False), (FAR, True))
    held = [swap(near), swap(back)]
    *sums, last_q, last_kv = project(blocks, held, [], *weights, sums, ahead)
    (far,) = after((sums[2],), far)
    other = swap(far)
    sums = project_far(far, (last_q, last_kv), sums)
    own_keys, own_values, inv_norm, other, send = project_keyval(
        table, other, sums[1:], last_kv, *tables
    )
    received = exchange(send)
    sources = (sums[0], other, inv_norm, *tables, own_keys, own_values)
    attended = attend(table, pages, sources, w_query)
    placed = place_pages(table, received)
    return attended, placed.reshape(SLOTS, 1, PAGE, 2, HD)


def solution(mesh):
    in_specs = (
        P("pool", "tp"),
        P(None, "tp"),
        P(None, "tp"),
        P("pool", "tp", None, None, None),
        P(),
        P(),
        P(),
    )
    out_specs = (P("pool", "tp"), P("pool", "tp", None, None, None))
    return jax.shard_map(body, mesh=mesh, in_specs=in_specs, out_specs=out_specs, check_vma=False)
```

```python
import functools
import math

import jax
import jax.numpy as jnp
from jax import lax
from jax.experimental import pallas as pl
from jax.experimental.pallas import tpu as pltpu
from jax.sharding import PartitionSpec as P

D = 8192
HD = 128
PAGE = 64
CAP = 4
PUSH_CAP = 2
HEADS = 4
FEAT = 1024
QW = 512
KVW = 256
POOL = 16
PAGES = 32
NEW_PAGES = 8
SLOTS = 32
ROWS = 512
PUSH, TAKE, PLACE = 4, 16, 17
MIB = 1024 * 1024
SCALE = math.log2(math.e) / math.sqrt(HD)
HIDES = 20_000_000_000
F32 = jnp.float32
BF16 = jnp.bfloat16
ANY = pl.BlockSpec(memory_space=pl.ANY)
HBM = pl.BlockSpec(memory_space=pltpu.HBM)
VMEM = pl.BlockSpec(memory_space=pltpu.VMEM)
SMEM = pl.BlockSpec(memory_space=pltpu.SMEM)


def params(mib):
    return pltpu.CompilerParams(vmem_limit_bytes=mib * MIB)


def cost(flops, nbytes):
    return pl.CostEstimate(flops=flops, bytes_accessed=nbytes, transcendentals=0)


def hbm(array):
    return pltpu.with_memory_space_constraint(array, pltpu.HBM)


def shape(dims, dtype):
    return jax.ShapeDtypeStruct(dims, dtype)


def fill_table(owners, slots, targets, out_ref):
    me = lax.axis_index("pool")
    out_ref[...] = jnp.zeros_like(out_ref)
    lanes = lax.broadcasted_iota(jnp.int32, owners.shape, 1)
    rows = lax.broadcasted_iota(jnp.int32, owners.shape, 0)
    ranks = jnp.zeros_like(owners)
    for j in range(PAGES):
        ranks += ((owners == owners[:, j : j + 1]) & (lanes > j)).astype(jnp.int32)
    for k in range(CAP):
        chosen = jnp.where((owners == me) & (ranks == k), slots, 0)
        out_ref[:POOL, k : k + 1] = jnp.sum(chosen, axis=1, keepdims=True)
    mine = jnp.where(rows == me, owners * CAP + ranks, 0)
    out_ref[TAKE : TAKE + 1, :PAGES] = jnp.sum(mine, axis=0, keepdims=True)
    lanes = lax.broadcasted_iota(jnp.int32, targets.shape, 1)
    rows = lax.broadcasted_iota(jnp.int32, targets.shape, 0)
    kept = (targets == me).astype(jnp.int32)
    ranks = jnp.zeros_like(targets)
    slot = jnp.zeros_like(targets)
    for j in range(NEW_PAGES):
        later = rows > j
        ranks += ((targets == targets[j : j + 1, :]) & later).astype(jnp.int32)
        slot += jnp.where(later, kept[j : j + 1, :], 0)
    mine = jnp.where(lanes == me, targets * PUSH_CAP + ranks, 0)
    out_ref[:NEW_PAGES, PUSH : PUSH + 1] = jnp.sum(mine, axis=1, keepdims=True)
    of_request = jnp.sum(kept, axis=0, keepdims=True)
    for r in range(POOL):
        slot += jnp.where(lanes > r, of_request[:, r : r + 1], 0)
    source = jnp.zeros((NEW_PAGES, SLOTS), jnp.int32)
    slot_lanes = lax.broadcasted_iota(jnp.int32, source.shape, 1)
    for r in range(POOL):
        hit = (kept[:, r : r + 1] > 0) & (slot[:, r : r + 1] == slot_lanes)
        source += jnp.where(hit, r * PUSH_CAP + ranks[:, r : r + 1] + 1, 0)
    out_ref[PLACE : PLACE + 1, :SLOTS] = jnp.sum(source, axis=0, keepdims=True)


def prelude_kernel(*refs):
    owner_in, slot_in, target_in, store_in, table_ref, out_ref = refs[:6]
    owner_ref, slot_ref, target_ref, store_ref, index_ref, sems, page_sems = refs[6:]
    pairs = (
        (owner_in, owner_ref),
        (slot_in, slot_ref),
        (target_in, target_ref),
        (store_in, store_ref),
    )
    copies = [pltpu.make_async_copy(x, y, sems.at[i]) for i, (x, y) in enumerate(pairs)]
    for copy in copies:
        copy.start()
    for copy in copies[:3]:
        copy.wait()
    fill_table(owner_ref[...], slot_ref[...], target_ref[...], table_ref)
    indices = pltpu.make_async_copy(table_ref, index_ref, sems.at[4])
    indices.start()
    indices.wait()
    copies[3].wait()
    pages = [
        pltpu.make_async_copy(
            store_ref.at[index_ref[i // CAP, i % CAP]], out_ref.at[i], page_sems.at[i]
        )
        for i in range(POOL * CAP)
    ]
    for page in pages:
        page.start()
    for page in pages:
        page.wait()


def prelude(page_owner, page_slot, new_owner, store):
    return pl.pallas_call(
        prelude_kernel,
        out_shape=[
            shape((24, HD), jnp.int32),
            pltpu.HBM((POOL * CAP, 2 * PAGE, HD), BF16),
        ],
        in_specs=[HBM] * 4,
        out_specs=[VMEM, HBM],
        scratch_shapes=[
            pltpu.VMEM((POOL, PAGES), jnp.int32),
            pltpu.VMEM((POOL, PAGES), jnp.int32),
            pltpu.VMEM((NEW_PAGES, POOL), jnp.int32),
            pltpu.VMEM(store.shape, BF16),
            pltpu.SMEM((24, HD), jnp.int32),
            pltpu.SemaphoreType.DMA((5,)),
            pltpu.SemaphoreType.DMA((POOL * CAP,)),
        ],
        compiler_params=params(8),
        cost_estimate=cost(0, 1),
        name="prelude",
    )(*[hbm(x) for x in (page_owner, page_slot, new_owner.T, store)])


def block_index(steps, other_core):
    index = lax.axis_index("tp")
    core = lax.rem(index, 2)
    if other_core:
        core = 1 - core
    z = lax.rem(index // 2 + jnp.where(core == 0, steps[0], steps[1]), 4)
    return 2 * z + core


def squares_of(rows):
    wide = rows.astype(F32)
    total = None
    for lane in range(0, FEAT, HD):
        part = wide[:, lane : lane + HD]
        total = part * part if total is None else total + part * part
    return total


def weight_copies(refs, buffers, sems, blocks):
    copies = []
    for i, (steps, other) in enumerate(blocks):
        rows = pl.ds(pl.multiple_of(block_index(steps, other) * FEAT, FEAT), FEAT)
        copies.append(
            [
                pltpu.make_async_copy(ref.at[rows, :], buffer.at[i], sems.at[len(refs) * i + j])
                for j, (ref, buffer) in enumerate(zip(refs, buffers))
            ]
        )
    for group in copies:
        for copy in group:
            copy.start()
    return copies


OWN, NEAR, BACK, FAR = (0, 0), (3, 1), (1, 3), (2, 2)
TILE = 128


def project_kernel(blocks, held, has_sums, tokens, ahead, *refs):
    count = len(blocks)
    x_refs, refs = refs[:count], refs[count:]
    wq_ref, wkv_ref, refs = refs[0], refs[1], refs[2:]
    before, refs = (refs[:3], refs[3:]) if has_sums else (None, refs)
    refs = refs[tokens:]
    sums, refs = refs[:3], refs[3:]
    fetched, refs = (refs[:2], refs[2:]) if ahead else (None, refs)
    x_buf, wq_buf, wkv_buf, sems, x_sems, ahead_sems = refs
    copies = weight_copies((wq_ref, wkv_ref), (wq_buf, wkv_buf), sems, blocks)
    x_copies = {}
    for i in range(held, count):
        x_copies[i] = pltpu.make_async_copy(x_refs[i], x_buf.at[i - held], x_sems.at[i - held])
        x_copies[i].start()
    later = weight_copies((wq_ref, wkv_ref), fetched, ahead_sems, ahead) if ahead else []
    for i in range(count):
        copies[i][0].wait()
        copies[i][1].wait()
        if i in x_copies:
            x_copies[i].wait()
        for r in range(0, ROWS, TILE):
            rows = slice(r, r + TILE)
            x = x_refs[i][rows, :] if i < held else x_buf[i - held, rows, :]
            parts = (
                jnp.dot(x, wq_buf[i], preferred_element_type=F32),
                jnp.dot(x, wkv_buf[i], preferred_element_type=F32),
                squares_of(x),
            )
            for j, part in enumerate(parts):
                if i > 0:
                    sums[j][rows, :] += part
                elif has_sums:
                    sums[j][rows, :] = before[j][rows, :] + part
                else:
                    sums[j][rows, :] = part
    for group in later:
        for copy in group:
            copy.wait()


def project(blocks, held, direct, w_query, w_keyval, sums=(), ahead=(), tokens=(), flops=0):
    count = len(blocks)
    shapes = [shape((ROWS, w), F32) for w in (QW, KVW, HD)]
    if ahead:
        shapes += [shape((len(ahead), FEAT, w), BF16) for w in (QW, KVW)]
    return pl.pallas_call(
        functools.partial(project_kernel, blocks, len(held), bool(sums), len(tokens), ahead),
        out_shape=shapes,
        in_specs=[VMEM] * len(held)
        + [HBM] * (len(direct) + 2)
        + [VMEM] * len(sums)
        + [ANY] * len(tokens),
        out_specs=[VMEM] * len(shapes),
        scratch_shapes=[
            pltpu.VMEM((max(len(direct), 1), ROWS, FEAT), BF16),
            pltpu.VMEM((count, FEAT, QW), BF16),
            pltpu.VMEM((count, FEAT, KVW), BF16),
            pltpu.SemaphoreType.DMA((2 * count,)),
            pltpu.SemaphoreType.DMA((max(len(direct), 1),)),
            pltpu.SemaphoreType.DMA((max(2 * len(ahead), 1),)),
        ],
        compiler_params=params(24),
        cost_estimate=cost(flops, 1),
        name="project",
    )(*held, *[hbm(x) for x in (*direct, w_query, w_keyval)], *sums, *tokens)


def far_kernel(x_ref, wq_ref, wkv_ref, *refs):
    before, sums = refs[:3], refs[3:]
    for r in range(0, ROWS, TILE):
        rows = slice(r, r + TILE)
        x = x_ref[rows, :]
        sums[0][rows, :] = before[0][rows, :] + jnp.dot(x, wq_ref[0], preferred_element_type=F32)
        sums[1][rows, :] = before[1][rows, :] + jnp.dot(x, wkv_ref[0], preferred_element_type=F32)
        sums[2][rows, :] = before[2][rows, :] + squares_of(x)


def project_far(block, weights, sums):
    return pl.pallas_call(
        far_kernel,
        out_shape=[pltpu.HBM((ROWS, QW), F32)] + [shape((ROWS, w), F32) for w in (KVW, HD)],
        in_specs=[VMEM] * 6,
        out_specs=[VMEM] * 3,
        compiler_params=params(16),
        cost_estimate=cost(0, 1),
        name="project_far",
    )(block, *weights, *sums)


def after_kernel(*refs):
    pass


def after(tokens, *arrays, flops=0):
    count, skip = len(arrays), len(tokens)
    return pl.pallas_call(
        after_kernel,
        out_shape=[shape(x.shape, x.dtype) for x in arrays],
        in_specs=[ANY] * (count + skip),
        out_specs=[ANY] * count,
        input_output_aliases={i + skip: i for i in range(count)},
        compiler_params=params(1),
        cost_estimate=cost(flops, 1),
        name="after",
    )(*tokens, *arrays)


def turn(values, cosine, sine):
    return values * cosine + pltpu.roll(values, HD // 2, 1) * sine


def keyval_kernel(table_ref, x_ref, kv_in, sq_in, wkv_ref, cos_ref, sin_ref, *refs):
    keys_out, values_out, inv_out, x_out, send_out = refs[:5]
    keys_buf, values_buf, inv_buf, page_buf, index_ref, sems, page_sems = refs[5:]
    indices = pltpu.make_async_copy(table_ref, index_ref, sems.at[0])
    indices.start()
    copies = [pltpu.make_async_copy(x_ref, x_out, sems.at[1])]
    copies[0].start()
    row = lax.broadcasted_iota(jnp.int32, (2 * PAGE, 2 * PAGE), 0)
    column = lax.broadcasted_iota(jnp.int32, (2 * PAGE, 2 * PAGE), 1)
    picker = (column == (row >> 1) + (row & 1) * PAGE).astype(BF16)
    values_buf[:, HD:] = jnp.ones((ROWS, HD), BF16)
    for r in range(0, ROWS, TILE):
        rows = slice(r, r + TILE)
        x = x_ref[rows, :]
        kv_sum = kv_in[rows, :] + jnp.dot(x, wkv_ref[1], preferred_element_type=F32)
        squares = sq_in[rows, :] + squares_of(x)
        mean = jnp.sum(squares, axis=1, keepdims=True) / D
        inv_norm = jnp.broadcast_to(lax.rsqrt(mean + 1e-05), (TILE, HD))
        inv_buf[rows, :] = inv_norm
        keys = turn(kv_sum[:, :HD] * inv_norm, cos_ref[rows, :], sin_ref[rows, :]).astype(BF16)
        values = (kv_sum[:, HD:] * inv_norm).astype(BF16)
        keys_buf[rows, :] = keys
        values_buf[rows, :HD] = values
        if r == 0:
            indices.wait()
        for p in range(0, TILE, PAGE):
            page = (r + p) // PAGE
            both = jnp.concatenate([keys[p : p + PAGE], values[p : p + PAGE]], axis=0)
            page_buf[page] = jnp.dot(picker, both, preferred_element_type=F32).astype(BF16)
            target = send_out.at[index_ref[page, PUSH]]
            copies.append(pltpu.make_async_copy(page_buf.at[page], target, page_sems.at[page]))
            copies[-1].start()
    results = ((keys_buf, keys_out), (values_buf, values_out), (inv_buf, inv_out))
    for i, (source, target) in enumerate(results):
        copies.append(pltpu.make_async_copy(source, target, sems.at[2 + i]))
        copies[-1].start()
    for copy in copies:
        copy.wait()


def project_keyval(table, block, sums, weights, cosine, sine):
    kept = [((ROWS, HD), BF16), ((ROWS, 2 * HD), BF16), ((ROWS, HD), F32)]
    sent = (POOL * PUSH_CAP, 2 * PAGE, HD)
    return pl.pallas_call(
        keyval_kernel,
        out_shape=[pltpu.HBM(*x) for x in (*kept, ((ROWS, FEAT), BF16), (sent, BF16))],
        in_specs=[VMEM] * 7,
        out_specs=[HBM] * 5,
        scratch_shapes=[
            *[pltpu.VMEM(*x) for x in kept],
            pltpu.VMEM((NEW_PAGES, 2 * PAGE, HD), BF16),
            pltpu.SMEM((24, HD), jnp.int32),
            pltpu.SemaphoreType.DMA((5,)),
            pltpu.SemaphoreType.DMA((NEW_PAGES,)),
        ],
        compiler_params=params(16),
        cost_estimate=cost(0, 1),
        name="project_keyval",
    )(table, block, *sums, weights, cosine, sine)


def dot_nt(a, b):
    return lax.dot_general(a, b, (((1,), (1,)), ((), ())), preferred_element_type=F32)


def attend_kernel(table_ref, *refs):
    sources, wq_ref, pages_ref, out_ref, refs = refs[:7], refs[7], refs[8], refs[9], refs[10:]
    targets, wq_buf, index_ref, page_buf, q_buf, keys, values, sems, page_sems = refs[:7], *refs[7:]
    q_sum, x, inv_norm, cosine, sine, own_keys, own_values = targets
    indices = pltpu.make_async_copy(table_ref, index_ref, sems.at[8])
    indices.start()
    copies = [pltpu.make_async_copy(a, b, sems.at[i]) for i, (a, b) in enumerate(zip(sources, targets))]
    rows = pl.ds(pl.multiple_of(block_index(FAR, True) * FEAT, FEAT), FEAT)
    copies.insert(0, pltpu.make_async_copy(wq_ref.at[rows, :], wq_buf, sems.at[7]))
    for copy in copies:
        copy.start()
    row = lax.broadcasted_iota(jnp.int32, (2 * PAGE, 2 * PAGE), 0)
    column = lax.broadcasted_iota(jnp.int32, (2 * PAGE, 2 * PAGE), 1)
    wanted = jnp.where(row < PAGE, 2 * row, 2 * (row - PAGE) + 1)
    picker = (column == wanted).astype(BF16)
    values[:, HD:] = jnp.ones((PAGES * PAGE, HD), BF16)
    indices.wait()
    fetches = [
        pltpu.make_async_copy(
            pages_ref.at[index_ref[TAKE, page]], page_buf.at[page], page_sems.at[page]
        )
        for page in range(PAGES)
    ]
    for fetch in fetches:
        fetch.start()
    for page in range(PAGES):
        fetches[page].wait()
        both = jnp.dot(picker, page_buf[page], preferred_element_type=F32)
        rows = slice(page * PAGE, (page + 1) * PAGE)
        keys[rows, :] = both[:PAGE].astype(BF16)
        values[rows, :HD] = both[PAGE:].astype(BF16)
    for copy in copies:
        copy.wait()
    for r in range(0, ROWS, TILE):
        rows = slice(r, r + TILE)
        total = q_sum[rows, :] + jnp.dot(x[rows, :], wq_buf[...], preferred_element_type=F32)
        for head in range(HEADS):
            part = total[:, head * HD : (head + 1) * HD] * inv_norm[rows, :]
            q_buf[head, rows, :] = turn(part, cosine[rows, :], sine[rows, :]).astype(BF16)
    block = 256
    allowed = lax.broadcasted_iota(jnp.int32, (block, block), 0) >= lax.broadcasted_iota(
        jnp.int32, (block, block), 1
    )
    for head in range(HEADS):
        lanes = slice(head * HD, (head + 1) * HD)
        for b in range(ROWS // block):
            rows = slice(b * block, (b + 1) * block)
            queries = q_buf[head, rows, :]
            own = dot_nt(queries, own_keys[: (b + 1) * block, :])
            diagonal = jnp.where(allowed, own[:, b * block :], -1e30)
            parts = [(diagonal, own_values[rows, :])]
            if b:
                parts.append((own[:, : b * block], own_values[: b * block, :]))
            parts.append((dot_nt(queries, keys[...]), values[...]))
            tops = [jnp.max(scores, axis=1, keepdims=True) for scores, _ in parts]
            top = functools.reduce(jnp.maximum, tops)
            both = jnp.zeros((block, 2 * HD), F32)
            for scores, held in parts:
                weights = jnp.exp2((scores - top) * SCALE).astype(BF16)
                both += jnp.dot(weights, held, preferred_element_type=F32)
            out_ref[rows, lanes] = (both[:, :HD] / both[:, HD:]).astype(BF16)


def attend(table, pages, sources, w_query):
    return pl.pallas_call(
        attend_kernel,
        out_shape=shape((ROWS, QW), BF16),
        in_specs=[VMEM] + [HBM] * (len(sources) + 2),
        out_specs=VMEM,
        scratch_shapes=[
            *[pltpu.VMEM(x.shape, x.dtype) for x in sources],
            pltpu.VMEM((FEAT, QW), BF16),
            pltpu.SMEM((24, HD), jnp.int32),
            pltpu.VMEM((PAGES, 2 * PAGE, HD), BF16),
            pltpu.VMEM((HEADS, ROWS, HD), BF16),
            pltpu.VMEM((PAGES * PAGE, HD), BF16),
            pltpu.VMEM((PAGES * PAGE, 2 * HD), BF16),
            pltpu.SemaphoreType.DMA((9,)),
            pltpu.SemaphoreType.DMA((PAGES,)),
        ],
        compiler_params=params(40),
        cost_estimate=cost(2 * ROWS * 4 * 2560 * 512, 8 * MIB),
        name="attend",
    )(table, *[hbm(x) for x in (*sources, w_query, pages)])


def place_kernel(table_ref, received_ref, out_ref, buffer, index_ref, index_sem, sems):
    indices = pltpu.make_async_copy(table_ref, index_ref, index_sem)
    indices.start()
    indices.wait()
    group = 4
    copies = []
    for i in range(SLOTS):
        source = index_ref[PLACE, i]
        page = received_ref[jnp.maximum(source - 1, 0)]
        buffer[i] = jnp.where(source > 0, page, jnp.zeros_like(page))
        if i % group == group - 1:
            slots = pl.ds(i + 1 - group, group)
            copy = pltpu.make_async_copy(
                buffer.at[slots], out_ref.at[slots], sems.at[i // group]
            )
            copy.start()
            copies.append(copy)
    for copy in copies:
        copy.wait()


def place_pages(table, received):
    return pl.pallas_call(
        place_kernel,
        out_shape=pltpu.HBM((SLOTS, 2 * PAGE, HD), BF16),
        in_specs=[VMEM, VMEM],
        out_specs=HBM,
        scratch_shapes=[
            pltpu.VMEM((SLOTS, 2 * PAGE, HD), BF16),
            pltpu.SMEM((24, HD), jnp.int32),
            pltpu.SemaphoreType.DMA,
            pltpu.SemaphoreType.DMA((SLOTS // 4,)),
        ],
        compiler_params=params(8),
        cost_estimate=cost(0, 2 * MIB),
        name="place_pages",
    )(table, received)


def shift(values, steps):
    pairs = [(i, ((i // 2 + steps[i % 2]) % 4) * 2 + i % 2) for i in range(8)]
    return lax.ppermute(values, "tp", pairs)


def swap(values):
    return lax.ppermute(values, "tp", [(i, i ^ 1) for i in range(8)])


def rope_tables(row_count, offset):
    half_dim = HD // 2
    frequency = 500000.0 ** (-(jnp.arange(half_dim, dtype=F32) * (2.0 / HD)))
    place = (offset + jnp.arange(row_count, dtype=jnp.int32)).astype(F32)
    angles = place[:, None] * frequency[None, :]
    cosine, sine = jnp.cos(angles), jnp.sin(angles)
    return jnp.concatenate([cosine, cosine], 1), jnp.concatenate([-sine, sine], 1)


def exchange(values):
    return lax.all_to_all(values, "pool", split_axis=0, concat_axis=0, tiled=True)


def body(hidden, w_query, w_keyval, store, page_owner, page_slot, new_owner):
    near = shift(hidden, (1, -1))
    table, packed = prelude(page_owner, page_slot, new_owner, store.reshape(64, 2 * PAGE, HD))
    pages = exchange(packed)
    sibling = swap(hidden)
    (sibling,) = after((table,), sibling)
    back = shift(sibling, (1, -1))
    tables = rope_tables(ROWS, PAGES * PAGE)
    weights = (w_query, w_keyval)
    blocks = ((OWN, True), (OWN, False))
    sums = project(blocks, [sibling], [hidden], *weights, tokens=tables)
    (near,) = after((sums[2],), near)
    far = shift(near, (1, -1))
    blocks = ((NEAR, False), (BACK, True))
    sums = project(blocks, [near, back], [], *weights, sums, flops=HIDES)
    blocks, ahead = ((NEAR, True), (BACK, False)), ((FAR, False), (FAR, True))
    held = [swap(near), swap(back)]
    *sums, last_q, last_kv = project(blocks, held, [], *weights, sums, ahead)
    (far,) = after((sums[2],), far)
    other = swap(far)
    sums = project_far(far, (last_q, last_kv), sums)
    own_keys, own_values, inv_norm, other, send = project_keyval(
        table, other, sums[1:], last_kv, *tables
    )
    received = exchange(send)
    sources = (sums[0], other, inv_norm, *tables, own_keys, own_values)
    attended = attend(table, pages, sources, w_query)
    placed = place_pages(table, received)
    return attended, placed.reshape(SLOTS, 1, PAGE, 2, HD)


def solution(mesh):
    in_specs = (
        P("pool", "tp"),
        P(None, "tp"),
        P(None, "tp"),
        P("pool", "tp", None, None, None),
        P(),
        P(),
        P(),
    )
    out_specs = (P("pool", "tp"), P("pool", "tp", None, None, None))
    return jax.shard_map(body, mesh=mesh, in_specs=in_specs, out_specs=out_specs, check_vma=False)
```

```python
import functools
import math

import jax
import jax.numpy as jnp
from jax import lax
from jax.experimental import pallas as pl
from jax.experimental.pallas import tpu as pltpu
from jax.sharding import PartitionSpec as P

D = 8192
HD = 128
PAGE = 64
CAP = 4
PUSH_CAP = 2
HEADS = 4
FEAT = 1024
QW = 512
KVW = 256
POOL = 16
PAGES = 32
NEW_PAGES = 8
SLOTS = 32
ROWS = 512
PUSH, TAKE, PLACE = 4, 16, 17
MIB = 1024 * 1024
SCALE = math.log2(math.e) / math.sqrt(HD)
HIDES = 20_000_000_000
F32 = jnp.float32
BF16 = jnp.bfloat16
ANY = pl.BlockSpec(memory_space=pl.ANY)
HBM = pl.BlockSpec(memory_space=pltpu.HBM)
VMEM = pl.BlockSpec(memory_space=pltpu.VMEM)
SMEM = pl.BlockSpec(memory_space=pltpu.SMEM)


def params(mib):
    return pltpu.CompilerParams(vmem_limit_bytes=mib * MIB)


def cost(flops, nbytes):
    return pl.CostEstimate(flops=flops, bytes_accessed=nbytes, transcendentals=0)


def hbm(array):
    return pltpu.with_memory_space_constraint(array, pltpu.HBM)


def shape(dims, dtype):
    return jax.ShapeDtypeStruct(dims, dtype)


def fill_table(owners, slots, targets, out_ref):
    me = lax.axis_index("pool")
    out_ref[...] = jnp.zeros_like(out_ref)
    lanes = lax.broadcasted_iota(jnp.int32, owners.shape, 1)
    rows = lax.broadcasted_iota(jnp.int32, owners.shape, 0)
    ranks = jnp.zeros_like(owners)
    for j in range(PAGES):
        ranks += ((owners == owners[:, j : j + 1]) & (lanes > j)).astype(jnp.int32)
    for k in range(CAP):
        chosen = jnp.where((owners == me) & (ranks == k), slots, 0)
        out_ref[:POOL, k : k + 1] = jnp.sum(chosen, axis=1, keepdims=True)
    mine = jnp.where(rows == me, owners * CAP + ranks, 0)
    out_ref[TAKE : TAKE + 1, :PAGES] = jnp.sum(mine, axis=0, keepdims=True)
    lanes = lax.broadcasted_iota(jnp.int32, targets.shape, 1)
    rows = lax.broadcasted_iota(jnp.int32, targets.shape, 0)
    kept = (targets == me).astype(jnp.int32)
    ranks = jnp.zeros_like(targets)
    slot = jnp.zeros_like(targets)
    for j in range(NEW_PAGES):
        later = rows > j
        ranks += ((targets == targets[j : j + 1, :]) & later).astype(jnp.int32)
        slot += jnp.where(later, kept[j : j + 1, :], 0)
    mine = jnp.where(lanes == me, targets * PUSH_CAP + ranks, 0)
    out_ref[:NEW_PAGES, PUSH : PUSH + 1] = jnp.sum(mine, axis=1, keepdims=True)
    of_request = jnp.sum(kept, axis=0, keepdims=True)
    for r in range(POOL):
        slot += jnp.where(lanes > r, of_request[:, r : r + 1], 0)
    source = jnp.zeros((NEW_PAGES, SLOTS), jnp.int32)
    slot_lanes = lax.broadcasted_iota(jnp.int32, source.shape, 1)
    for r in range(POOL):
        hit = (kept[:, r : r + 1] > 0) & (slot[:, r : r + 1] == slot_lanes)
        source += jnp.where(hit, r * PUSH_CAP + ranks[:, r : r + 1] + 1, 0)
    out_ref[PLACE : PLACE + 1, :SLOTS] = jnp.sum(source, axis=0, keepdims=True)


def prelude_kernel(*refs):
    owner_in, slot_in, target_in, store_in, table_ref, out_ref = refs[:6]
    owner_ref, slot_ref, target_ref, store_ref, index_ref, sems, page_sems = refs[6:]
    pairs = (
        (owner_in, owner_ref),
        (slot_in, slot_ref),
        (target_in, target_ref),
        (store_in, store_ref),
    )
    copies = [pltpu.make_async_copy(x, y, sems.at[i]) for i, (x, y) in enumerate(pairs)]
    for copy in copies:
        copy.start()
    for copy in copies[:3]:
        copy.wait()
    fill_table(owner_ref[...], slot_ref[...], target_ref[...], table_ref)
    indices = pltpu.make_async_copy(table_ref, index_ref, sems.at[4])
    indices.start()
    indices.wait()
    copies[3].wait()
    pages = [
        pltpu.make_async_copy(
            store_ref.at[index_ref[i // CAP, i % CAP]], out_ref.at[i], page_sems.at[i]
        )
        for i in range(POOL * CAP)
    ]
    for page in pages:
        page.start()
    for page in pages:
        page.wait()


def prelude(page_owner, page_slot, new_owner, store):
    return pl.pallas_call(
        prelude_kernel,
        out_shape=[
            shape((24, HD), jnp.int32),
            pltpu.HBM((POOL * CAP, 2 * PAGE, HD), BF16),
        ],
        in_specs=[HBM] * 4,
        out_specs=[VMEM, HBM],
        scratch_shapes=[
            pltpu.VMEM((POOL, PAGES), jnp.int32),
            pltpu.VMEM((POOL, PAGES), jnp.int32),
            pltpu.VMEM((NEW_PAGES, POOL), jnp.int32),
            pltpu.VMEM(store.shape, BF16),
            pltpu.SMEM((24, HD), jnp.int32),
            pltpu.SemaphoreType.DMA((5,)),
            pltpu.SemaphoreType.DMA((POOL * CAP,)),
        ],
        compiler_params=params(8),
        cost_estimate=cost(0, 1),
        name="prelude",
    )(*[hbm(x) for x in (page_owner, page_slot, new_owner.T, store)])


def block_index(steps, other_core):
    index = lax.axis_index("tp")
    core = lax.rem(index, 2)
    if other_core:
        core = 1 - core
    z = lax.rem(index // 2 + jnp.where(core == 0, steps[0], steps[1]), 4)
    return 2 * z + core


def squares_of(rows):
    wide = rows.astype(F32)
    total = None
    for lane in range(0, FEAT, HD):
        part = wide[:, lane : lane + HD]
        total = part * part if total is None else total + part * part
    return total


def weight_copies(refs, buffers, sems, blocks):
    copies = []
    for i, (steps, other) in enumerate(blocks):
        rows = pl.ds(pl.multiple_of(block_index(steps, other) * FEAT, FEAT), FEAT)
        copies.append(
            [
                pltpu.make_async_copy(ref.at[rows, :], buffer.at[i], sems.at[len(refs) * i + j])
                for j, (ref, buffer) in enumerate(zip(refs, buffers))
            ]
        )
    for group in copies:
        for copy in group:
            copy.start()
    return copies


OWN, NEAR, BACK, FAR = (0, 0), (3, 1), (1, 3), (2, 2)
TILE = 128


def project_kernel(blocks, held, has_sums, tokens, ahead, *refs):
    count = len(blocks)
    x_refs, refs = refs[:count], refs[count:]
    wq_ref, wkv_ref, refs = refs[0], refs[1], refs[2:]
    before, refs = (refs[:3], refs[3:]) if has_sums else (None, refs)
    refs = refs[tokens:]
    sums, refs = refs[:3], refs[3:]
    fetched, refs = (refs[:2], refs[2:]) if ahead else (None, refs)
    x_buf, wq_buf, wkv_buf, sems, x_sems, ahead_sems = refs
    copies = weight_copies((wq_ref, wkv_ref), (wq_buf, wkv_buf), sems, blocks)
    x_copies = {}
    for i in range(held, count):
        x_copies[i] = pltpu.make_async_copy(x_refs[i], x_buf.at[i - held], x_sems.at[i - held])
        x_copies[i].start()
    later = weight_copies((wq_ref, wkv_ref), fetched, ahead_sems, ahead) if ahead else []
    for i in range(count):
        copies[i][0].wait()
        copies[i][1].wait()
        if i in x_copies:
            x_copies[i].wait()
        for r in range(0, ROWS, TILE):
            rows = slice(r, r + TILE)
            x = x_refs[i][rows, :] if i < held else x_buf[i - held, rows, :]
            parts = (
                jnp.dot(x, wq_buf[i], preferred_element_type=F32),
                jnp.dot(x, wkv_buf[i], preferred_element_type=F32),
                squares_of(x),
            )
            for j, part in enumerate(parts):
                if i > 0:
                    sums[j][rows, :] += part
                elif has_sums:
                    sums[j][rows, :] = before[j][rows, :] + part
                else:
                    sums[j][rows, :] = part
    for group in later:
        for copy in group:
            copy.wait()


def project(blocks, held, direct, w_query, w_keyval, sums=(), ahead=(), tokens=(), flops=0):
    count = len(blocks)
    shapes = [shape((ROWS, w), F32) for w in (QW, KVW, HD)]
    if ahead:
        shapes += [shape((len(ahead), FEAT, w), BF16) for w in (QW, KVW)]
    return pl.pallas_call(
        functools.partial(project_kernel, blocks, len(held), bool(sums), len(tokens), ahead),
        out_shape=shapes,
        in_specs=[VMEM] * len(held)
        + [HBM] * (len(direct) + 2)
        + [VMEM] * len(sums)
        + [ANY] * len(tokens),
        out_specs=[VMEM] * len(shapes),
        scratch_shapes=[
            pltpu.VMEM((max(len(direct), 1), ROWS, FEAT), BF16),
            pltpu.VMEM((count, FEAT, QW), BF16),
            pltpu.VMEM((count, FEAT, KVW), BF16),
            pltpu.SemaphoreType.DMA((2 * count,)),
            pltpu.SemaphoreType.DMA((max(len(direct), 1),)),
            pltpu.SemaphoreType.DMA((max(2 * len(ahead), 1),)),
        ],
        compiler_params=params(24),
        cost_estimate=cost(flops, 1),
        name="project",
    )(*held, *[hbm(x) for x in (*direct, w_query, w_keyval)], *sums, *tokens)


def far_kernel(x_ref, wq_ref, wkv_ref, *refs):
    before, sums = refs[:3], refs[3:]
    for r in range(0, ROWS, TILE):
        rows = slice(r, r + TILE)
        x = x_ref[rows, :]
        sums[0][rows, :] = before[0][rows, :] + jnp.dot(x, wq_ref[0], preferred_element_type=F32)
        sums[1][rows, :] = before[1][rows, :] + jnp.dot(x, wkv_ref[0], preferred_element_type=F32)
        sums[2][rows, :] = before[2][rows, :] + squares_of(x)


def project_far(block, weights, sums):
    return pl.pallas_call(
        far_kernel,
        out_shape=[shape((ROWS, w), F32) for w in (QW, KVW, HD)],
        in_specs=[VMEM] * 6,
        out_specs=[VMEM] * 3,
        compiler_params=params(16),
        cost_estimate=cost(0, 1),
        name="project_far",
    )(block, *weights, *sums)


def after_kernel(*refs):
    pass


def after(tokens, *arrays, flops=0):
    count, skip = len(arrays), len(tokens)
    return pl.pallas_call(
        after_kernel,
        out_shape=[shape(x.shape, x.dtype) for x in arrays],
        in_specs=[ANY] * (count + skip),
        out_specs=[ANY] * count,
        input_output_aliases={i + skip: i for i in range(count)},
        compiler_params=params(1),
        cost_estimate=cost(flops, 1),
        name="after",
    )(*tokens, *arrays)


def turn(values, cosine, sine):
    return values * cosine + pltpu.roll(values, HD // 2, 1) * sine


def late_kernel(table_ref, x_ref, q_in, kv_in, sq_in, wq_ref, wkv_ref, cos_ref, sin_ref, *refs):
    q_out, keys_out, values_out, send_out = refs[:4]
    q_buf, keys_buf, values_buf, page_buf, index_ref, index_sem, sems, page_sems = refs[4:]
    indices = pltpu.make_async_copy(table_ref, index_ref, index_sem)
    indices.start()
    row = lax.broadcasted_iota(jnp.int32, (2 * PAGE, 2 * PAGE), 0)
    column = lax.broadcasted_iota(jnp.int32, (2 * PAGE, 2 * PAGE), 1)
    picker = (column == (row >> 1) + (row & 1) * PAGE).astype(BF16)
    values_buf[:, HD:] = jnp.ones((ROWS, HD), BF16)
    copies = []
    for r in range(0, ROWS, TILE):
        rows = slice(r, r + TILE)
        x = x_ref[rows, :]
        kv_sum = kv_in[rows, :] + jnp.dot(x, wkv_ref[1], preferred_element_type=F32)
        q_sum = q_in[rows, :] + jnp.dot(x, wq_ref[1], preferred_element_type=F32)
        squares = sq_in[rows, :] + squares_of(x)
        mean = jnp.sum(squares, axis=1, keepdims=True) / D
        inv_norm = jnp.broadcast_to(lax.rsqrt(mean + 1e-05), (TILE, HD))
        cosine, sine = cos_ref[rows, :], sin_ref[rows, :]
        keys = turn(kv_sum[:, :HD] * inv_norm, cosine, sine).astype(BF16)
        values = (kv_sum[:, HD:] * inv_norm).astype(BF16)
        keys_buf[rows, :] = keys
        values_buf[rows, :HD] = values
        if r == 0:
            indices.wait()
        for p in range(0, TILE, PAGE):
            page = (r + p) // PAGE
            both = jnp.concatenate([keys[p : p + PAGE], values[p : p + PAGE]], axis=0)
            page_buf[page] = jnp.dot(picker, both, preferred_element_type=F32).astype(BF16)
            target = send_out.at[index_ref[page, PUSH]]
            copies.append(pltpu.make_async_copy(page_buf.at[page], target, page_sems.at[page]))
            copies[-1].start()
        for head in range(HEADS):
            part = q_sum[:, head * HD : (head + 1) * HD] * inv_norm
            q_buf[head, rows, :] = turn(part, cosine, sine).astype(BF16)
        span = pl.ds(r, TILE)
        results = (
            (q_buf.at[:, span, :], q_out.at[:, span, :]),
            (keys_buf.at[span, :], keys_out.at[span, :]),
            (values_buf.at[span, :], values_out.at[span, :]),
        )
        for i, (source, target) in enumerate(results):
            copies.append(pltpu.make_async_copy(source, target, sems.at[3 * (r // TILE) + i]))
            copies[-1].start()
    for copy in copies:
        copy.wait()


def project_late(table, block, sums, weights, cosine, sine):
    results = [(HEADS, ROWS, HD), (ROWS, HD), (ROWS, 2 * HD)]
    return pl.pallas_call(
        late_kernel,
        out_shape=[pltpu.HBM(x, BF16) for x in results]
        + [pltpu.HBM((POOL * PUSH_CAP, 2 * PAGE, HD), BF16)],
        in_specs=[VMEM] * 9,
        out_specs=[HBM] * 4,
        scratch_shapes=[
            *[pltpu.VMEM(x, BF16) for x in results],
            pltpu.VMEM((NEW_PAGES, 2 * PAGE, HD), BF16),
            pltpu.SMEM((24, HD), jnp.int32),
            pltpu.SemaphoreType.DMA,
            pltpu.SemaphoreType.DMA((3 * ROWS // TILE,)),
            pltpu.SemaphoreType.DMA((NEW_PAGES,)),
        ],
        compiler_params=params(16),
        cost_estimate=cost(0, 1),
        name="project_late",
    )(table, block, *sums, *weights, cosine, sine)


def dot_nt(a, b):
    return lax.dot_general(a, b, (((1,), (1,)), ((), ())), preferred_element_type=F32)


def attend_kernel(table_ref, *refs):
    sources, out_ref, targets, (index_ref, keys, values, sems) = refs[:4], refs[4], refs[5:9], refs[9:]
    page_buf, q_buf, own_keys, own_values = targets
    indices = pltpu.make_async_copy(table_ref, index_ref, sems.at[4])
    indices.start()
    copies = [pltpu.make_async_copy(a, b, sems.at[i]) for i, (a, b) in enumerate(zip(sources, targets))]
    for copy in copies:
        copy.start()
    row = lax.broadcasted_iota(jnp.int32, (2 * PAGE, 2 * PAGE), 0)
    column = lax.broadcasted_iota(jnp.int32, (2 * PAGE, 2 * PAGE), 1)
    wanted = jnp.where(row < PAGE, 2 * row, 2 * (row - PAGE) + 1)
    picker = (column == wanted).astype(BF16)
    values[:, HD:] = jnp.ones((PAGES * PAGE, HD), BF16)
    indices.wait()
    copies[0].wait()
    for page in range(PAGES):
        both = jnp.dot(picker, page_buf[index_ref[TAKE, page]], preferred_element_type=F32)
        rows = slice(page * PAGE, (page + 1) * PAGE)
        keys[rows, :] = both[:PAGE].astype(BF16)
        values[rows, :HD] = both[PAGE:].astype(BF16)
    for copy in copies[1:]:
        copy.wait()
    block = 256
    allowed = lax.broadcasted_iota(jnp.int32, (block, block), 0) >= lax.broadcasted_iota(
        jnp.int32, (block, block), 1
    )
    for head in range(HEADS):
        lanes = slice(head * HD, (head + 1) * HD)
        for b in range(ROWS // block):
            rows = slice(b * block, (b + 1) * block)
            queries = q_buf[head, rows, :]
            own = dot_nt(queries, own_keys[: (b + 1) * block, :])
            diagonal = jnp.where(allowed, own[:, b * block :], -1e30)
            parts = [(diagonal, own_values[rows, :])]
            if b:
                parts.append((own[:, : b * block], own_values[: b * block, :]))
            parts.append((dot_nt(queries, keys[...]), values[...]))
            tops = [jnp.max(scores, axis=1, keepdims=True) for scores, _ in parts]
            top = functools.reduce(jnp.maximum, tops)
            both = jnp.zeros((block, 2 * HD), F32)
            for scores, held in parts:
                weights = jnp.exp2((scores - top) * SCALE).astype(BF16)
                both += jnp.dot(weights, held, preferred_element_type=F32)
            out_ref[rows, lanes] = (both[:, :HD] / both[:, HD:]).astype(BF16)


def attend(table, *sources):
    return pl.pallas_call(
        attend_kernel,
        out_shape=shape((ROWS, QW), BF16),
        in_specs=[VMEM] + [HBM] * len(sources),
        out_specs=VMEM,
        scratch_shapes=[
            *[pltpu.VMEM(x.shape, x.dtype) for x in sources],
            pltpu.SMEM((24, HD), jnp.int32),
            pltpu.VMEM((PAGES * PAGE, HD), BF16),
            pltpu.VMEM((PAGES * PAGE, 2 * HD), BF16),
            pltpu.SemaphoreType.DMA((5,)),
        ],
        compiler_params=params(40),
        cost_estimate=cost(2 * ROWS * 4 * 2560 * 512, 8 * MIB),
        name="attend",
    )(table, *[hbm(x) for x in sources])


def place_kernel(table_ref, received_ref, out_ref, buffer, index_ref, index_sem, sems):
    indices = pltpu.make_async_copy(table_ref, index_ref, index_sem)
    indices.start()
    indices.wait()
    group = 4
    copies = []
    for i in range(SLOTS):
        source = index_ref[PLACE, i]
        page = received_ref[jnp.maximum(source - 1, 0)]
        buffer[i] = jnp.where(source > 0, page, jnp.zeros_like(page))
        if i % group == group - 1:
            slots = pl.ds(i + 1 - group, group)
            copy = pltpu.make_async_copy(
                buffer.at[slots], out_ref.at[slots], sems.at[i // group]
            )
            copy.start()
            copies.append(copy)
    for copy in copies:
        copy.wait()


def place_pages(table, received):
    return pl.pallas_call(
        place_kernel,
        out_shape=pltpu.HBM((SLOTS, 2 * PAGE, HD), BF16),
        in_specs=[VMEM, VMEM],
        out_specs=HBM,
        scratch_shapes=[
            pltpu.VMEM((SLOTS, 2 * PAGE, HD), BF16),
            pltpu.SMEM((24, HD), jnp.int32),
            pltpu.SemaphoreType.DMA,
            pltpu.SemaphoreType.DMA((SLOTS // 4,)),
        ],
        compiler_params=params(8),
        cost_estimate=cost(0, 2 * MIB),
        name="place_pages",
    )(table, received)


def shift(values, steps):
    pairs = [(i, ((i // 2 + steps[i % 2]) % 4) * 2 + i % 2) for i in range(8)]
    return lax.ppermute(values, "tp", pairs)


def swap(values):
    return lax.ppermute(values, "tp", [(i, i ^ 1) for i in range(8)])


def rope_tables(row_count, offset):
    half_dim = HD // 2
    frequency = 500000.0 ** (-(jnp.arange(half_dim, dtype=F32) * (2.0 / HD)))
    place = (offset + jnp.arange(row_count, dtype=jnp.int32)).astype(F32)
    angles = place[:, None] * frequency[None, :]
    cosine, sine = jnp.cos(angles), jnp.sin(angles)
    return jnp.concatenate([cosine, cosine], 1), jnp.concatenate([-sine, sine], 1)


def exchange(values):
    return lax.all_to_all(values, "pool", split_axis=0, concat_axis=0, tiled=True)


def body(hidden, w_query, w_keyval, store, page_owner, page_slot, new_owner):
    near = shift(hidden, (1, -1))
    table, packed = prelude(page_owner, page_slot, new_owner, store.reshape(64, 2 * PAGE, HD))
    pages = exchange(packed)
    sibling = swap(hidden)
    (sibling,) = after((table,), sibling)
    back = shift(sibling, (1, -1))
    tables = rope_tables(ROWS, PAGES * PAGE)
    weights = (w_query, w_keyval)
    blocks = ((OWN, True), (OWN, False))
    sums = project(blocks, [sibling], [hidden], *weights, tokens=tables)
    (near,) = after((sums[2],), near)
    far = shift(near, (1, -1))
    blocks = ((NEAR, False), (BACK, True))
    sums = project(blocks, [near, back], [], *weights, sums, flops=HIDES)
    blocks, ahead = ((NEAR, True), (BACK, False)), ((FAR, False), (FAR, True))
    held = [swap(near), swap(back)]
    *sums, last_q, last_kv = project(blocks, held, [], *weights, sums, ahead)
    (far,) = after((sums[2],), far)
    other = swap(far)
    sums = project_far(far, (last_q, last_kv), sums)
    queries, own_keys, own_values, send = project_late(
        table, other, sums, (last_q, last_kv), *tables
    )
    received = exchange(send)
    attended = attend(table, pages, queries, own_keys, own_values)
    placed = place_pages(table, received)
    return attended, placed.reshape(SLOTS, 1, PAGE, 2, HD)


def solution(mesh):
    in_specs = (
        P("pool", "tp"),
        P(None, "tp"),
        P(None, "tp"),
        P("pool", "tp", None, None, None),
        P(),
        P(),
        P(),
    )
    out_specs = (P("pool", "tp"), P("pool", "tp", None, None, None))
    return jax.shard_map(body, mesh=mesh, in_specs=in_specs, out_specs=out_specs, check_vma=False)
```

```python
import functools
import math

import jax
import jax.numpy as jnp
from jax import lax
from jax.experimental import pallas as pl
from jax.experimental.pallas import tpu as pltpu
from jax.sharding import PartitionSpec as P

D = 8192
HD = 128
PAGE = 64
CAP = 4
PUSH_CAP = 2
HEADS = 4
FEAT = 1024
QW = 512
KVW = 256
POOL = 16
PAGES = 32
NEW_PAGES = 8
SLOTS = 32
ROWS = 512
PUSH, TAKE, PLACE = 4, 16, 17
MIB = 1024 * 1024
SCALE = math.log2(math.e) / math.sqrt(HD)
HIDES = 20_000_000_000
F32 = jnp.float32
BF16 = jnp.bfloat16
ANY = pl.BlockSpec(memory_space=pl.ANY)
HBM = pl.BlockSpec(memory_space=pltpu.HBM)
VMEM = pl.BlockSpec(memory_space=pltpu.VMEM)
SMEM = pl.BlockSpec(memory_space=pltpu.SMEM)


def params(mib):
    return pltpu.CompilerParams(vmem_limit_bytes=mib * MIB)


def cost(flops, nbytes):
    return pl.CostEstimate(flops=flops, bytes_accessed=nbytes, transcendentals=0)


def hbm(array):
    return pltpu.with_memory_space_constraint(array, pltpu.HBM)


def shape(dims, dtype):
    return jax.ShapeDtypeStruct(dims, dtype)


def fill_table(owners, slots, targets, out_ref):
    me = lax.axis_index("pool")
    out_ref[...] = jnp.zeros_like(out_ref)
    lanes = lax.broadcasted_iota(jnp.int32, owners.shape, 1)
    rows = lax.broadcasted_iota(jnp.int32, owners.shape, 0)
    ranks = jnp.zeros_like(owners)
    for j in range(PAGES):
        ranks += ((owners == owners[:, j : j + 1]) & (lanes > j)).astype(jnp.int32)
    for k in range(CAP):
        chosen = jnp.where((owners == me) & (ranks == k), slots, 0)
        out_ref[:POOL, k : k + 1] = jnp.sum(chosen, axis=1, keepdims=True)
    mine = jnp.where(rows == me, owners * CAP + ranks, 0)
    out_ref[TAKE : TAKE + 1, :PAGES] = jnp.sum(mine, axis=0, keepdims=True)
    lanes = lax.broadcasted_iota(jnp.int32, targets.shape, 1)
    rows = lax.broadcasted_iota(jnp.int32, targets.shape, 0)
    kept = (targets == me).astype(jnp.int32)
    ranks = jnp.zeros_like(targets)
    slot = jnp.zeros_like(targets)
    for j in range(NEW_PAGES):
        later = rows > j
        ranks += ((targets == targets[j : j + 1, :]) & later).astype(jnp.int32)
        slot += jnp.where(later, kept[j : j + 1, :], 0)
    mine = jnp.where(lanes == me, targets * PUSH_CAP + ranks, 0)
    out_ref[:NEW_PAGES, PUSH : PUSH + 1] = jnp.sum(mine, axis=1, keepdims=True)
    of_request = jnp.sum(kept, axis=0, keepdims=True)
    for r in range(POOL):
        slot += jnp.where(lanes > r, of_request[:, r : r + 1], 0)
    source = jnp.zeros((NEW_PAGES, SLOTS), jnp.int32)
    slot_lanes = lax.broadcasted_iota(jnp.int32, source.shape, 1)
    for r in range(POOL):
        hit = (kept[:, r : r + 1] > 0) & (slot[:, r : r + 1] == slot_lanes)
        source += jnp.where(hit, r * PUSH_CAP + ranks[:, r : r + 1] + 1, 0)
    out_ref[PLACE : PLACE + 1, :SLOTS] = jnp.sum(source, axis=0, keepdims=True)


def prelude_kernel(*refs):
    owner_in, slot_in, target_in, store_in, table_ref, out_ref = refs[:6]
    owner_ref, slot_ref, target_ref, store_ref, index_ref, sems, page_sems = refs[6:]
    pairs = (
        (owner_in, owner_ref),
        (slot_in, slot_ref),
        (target_in, target_ref),
        (store_in, store_ref),
    )
    copies = [pltpu.make_async_copy(x, y, sems.at[i]) for i, (x, y) in enumerate(pairs)]
    for copy in copies:
        copy.start()
    for copy in copies[:3]:
        copy.wait()
    fill_table(owner_ref[...], slot_ref[...], target_ref[...], table_ref)
    indices = pltpu.make_async_copy(table_ref, index_ref, sems.at[4])
    indices.start()
    indices.wait()
    copies[3].wait()
    pages = [
        pltpu.make_async_copy(
            store_ref.at[index_ref[i // CAP, i % CAP]], out_ref.at[i], page_sems.at[i]
        )
        for i in range(POOL * CAP)
    ]
    for page in pages:
        page.start()
    for page in pages:
        page.wait()


def prelude(page_owner, page_slot, new_owner, store):
    return pl.pallas_call(
        prelude_kernel,
        out_shape=[
            shape((24, HD), jnp.int32),
            pltpu.HBM((POOL * CAP, 2 * PAGE, HD), BF16),
        ],
        in_specs=[HBM] * 4,
        out_specs=[VMEM, HBM],
        scratch_shapes=[
            pltpu.VMEM((POOL, PAGES), jnp.int32),
            pltpu.VMEM((POOL, PAGES), jnp.int32),
            pltpu.VMEM((NEW_PAGES, POOL), jnp.int32),
            pltpu.VMEM(store.shape, BF16),
            pltpu.SMEM((24, HD), jnp.int32),
            pltpu.SemaphoreType.DMA((5,)),
            pltpu.SemaphoreType.DMA((POOL * CAP,)),
        ],
        compiler_params=params(8),
        cost_estimate=cost(0, 1),
        name="prelude",
    )(*[hbm(x) for x in (page_owner, page_slot, new_owner.T, store)])


def block_index(steps, other_core):
    index = lax.axis_index("tp")
    core = lax.rem(index, 2)
    if other_core:
        core = 1 - core
    z = lax.rem(index // 2 + jnp.where(core == 0, steps[0], steps[1]), 4)
    return 2 * z + core


def squares_of(rows):
    wide = rows.astype(F32)
    total = None
    for lane in range(0, FEAT, HD):
        part = wide[:, lane : lane + HD]
        total = part * part if total is None else total + part * part
    return total


def weight_copies(refs, buffers, sems, blocks):
    copies = []
    for i, (steps, other) in enumerate(blocks):
        rows = pl.ds(pl.multiple_of(block_index(steps, other) * FEAT, FEAT), FEAT)
        copies.append(
            [
                pltpu.make_async_copy(ref.at[rows, :], buffer.at[i], sems.at[len(refs) * i + j])
                for j, (ref, buffer) in enumerate(zip(refs, buffers))
            ]
        )
    for group in copies:
        for copy in group:
            copy.start()
    return copies


OWN, NEAR, BACK, FAR = (0, 0), (3, 1), (1, 3), (2, 2)
TILE = 128


def project_kernel(blocks, held, has_sums, tokens, ahead, *refs):
    count = len(blocks)
    x_refs, refs = refs[:count], refs[count:]
    wq_ref, wkv_ref, refs = refs[0], refs[1], refs[2:]
    before, refs = (refs[:3], refs[3:]) if has_sums else (None, refs)
    refs = refs[tokens:]
    sums, refs = refs[:3], refs[3:]
    fetched, refs = (refs[:2], refs[2:]) if ahead else (None, refs)
    x_buf, wq_buf, wkv_buf, sems, x_sems, ahead_sems = refs
    copies = weight_copies((wq_ref, wkv_ref), (wq_buf, wkv_buf), sems, blocks)
    x_copies = {}
    for i in range(held, count):
        x_copies[i] = pltpu.make_async_copy(x_refs[i], x_buf.at[i - held], x_sems.at[i - held])
        x_copies[i].start()
    later = weight_copies((wq_ref, wkv_ref), fetched, ahead_sems, ahead) if ahead else []
    for i in range(count):
        copies[i][0].wait()
        copies[i][1].wait()
        if i in x_copies:
            x_copies[i].wait()
        for r in range(0, ROWS, TILE):
            rows = slice(r, r + TILE)
            x = x_refs[i][rows, :] if i < held else x_buf[i - held, rows, :]
            parts = (
                jnp.dot(x, wq_buf[i], preferred_element_type=F32),
                jnp.dot(x, wkv_buf[i], preferred_element_type=F32),
                squares_of(x),
            )
            for j, part in enumerate(parts):
                if i > 0:
                    sums[j][rows, :] += part
                elif has_sums:
                    sums[j][rows, :] = before[j][rows, :] + part
                else:
                    sums[j][rows, :] = part
    for group in later:
        for copy in group:
            copy.wait()


def project(blocks, held, direct, w_query, w_keyval, sums=(), ahead=(), tokens=(), flops=0):
    count = len(blocks)
    shapes = [shape((ROWS, w), F32) for w in (QW, KVW, HD)]
    if ahead:
        shapes += [shape((len(ahead), FEAT, w), BF16) for w in (QW, KVW)]
    return pl.pallas_call(
        functools.partial(project_kernel, blocks, len(held), bool(sums), len(tokens), ahead),
        out_shape=shapes,
        in_specs=[VMEM] * len(held)
        + [HBM] * (len(direct) + 2)
        + [VMEM] * len(sums)
        + [ANY] * len(tokens),
        out_specs=[VMEM] * len(shapes),
        scratch_shapes=[
            pltpu.VMEM((max(len(direct), 1), ROWS, FEAT), BF16),
            pltpu.VMEM((count, FEAT, QW), BF16),
            pltpu.VMEM((count, FEAT, KVW), BF16),
            pltpu.SemaphoreType.DMA((2 * count,)),
            pltpu.SemaphoreType.DMA((max(len(direct), 1),)),
            pltpu.SemaphoreType.DMA((max(2 * len(ahead), 1),)),
        ],
        compiler_params=params(24),
        cost_estimate=cost(flops, 1),
        name="project",
    )(*held, *[hbm(x) for x in (*direct, w_query, w_keyval)], *sums, *tokens)


def far_kernel(x_ref, wq_ref, wkv_ref, *refs):
    before, sums = refs[:3], refs[3:]
    for r in range(0, ROWS, TILE):
        rows = slice(r, r + TILE)
        x = x_ref[rows, :]
        sums[0][rows, :] = before[0][rows, :] + jnp.dot(x, wq_ref[0], preferred_element_type=F32)
        sums[1][rows, :] = before[1][rows, :] + jnp.dot(x, wkv_ref[0], preferred_element_type=F32)
        sums[2][rows, :] = before[2][rows, :] + squares_of(x)


def project_far(block, weights, sums):
    return pl.pallas_call(
        far_kernel,
        out_shape=[shape((ROWS, w), F32) for w in (QW, KVW, HD)],
        in_specs=[VMEM] * 6,
        out_specs=[VMEM] * 3,
        compiler_params=params(16),
        cost_estimate=cost(0, 1),
        name="project_far",
    )(block, *weights, *sums)


def after_kernel(*refs):
    pass


def after(tokens, *arrays, flops=0):
    count, skip = len(arrays), len(tokens)
    return pl.pallas_call(
        after_kernel,
        out_shape=[shape(x.shape, x.dtype) for x in arrays],
        in_specs=[ANY] * (count + skip),
        out_specs=[ANY] * count,
        input_output_aliases={i + skip: i for i in range(count)},
        compiler_params=params(1),
        cost_estimate=cost(flops, 1),
        name="after",
    )(*tokens, *arrays)


def turn(values, cosine, sine):
    return values * cosine + pltpu.roll(values, HD // 2, 1) * sine


def late_kernel(table_ref, x_ref, q_in, kv_in, sq_in, wq_ref, wkv_ref, cos_ref, sin_ref, *refs):
    q_out, keys_out, values_out, send_out = refs[:4]
    q_buf, keys_buf, values_buf, page_buf, index_ref, index_sem, sems, page_sems = refs[4:]
    indices = pltpu.make_async_copy(table_ref, index_ref, index_sem)
    indices.start()
    row = lax.broadcasted_iota(jnp.int32, (2 * PAGE, 2 * PAGE), 0)
    column = lax.broadcasted_iota(jnp.int32, (2 * PAGE, 2 * PAGE), 1)
    picker = (column == (row >> 1) + (row & 1) * PAGE).astype(BF16)
    values_buf[:, HD:] = jnp.ones((ROWS, HD), BF16)
    copies = []
    for r in range(0, ROWS, TILE):
        rows = slice(r, r + TILE)
        x = x_ref[rows, :]
        kv_sum = kv_in[rows, :] + jnp.dot(x, wkv_ref[1], preferred_element_type=F32)
        q_sum = q_in[rows, :] + jnp.dot(x, wq_ref[1], preferred_element_type=F32)
        squares = sq_in[rows, :] + squares_of(x)
        mean = jnp.sum(squares, axis=1, keepdims=True) / D
        inv_norm = jnp.broadcast_to(lax.rsqrt(mean + 1e-05), (TILE, HD))
        cosine, sine = cos_ref[rows, :], sin_ref[rows, :]
        keys = turn(kv_sum[:, :HD] * inv_norm, cosine, sine).astype(BF16)
        values = (kv_sum[:, HD:] * inv_norm).astype(BF16)
        keys_buf[rows, :] = keys
        values_buf[rows, :HD] = values
        if r == 0:
            indices.wait()
        for p in range(0, TILE, PAGE):
            page = (r + p) // PAGE
            both = jnp.concatenate([keys[p : p + PAGE], values[p : p + PAGE]], axis=0)
            page_buf[page] = jnp.dot(picker, both, preferred_element_type=F32).astype(BF16)
            target = send_out.at[index_ref[page, PUSH]]
            copies.append(pltpu.make_async_copy(page_buf.at[page], target, page_sems.at[page]))
            copies[-1].start()
        for head in range(HEADS):
            part = q_sum[:, head * HD : (head + 1) * HD] * inv_norm
            q_buf[head, rows, :] = turn(part, cosine, sine).astype(BF16)
        span = pl.ds(r, TILE)
        results = (
            (q_buf.at[:, span, :], q_out.at[:, span, :]),
            (keys_buf.at[span, :], keys_out.at[span, :]),
            (values_buf.at[span, :], values_out.at[span, :]),
        )
        for i, (source, target) in enumerate(results):
            copies.append(pltpu.make_async_copy(source, target, sems.at[3 * (r // TILE) + i]))
            copies[-1].start()
    for copy in copies:
        copy.wait()


def project_late(table, block, sums, weights, cosine, sine):
    results = [(HEADS, ROWS, HD), (ROWS, HD), (ROWS, 2 * HD)]
    return pl.pallas_call(
        late_kernel,
        out_shape=[pltpu.HBM(x, BF16) for x in results]
        + [pltpu.HBM((POOL * PUSH_CAP, 2 * PAGE, HD), BF16)],
        in_specs=[VMEM] * 9,
        out_specs=[HBM] * 4,
        scratch_shapes=[
            *[pltpu.VMEM(x, BF16) for x in results],
            pltpu.VMEM((NEW_PAGES, 2 * PAGE, HD), BF16),
            pltpu.SMEM((24, HD), jnp.int32),
            pltpu.SemaphoreType.DMA,
            pltpu.SemaphoreType.DMA((3 * ROWS // TILE,)),
            pltpu.SemaphoreType.DMA((NEW_PAGES,)),
        ],
        compiler_params=params(16),
        cost_estimate=cost(0, 1),
        name="project_late",
    )(table, block, *sums, *weights, cosine, sine)


def dot_nt(a, b):
    return lax.dot_general(a, b, (((1,), (1,)), ((), ())), preferred_element_type=F32)


def attend_kernel(table_ref, *refs):
    sources, out_ref, targets, (index_ref, keys, values, sems) = refs[:4], refs[4], refs[5:9], refs[9:]
    page_buf, q_buf, own_keys, own_values = targets
    indices = pltpu.make_async_copy(table_ref, index_ref, sems.at[4])
    indices.start()
    copies = [pltpu.make_async_copy(a, b, sems.at[i]) for i, (a, b) in enumerate(zip(sources, targets))]
    for copy in copies:
        copy.start()
    row = lax.broadcasted_iota(jnp.int32, (2 * PAGE, 2 * PAGE), 0)
    column = lax.broadcasted_iota(jnp.int32, (2 * PAGE, 2 * PAGE), 1)
    wanted = jnp.where(row < PAGE, 2 * row, 2 * (row - PAGE) + 1)
    picker = (column == wanted).astype(BF16)
    values[:, HD:] = jnp.ones((PAGES * PAGE, HD), BF16)
    indices.wait()
    copies[0].wait()
    for page in range(PAGES):
        both = jnp.dot(picker, page_buf[index_ref[TAKE, page]], preferred_element_type=F32)
        rows = slice(page * PAGE, (page + 1) * PAGE)
        keys[rows, :] = both[:PAGE].astype(BF16)
        values[rows, :HD] = both[PAGE:].astype(BF16)
    for copy in copies[1:]:
        copy.wait()
    block = 256
    allowed = lax.broadcasted_iota(jnp.int32, (block, block), 0) >= lax.broadcasted_iota(
        jnp.int32, (block, block), 1
    )
    for head in range(HEADS):
        lanes = slice(head * HD, (head + 1) * HD)
        for b in range(ROWS // block):
            rows = slice(b * block, (b + 1) * block)
            queries = q_buf[head, rows, :]
            own = dot_nt(queries, own_keys[: (b + 1) * block, :])
            diagonal = jnp.where(allowed, own[:, b * block :], -1e30)
            parts = [(diagonal, own_values[rows, :])]
            if b:
                parts.append((own[:, : b * block], own_values[: b * block, :]))
            parts.append((dot_nt(queries, keys[...]), values[...]))
            tops = [jnp.max(scores, axis=1, keepdims=True) for scores, _ in parts]
            top = functools.reduce(jnp.maximum, tops)
            both = jnp.zeros((block, 2 * HD), F32)
            for scores, held in parts:
                weights = jnp.exp2((scores - top) * SCALE).astype(BF16)
                both += jnp.dot(weights, held, preferred_element_type=F32)
            out_ref[rows, lanes] = (both[:, :HD] / both[:, HD:]).astype(BF16)


def attend(table, *sources):
    return pl.pallas_call(
        attend_kernel,
        out_shape=shape((ROWS, QW), BF16),
        in_specs=[VMEM] + [HBM] * len(sources),
        out_specs=VMEM,
        scratch_shapes=[
            *[pltpu.VMEM(x.shape, x.dtype) for x in sources],
            pltpu.SMEM((24, HD), jnp.int32),
            pltpu.VMEM((PAGES * PAGE, HD), BF16),
            pltpu.VMEM((PAGES * PAGE, 2 * HD), BF16),
            pltpu.SemaphoreType.DMA((5,)),
        ],
        compiler_params=params(40),
        cost_estimate=cost(2 * ROWS * 4 * 2560 * 512, 8 * MIB),
        name="attend",
    )(table, *[hbm(x) for x in sources])


def place_kernel(table_ref, received_ref, out_ref, buffer, index_ref, index_sem, sems):
    indices = pltpu.make_async_copy(table_ref, index_ref, index_sem)
    indices.start()
    indices.wait()
    group = 4
    copies = []
    for i in range(SLOTS):
        source = index_ref[PLACE, i]
        page = received_ref[jnp.maximum(source - 1, 0)]
        buffer[i] = jnp.where(source > 0, page, jnp.zeros_like(page))
        if i % group == group - 1:
            slots = pl.ds(i + 1 - group, group)
            copy = pltpu.make_async_copy(
                buffer.at[slots], out_ref.at[slots], sems.at[i // group]
            )
            copy.start()
            copies.append(copy)
    for copy in copies:
        copy.wait()


def place_pages(table, received):
    return pl.pallas_call(
        place_kernel,
        out_shape=pltpu.HBM((SLOTS, 2 * PAGE, HD), BF16),
        in_specs=[VMEM, VMEM],
        out_specs=HBM,
        scratch_shapes=[
            pltpu.VMEM((SLOTS, 2 * PAGE, HD), BF16),
            pltpu.SMEM((24, HD), jnp.int32),
            pltpu.SemaphoreType.DMA,
            pltpu.SemaphoreType.DMA((SLOTS // 4,)),
        ],
        compiler_params=params(8),
        cost_estimate=cost(0, 2 * MIB),
        name="place_pages",
    )(table, received)


def shift(values, steps):
    pairs = [(i, ((i // 2 + steps[i % 2]) % 4) * 2 + i % 2) for i in range(8)]
    return lax.ppermute(values, "tp", pairs)


def swap(values):
    return lax.ppermute(values, "tp", [(i, i ^ 1) for i in range(8)])


def rope_tables(row_count, offset):
    half_dim = HD // 2
    frequency = 500000.0 ** (-(jnp.arange(half_dim, dtype=F32) * (2.0 / HD)))
    place = (offset + jnp.arange(row_count, dtype=jnp.int32)).astype(F32)
    angles = place[:, None] * frequency[None, :]
    cosine, sine = jnp.cos(angles), jnp.sin(angles)
    return jnp.concatenate([cosine, cosine], 1), jnp.concatenate([-sine, sine], 1)


def exchange(values):
    return lax.all_to_all(values, "pool", split_axis=0, concat_axis=0, tiled=True)


def body(hidden, w_query, w_keyval, store, page_owner, page_slot, new_owner):
    near = shift(hidden, (1, -1))
    table, packed = prelude(page_owner, page_slot, new_owner, store.reshape(64, 2 * PAGE, HD))
    pages = exchange(packed)
    sibling = swap(hidden)
    back = shift(sibling, (1, -1))
    tables = rope_tables(ROWS, PAGES * PAGE)
    weights = (w_query, w_keyval)
    blocks = ((OWN, True), (OWN, False))
    sums = project(blocks, [sibling], [hidden], *weights, tokens=tables, flops=HIDES)
    blocks = ((NEAR, True), (NEAR, False))
    sums = project(blocks, [swap(near), near], [], *weights, sums, flops=HIDES)
    (near,) = after((sums[2],), near)
    far = shift(near, (1, -1))
    sums = project(((BACK, True),), [back], [], *weights, sums, flops=HIDES)
    blocks, ahead = ((BACK, False),), ((FAR, False), (FAR, True))
    *sums, last_q, last_kv = project(blocks, [swap(back)], [], *weights, sums, ahead)
    (far,) = after((sums[2],), far)
    other = swap(far)
    sums = project_far(far, (last_q, last_kv), sums)
    queries, own_keys, own_values, send = project_late(
        table, other, sums, (last_q, last_kv), *tables
    )
    received = exchange(send)
    attended = attend(table, pages, queries, own_keys, own_values)
    placed = place_pages(table, received)
    return attended, placed.reshape(SLOTS, 1, PAGE, 2, HD)


def solution(mesh):
    in_specs = (
        P("pool", "tp"),
        P(None, "tp"),
        P(None, "tp"),
        P("pool", "tp", None, None, None),
        P(),
        P(),
        P(),
    )
    out_specs = (P("pool", "tp"), P("pool", "tp", None, None, None))
    return jax.shard_map(body, mesh=mesh, in_specs=in_specs, out_specs=out_specs, check_vma=False)
```

```python
import functools
import math

import jax
import jax.numpy as jnp
from jax import lax
from jax.experimental import pallas as pl
from jax.experimental.pallas import tpu as pltpu
from jax.sharding import PartitionSpec as P

D = 8192
HD = 128
PAGE = 64
CAP = 4
PUSH_CAP = 2
HEADS = 4
FEAT = 1024
QW = 512
KVW = 256
POOL = 16
PAGES = 32
NEW_PAGES = 8
SLOTS = 32
ROWS = 512
PUSH, TAKE, PLACE = 4, 16, 17
MIB = 1024 * 1024
SCALE = math.log2(math.e) / math.sqrt(HD)
HIDES = 20_000_000_000
F32 = jnp.float32
BF16 = jnp.bfloat16
ANY = pl.BlockSpec(memory_space=pl.ANY)
HBM = pl.BlockSpec(memory_space=pltpu.HBM)
VMEM = pl.BlockSpec(memory_space=pltpu.VMEM)
SMEM = pl.BlockSpec(memory_space=pltpu.SMEM)


def params(mib):
    return pltpu.CompilerParams(vmem_limit_bytes=mib * MIB)


def cost(flops, nbytes):
    return pl.CostEstimate(flops=flops, bytes_accessed=nbytes, transcendentals=0)


def hbm(array):
    return pltpu.with_memory_space_constraint(array, pltpu.HBM)


def shape(dims, dtype):
    return jax.ShapeDtypeStruct(dims, dtype)


def fill_table(owners, slots, targets, out_ref):
    me = lax.axis_index("pool")
    out_ref[...] = jnp.zeros_like(out_ref)
    lanes = lax.broadcasted_iota(jnp.int32, owners.shape, 1)
    rows = lax.broadcasted_iota(jnp.int32, owners.shape, 0)
    ranks = jnp.zeros_like(owners)
    for j in range(PAGES):
        ranks += ((owners == owners[:, j : j + 1]) & (lanes > j)).astype(jnp.int32)
    for k in range(CAP):
        chosen = jnp.where((owners == me) & (ranks == k), slots, 0)
        out_ref[:POOL, k : k + 1] = jnp.sum(chosen, axis=1, keepdims=True)
    mine = jnp.where(rows == me, owners * CAP + ranks, 0)
    out_ref[TAKE : TAKE + 1, :PAGES] = jnp.sum(mine, axis=0, keepdims=True)
    lanes = lax.broadcasted_iota(jnp.int32, targets.shape, 1)
    rows = lax.broadcasted_iota(jnp.int32, targets.shape, 0)
    kept = (targets == me).astype(jnp.int32)
    ranks = jnp.zeros_like(targets)
    slot = jnp.zeros_like(targets)
    for j in range(NEW_PAGES):
        later = rows > j
        ranks += ((targets == targets[j : j + 1, :]) & later).astype(jnp.int32)
        slot += jnp.where(later, kept[j : j + 1, :], 0)
    mine = jnp.where(lanes == me, targets * PUSH_CAP + ranks, 0)
    out_ref[:NEW_PAGES, PUSH : PUSH + 1] = jnp.sum(mine, axis=1, keepdims=True)
    of_request = jnp.sum(kept, axis=0, keepdims=True)
    for r in range(POOL):
        slot += jnp.where(lanes > r, of_request[:, r : r + 1], 0)
    source = jnp.zeros((NEW_PAGES, SLOTS), jnp.int32)
    slot_lanes = lax.broadcasted_iota(jnp.int32, source.shape, 1)
    for r in range(POOL):
        hit = (kept[:, r : r + 1] > 0) & (slot[:, r : r + 1] == slot_lanes)
        source += jnp.where(hit, r * PUSH_CAP + ranks[:, r : r + 1] + 1, 0)
    out_ref[PLACE : PLACE + 1, :SLOTS] = jnp.sum(source, axis=0, keepdims=True)


def prelude_kernel(*refs):
    owner_in, slot_in, target_in, store_in, table_ref, out_ref = refs[:6]
    owner_ref, slot_ref, target_ref, store_ref, index_ref, sems, page_sems = refs[6:]
    pairs = (
        (owner_in, owner_ref),
        (slot_in, slot_ref),
        (target_in, target_ref),
        (store_in, store_ref),
    )
    copies = [pltpu.make_async_copy(x, y, sems.at[i]) for i, (x, y) in enumerate(pairs)]
    for copy in copies:
        copy.start()
    for copy in copies[:3]:
        copy.wait()
    fill_table(owner_ref[...], slot_ref[...], target_ref[...], table_ref)
    indices = pltpu.make_async_copy(table_ref, index_ref, sems.at[4])
    indices.start()
    indices.wait()
    copies[3].wait()
    pages = [
        pltpu.make_async_copy(
            store_ref.at[index_ref[i // CAP, i % CAP]], out_ref.at[i], page_sems.at[i]
        )
        for i in range(POOL * CAP)
    ]
    for page in pages:
        page.start()
    for page in pages:
        page.wait()


def prelude(page_owner, page_slot, new_owner, store):
    return pl.pallas_call(
        prelude_kernel,
        out_shape=[
            shape((24, HD), jnp.int32),
            pltpu.HBM((POOL * CAP, 2 * PAGE, HD), BF16),
        ],
        in_specs=[HBM] * 4,
        out_specs=[VMEM, HBM],
        scratch_shapes=[
            pltpu.VMEM((POOL, PAGES), jnp.int32),
            pltpu.VMEM((POOL, PAGES), jnp.int32),
            pltpu.VMEM((NEW_PAGES, POOL), jnp.int32),
            pltpu.VMEM(store.shape, BF16),
            pltpu.SMEM((24, HD), jnp.int32),
            pltpu.SemaphoreType.DMA((5,)),
            pltpu.SemaphoreType.DMA((POOL * CAP,)),
        ],
        compiler_params=params(8),
        cost_estimate=cost(0, 1),
        name="prelude",
    )(*[hbm(x) for x in (page_owner, page_slot, new_owner.T, store)])


def block_index(steps, other_core):
    index = lax.axis_index("tp")
    core = lax.rem(index, 2)
    if other_core:
        core = 1 - core
    z = lax.rem(index // 2 + jnp.where(core == 0, steps[0], steps[1]), 4)
    return 2 * z + core


def squares_of(rows):
    wide = rows.astype(F32)
    total = None
    for lane in range(0, FEAT, HD):
        part = wide[:, lane : lane + HD]
        total = part * part if total is None else total + part * part
    return total


def weight_copies(refs, buffers, sems, blocks):
    copies = []
    for i, (steps, other) in enumerate(blocks):
        rows = pl.ds(pl.multiple_of(block_index(steps, other) * FEAT, FEAT), FEAT)
        copies.append(
            [
                pltpu.make_async_copy(ref.at[rows, :], buffer.at[i], sems.at[len(refs) * i + j])
                for j, (ref, buffer) in enumerate(zip(refs, buffers))
            ]
        )
    for group in copies:
        for copy in group:
            copy.start()
    return copies


OWN, NEAR, BACK, FAR = (0, 0), (3, 1), (1, 3), (2, 2)
TILE = 128


def project_kernel(blocks, held, has_sums, tokens, ahead, *refs):
    count = len(blocks)
    x_refs, refs = refs[:count], refs[count:]
    wq_ref, wkv_ref, refs = refs[0], refs[1], refs[2:]
    before, refs = (refs[:3], refs[3:]) if has_sums else (None, refs)
    refs = refs[tokens:]
    sums, refs = refs[:3], refs[3:]
    fetched, refs = (refs[:2], refs[2:]) if ahead else (None, refs)
    x_buf, wq_buf, wkv_buf, sems, x_sems, ahead_sems = refs
    copies = weight_copies((wq_ref, wkv_ref), (wq_buf, wkv_buf), sems, blocks)
    x_copies = {}
    for i in range(held, count):
        x_copies[i] = pltpu.make_async_copy(x_refs[i], x_buf.at[i - held], x_sems.at[i - held])
        x_copies[i].start()
    later = weight_copies((wq_ref, wkv_ref), fetched, ahead_sems, ahead) if ahead else []
    for i in range(count):
        copies[i][0].wait()
        copies[i][1].wait()
        if i in x_copies:
            x_copies[i].wait()
        for r in range(0, ROWS, TILE):
            rows = slice(r, r + TILE)
            x = x_refs[i][rows, :] if i < held else x_buf[i - held, rows, :]
            parts = (
                jnp.dot(x, wq_buf[i], preferred_element_type=F32),
                jnp.dot(x, wkv_buf[i], preferred_element_type=F32),
                squares_of(x),
            )
            for j, part in enumerate(parts):
                if i > 0:
                    sums[j][rows, :] += part
                elif has_sums:
                    sums[j][rows, :] = before[j][rows, :] + part
                else:
                    sums[j][rows, :] = part
    for group in later:
        for copy in group:
            copy.wait()


def project(blocks, held, direct, w_query, w_keyval, sums=(), ahead=(), tokens=(), flops=0):
    count = len(blocks)
    shapes = [shape((ROWS, w), F32) for w in (QW, KVW, HD)]
    if ahead:
        shapes += [shape((len(ahead), FEAT, w), BF16) for w in (QW, KVW)]
    return pl.pallas_call(
        functools.partial(project_kernel, blocks, len(held), bool(sums), len(tokens), ahead),
        out_shape=shapes,
        in_specs=[VMEM] * len(held)
        + [HBM] * (len(direct) + 2)
        + [VMEM] * len(sums)
        + [ANY] * len(tokens),
        out_specs=[VMEM] * len(shapes),
        scratch_shapes=[
            pltpu.VMEM((max(len(direct), 1), ROWS, FEAT), BF16),
            pltpu.VMEM((count, FEAT, QW), BF16),
            pltpu.VMEM((count, FEAT, KVW), BF16),
            pltpu.SemaphoreType.DMA((2 * count,)),
            pltpu.SemaphoreType.DMA((max(len(direct), 1),)),
            pltpu.SemaphoreType.DMA((max(2 * len(ahead), 1),)),
        ],
        compiler_params=params(24),
        cost_estimate=cost(flops, 1),
        name="project",
    )(*held, *[hbm(x) for x in (*direct, w_query, w_keyval)], *sums, *tokens)


def far_kernel(x_ref, wq_ref, wkv_ref, *refs):
    before, sums = refs[:3], refs[3:]
    for r in range(0, ROWS, TILE):
        rows = slice(r, r + TILE)
        x = x_ref[rows, :]
        sums[0][rows, :] = before[0][rows, :] + jnp.dot(x, wq_ref[0], preferred_element_type=F32)
        sums[1][rows, :] = before[1][rows, :] + jnp.dot(x, wkv_ref[0], preferred_element_type=F32)
        sums[2][rows, :] = before[2][rows, :] + squares_of(x)


def project_far(block, weights, sums):
    return pl.pallas_call(
        far_kernel,
        out_shape=[shape((ROWS, w), F32) for w in (QW, KVW, HD)],
        in_specs=[VMEM] * 6,
        out_specs=[VMEM] * 3,
        compiler_params=params(16),
        cost_estimate=cost(0, 1),
        name="project_far",
    )(block, *weights, *sums)


def after_kernel(*refs):
    pass


def after(tokens, *arrays, flops=0):
    count, skip = len(arrays), len(tokens)
    return pl.pallas_call(
        after_kernel,
        out_shape=[shape(x.shape, x.dtype) for x in arrays],
        in_specs=[ANY] * (count + skip),
        out_specs=[ANY] * count,
        input_output_aliases={i + skip: i for i in range(count)},
        compiler_params=params(1),
        cost_estimate=cost(flops, 1),
        name="after",
    )(*tokens, *arrays)


def turn(values, cosine, sine):
    return values * cosine + pltpu.roll(values, HD // 2, 1) * sine


def late_kernel(table_ref, x_ref, q_in, kv_in, sq_in, wq_ref, wkv_ref, cos_ref, sin_ref, *refs):
    q_out, keys_out, values_out, send_out = refs[:4]
    q_buf, keys_buf, values_buf, page_buf, index_ref, index_sem, sems, page_sems = refs[4:]
    indices = pltpu.make_async_copy(table_ref, index_ref, index_sem)
    indices.start()
    row = lax.broadcasted_iota(jnp.int32, (2 * PAGE, 2 * PAGE), 0)
    column = lax.broadcasted_iota(jnp.int32, (2 * PAGE, 2 * PAGE), 1)
    picker = (column == (row >> 1) + (row & 1) * PAGE).astype(BF16)
    values_buf[:, HD:] = jnp.ones((ROWS, HD), BF16)
    copies = []
    for r in range(0, ROWS, TILE):
        rows = slice(r, r + TILE)
        x = x_ref[rows, :]
        kv_sum = kv_in[rows, :] + jnp.dot(x, wkv_ref[1], preferred_element_type=F32)
        q_sum = q_in[rows, :] + jnp.dot(x, wq_ref[1], preferred_element_type=F32)
        squares = sq_in[rows, :] + squares_of(x)
        mean = jnp.sum(squares, axis=1, keepdims=True) / D
        inv_norm = jnp.broadcast_to(lax.rsqrt(mean + 1e-05), (TILE, HD))
        cosine, sine = cos_ref[rows, :], sin_ref[rows, :]
        keys = turn(kv_sum[:, :HD] * inv_norm, cosine, sine).astype(BF16)
        values = (kv_sum[:, HD:] * inv_norm).astype(BF16)
        keys_buf[rows, :] = keys
        values_buf[rows, :HD] = values
        if r == 0:
            indices.wait()
        for p in range(0, TILE, PAGE):
            page = (r + p) // PAGE
            both = jnp.concatenate([keys[p : p + PAGE], values[p : p + PAGE]], axis=0)
            page_buf[page] = jnp.dot(picker, both, preferred_element_type=F32).astype(BF16)
            target = send_out.at[index_ref[page, PUSH]]
            copies.append(pltpu.make_async_copy(page_buf.at[page], target, page_sems.at[page]))
            copies[-1].start()
        for head in range(HEADS):
            part = q_sum[:, head * HD : (head + 1) * HD] * inv_norm
            q_buf[head, rows, :] = turn(part, cosine, sine).astype(BF16)
        span = pl.ds(r, TILE)
        results = (
            (q_buf.at[:, span, :], q_out.at[:, span, :]),
            (keys_buf.at[span, :], keys_out.at[span, :]),
            (values_buf.at[span, :], values_out.at[span, :]),
        )
        for i, (source, target) in enumerate(results):
            copies.append(pltpu.make_async_copy(source, target, sems.at[3 * (r // TILE) + i]))
            copies[-1].start()
    for copy in copies:
        copy.wait()


def project_late(table, block, sums, weights, cosine, sine):
    results = [(HEADS, ROWS, HD), (ROWS, HD), (ROWS, 2 * HD)]
    return pl.pallas_call(
        late_kernel,
        out_shape=[pltpu.HBM(x, BF16) for x in results]
        + [pltpu.HBM((POOL * PUSH_CAP, 2 * PAGE, HD), BF16)],
        in_specs=[VMEM] * 9,
        out_specs=[HBM] * 4,
        scratch_shapes=[
            *[pltpu.VMEM(x, BF16) for x in results],
            pltpu.VMEM((NEW_PAGES, 2 * PAGE, HD), BF16),
            pltpu.SMEM((24, HD), jnp.int32),
            pltpu.SemaphoreType.DMA,
            pltpu.SemaphoreType.DMA((3 * ROWS // TILE,)),
            pltpu.SemaphoreType.DMA((NEW_PAGES,)),
        ],
        compiler_params=params(16),
        cost_estimate=cost(0, 1),
        name="project_late",
    )(table, block, *sums, *weights, cosine, sine)


def dot_nt(a, b):
    return lax.dot_general(a, b, (((1,), (1,)), ((), ())), preferred_element_type=F32)


def attend_kernel(table_ref, *refs):
    sources, out_ref, targets, (index_ref, keys, values, sems) = refs[:4], refs[4], refs[5:9], refs[9:]
    page_buf, q_buf, own_keys, own_values = targets
    indices = pltpu.make_async_copy(table_ref, index_ref, sems.at[4])
    indices.start()
    copies = [pltpu.make_async_copy(a, b, sems.at[i]) for i, (a, b) in enumerate(zip(sources, targets))]
    for copy in copies:
        copy.start()
    row = lax.broadcasted_iota(jnp.int32, (2 * PAGE, 2 * PAGE), 0)
    column = lax.broadcasted_iota(jnp.int32, (2 * PAGE, 2 * PAGE), 1)
    wanted = jnp.where(row < PAGE, 2 * row, 2 * (row - PAGE) + 1)
    picker = (column == wanted).astype(BF16)
    values[:, HD:] = jnp.ones((PAGES * PAGE, HD), BF16)
    indices.wait()
    copies[0].wait()
    for page in range(PAGES):
        both = jnp.dot(picker, page_buf[index_ref[TAKE, page]], preferred_element_type=F32)
        rows = slice(page * PAGE, (page + 1) * PAGE)
        keys[rows, :] = both[:PAGE].astype(BF16)
        values[rows, :HD] = both[PAGE:].astype(BF16)
    for copy in copies[1:]:
        copy.wait()
    block = 256
    allowed = lax.broadcasted_iota(jnp.int32, (block, block), 0) >= lax.broadcasted_iota(
        jnp.int32, (block, block), 1
    )
    for head in range(HEADS):
        lanes = slice(head * HD, (head + 1) * HD)
        for b in range(ROWS // block):
            rows = slice(b * block, (b + 1) * block)
            queries = q_buf[head, rows, :]
            own = dot_nt(queries, own_keys[: (b + 1) * block, :])
            diagonal = jnp.where(allowed, own[:, b * block :], -1e30)
            parts = [(diagonal, own_values[rows, :])]
            if b:
                parts.append((own[:, : b * block], own_values[: b * block, :]))
            parts.append((dot_nt(queries, keys[...]), values[...]))
            tops = [jnp.max(scores, axis=1, keepdims=True) for scores, _ in parts]
            top = functools.reduce(jnp.maximum, tops)
            both = jnp.zeros((block, 2 * HD), F32)
            for scores, held in parts:
                weights = jnp.exp2((scores - top) * SCALE).astype(BF16)
                both += jnp.dot(weights, held, preferred_element_type=F32)
            out_ref[rows, lanes] = (both[:, :HD] / both[:, HD:]).astype(BF16)


def attend(table, *sources):
    return pl.pallas_call(
        attend_kernel,
        out_shape=shape((ROWS, QW), BF16),
        in_specs=[VMEM] + [HBM] * len(sources),
        out_specs=VMEM,
        scratch_shapes=[
            *[pltpu.VMEM(x.shape, x.dtype) for x in sources],
            pltpu.SMEM((24, HD), jnp.int32),
            pltpu.VMEM((PAGES * PAGE, HD), BF16),
            pltpu.VMEM((PAGES * PAGE, 2 * HD), BF16),
            pltpu.SemaphoreType.DMA((5,)),
        ],
        compiler_params=params(40),
        cost_estimate=cost(2 * ROWS * 4 * 2560 * 512, 8 * MIB),
        name="attend",
    )(table, *[hbm(x) for x in sources])


def place_kernel(table_ref, source_ref, out_ref, received_ref, buffer, index_ref, in_sems, sems):
    indices = pltpu.make_async_copy(table_ref, index_ref, in_sems.at[0])
    arrival = pltpu.make_async_copy(source_ref, received_ref, in_sems.at[1])
    indices.start()
    arrival.start()
    indices.wait()
    arrival.wait()
    group = 4
    copies = []
    for i in range(SLOTS):
        source = index_ref[PLACE, i]
        page = received_ref[jnp.maximum(source - 1, 0)]
        buffer[i] = jnp.where(source > 0, page, jnp.zeros_like(page))
        if i % group == group - 1:
            slots = pl.ds(i + 1 - group, group)
            copy = pltpu.make_async_copy(
                buffer.at[slots], out_ref.at[slots], sems.at[i // group]
            )
            copy.start()
            copies.append(copy)
    for copy in copies:
        copy.wait()


def place_pages(table, received):
    return pl.pallas_call(
        place_kernel,
        out_shape=pltpu.HBM((SLOTS, 2 * PAGE, HD), BF16),
        in_specs=[VMEM, HBM],
        out_specs=HBM,
        scratch_shapes=[
            pltpu.VMEM(received.shape, BF16),
            pltpu.VMEM((SLOTS, 2 * PAGE, HD), BF16),
            pltpu.SMEM((24, HD), jnp.int32),
            pltpu.SemaphoreType.DMA((2,)),
            pltpu.SemaphoreType.DMA((SLOTS // 4,)),
        ],
        compiler_params=params(8),
        cost_estimate=cost(0, 2 * MIB),
        name="place_pages",
    )(table, hbm(received))


def shift(values, steps):
    pairs = [(i, ((i // 2 + steps[i % 2]) % 4) * 2 + i % 2) for i in range(8)]
    return lax.ppermute(values, "tp", pairs)


def swap(values):
    return lax.ppermute(values, "tp", [(i, i ^ 1) for i in range(8)])


def rope_tables(row_count, offset):
    half_dim = HD // 2
    frequency = 500000.0 ** (-(jnp.arange(half_dim, dtype=F32) * (2.0 / HD)))
    place = (offset + jnp.arange(row_count, dtype=jnp.int32)).astype(F32)
    angles = place[:, None] * frequency[None, :]
    cosine, sine = jnp.cos(angles), jnp.sin(angles)
    return jnp.concatenate([cosine, cosine], 1), jnp.concatenate([-sine, sine], 1)


def exchange(values):
    return lax.all_to_all(values, "pool", split_axis=0, concat_axis=0, tiled=True)


def body(hidden, w_query, w_keyval, store, page_owner, page_slot, new_owner):
    near = shift(hidden, (1, -1))
    table, packed = prelude(page_owner, page_slot, new_owner, store.reshape(64, 2 * PAGE, HD))
    pages = exchange(packed)
    sibling = swap(hidden)
    (sibling,) = after((table,), sibling)
    back = shift(sibling, (1, -1))
    tables = rope_tables(ROWS, PAGES * PAGE)
    weights = (w_query, w_keyval)
    blocks = ((OWN, True), (OWN, False))
    sums = project(blocks, [sibling], [hidden], *weights, tokens=tables)
    (near,) = after((sums[2],), near)
    far = shift(near, (1, -1))
    blocks = ((NEAR, False), (BACK, True))
    sums = project(blocks, [near, back], [], *weights, sums, flops=HIDES)
    blocks, ahead = ((NEAR, True), (BACK, False)), ((FAR, False), (FAR, True))
    held = [swap(near), swap(back)]
    *sums, last_q, last_kv = project(blocks, held, [], *weights, sums, ahead)
    (far,) = after((sums[2],), far)
    other = swap(far)
    sums = project_far(far, (last_q, last_kv), sums)
    queries, own_keys, own_values, send = project_late(
        table, other, sums, (last_q, last_kv), *tables
    )
    received = exchange(send)
    attended = attend(table, pages, queries, own_keys, own_values)
    placed = place_pages(table, received)
    return attended, placed.reshape(SLOTS, 1, PAGE, 2, HD)


def solution(mesh):
    in_specs = (
        P("pool", "tp"),
        P(None, "tp"),
        P(None, "tp"),
        P("pool", "tp", None, None, None),
        P(),
        P(),
        P(),
    )
    out_specs = (P("pool", "tp"), P("pool", "tp", None, None, None))
    return jax.shard_map(body, mesh=mesh, in_specs=in_specs, out_specs=out_specs, check_vma=False)
```

```python
import functools
import math

import jax
import jax.numpy as jnp
from jax import lax
from jax.experimental import pallas as pl
from jax.experimental.pallas import tpu as pltpu
from jax.sharding import PartitionSpec as P

D = 8192
HD = 128
PAGE = 64
CAP = 4
PUSH_CAP = 2
HEADS = 4
FEAT = 1024
QW = 512
KVW = 256
POOL = 16
PAGES = 32
NEW_PAGES = 8
SLOTS = 32
ROWS = 512
PUSH, TAKE, PLACE = 4, 16, 17
MIB = 1024 * 1024
SCALE = math.log2(math.e) / math.sqrt(HD)
HIDES = 20_000_000_000
F32 = jnp.float32
BF16 = jnp.bfloat16
ANY = pl.BlockSpec(memory_space=pl.ANY)
HBM = pl.BlockSpec(memory_space=pltpu.HBM)
VMEM = pl.BlockSpec(memory_space=pltpu.VMEM)
SMEM = pl.BlockSpec(memory_space=pltpu.SMEM)


def params(mib):
    return pltpu.CompilerParams(vmem_limit_bytes=mib * MIB)


def cost(flops, nbytes):
    return pl.CostEstimate(flops=flops, bytes_accessed=nbytes, transcendentals=0)


def hbm(array):
    return pltpu.with_memory_space_constraint(array, pltpu.HBM)


def shape(dims, dtype):
    return jax.ShapeDtypeStruct(dims, dtype)


def fill_table(owners, slots, targets, out_ref):
    me = lax.axis_index("pool")
    out_ref[...] = jnp.zeros_like(out_ref)
    lanes = lax.broadcasted_iota(jnp.int32, owners.shape, 1)
    rows = lax.broadcasted_iota(jnp.int32, owners.shape, 0)
    ranks = jnp.zeros_like(owners)
    for j in range(PAGES):
        ranks += ((owners == owners[:, j : j + 1]) & (lanes > j)).astype(jnp.int32)
    for k in range(CAP):
        chosen = jnp.where((owners == me) & (ranks == k), slots, 0)
        out_ref[:POOL, k : k + 1] = jnp.sum(chosen, axis=1, keepdims=True)
    mine = jnp.where(rows == me, owners * CAP + ranks, 0)
    out_ref[TAKE : TAKE + 1, :PAGES] = jnp.sum(mine, axis=0, keepdims=True)
    lanes = lax.broadcasted_iota(jnp.int32, targets.shape, 1)
    rows = lax.broadcasted_iota(jnp.int32, targets.shape, 0)
    kept = (targets == me).astype(jnp.int32)
    ranks = jnp.zeros_like(targets)
    slot = jnp.zeros_like(targets)
    for j in range(NEW_PAGES):
        later = rows > j
        ranks += ((targets == targets[j : j + 1, :]) & later).astype(jnp.int32)
        slot += jnp.where(later, kept[j : j + 1, :], 0)
    mine = jnp.where(lanes == me, targets * PUSH_CAP + ranks, 0)
    out_ref[:NEW_PAGES, PUSH : PUSH + 1] = jnp.sum(mine, axis=1, keepdims=True)
    of_request = jnp.sum(kept, axis=0, keepdims=True)
    for r in range(POOL):
        slot += jnp.where(lanes > r, of_request[:, r : r + 1], 0)
    source = jnp.zeros((NEW_PAGES, SLOTS), jnp.int32)
    slot_lanes = lax.broadcasted_iota(jnp.int32, source.shape, 1)
    for r in range(POOL):
        hit = (kept[:, r : r + 1] > 0) & (slot[:, r : r + 1] == slot_lanes)
        source += jnp.where(hit, r * PUSH_CAP + ranks[:, r : r + 1] + 1, 0)
    out_ref[PLACE : PLACE + 1, :SLOTS] = jnp.sum(source, axis=0, keepdims=True)


def prelude_kernel(*refs):
    owner_in, slot_in, target_in, store_in, table_ref, out_ref = refs[:6]
    owner_ref, slot_ref, target_ref, store_ref, index_ref, sems, page_sems = refs[6:]
    pairs = (
        (owner_in, owner_ref),
        (slot_in, slot_ref),
        (target_in, target_ref),
        (store_in, store_ref),
    )
    copies = [pltpu.make_async_copy(x, y, sems.at[i]) for i, (x, y) in enumerate(pairs)]
    for copy in copies:
        copy.start()
    for copy in copies[:3]:
        copy.wait()
    fill_table(owner_ref[...], slot_ref[...], target_ref[...], table_ref)
    indices = pltpu.make_async_copy(table_ref, index_ref, sems.at[4])
    indices.start()
    indices.wait()
    copies[3].wait()
    pages = [
        pltpu.make_async_copy(
            store_ref.at[index_ref[i // CAP, i % CAP]], out_ref.at[i], page_sems.at[i]
        )
        for i in range(POOL * CAP)
    ]
    for page in pages:
        page.start()
    for page in pages:
        page.wait()


def prelude(page_owner, page_slot, new_owner, store):
    return pl.pallas_call(
        prelude_kernel,
        out_shape=[
            shape((24, HD), jnp.int32),
            pltpu.HBM((POOL * CAP, 2 * PAGE, HD), BF16),
        ],
        in_specs=[HBM] * 4,
        out_specs=[VMEM, HBM],
        scratch_shapes=[
            pltpu.VMEM((POOL, PAGES), jnp.int32),
            pltpu.VMEM((POOL, PAGES), jnp.int32),
            pltpu.VMEM((NEW_PAGES, POOL), jnp.int32),
            pltpu.VMEM(store.shape, BF16),
            pltpu.SMEM((24, HD), jnp.int32),
            pltpu.SemaphoreType.DMA((5,)),
            pltpu.SemaphoreType.DMA((POOL * CAP,)),
        ],
        compiler_params=params(8),
        cost_estimate=cost(0, 1),
        name="prelude",
    )(*[hbm(x) for x in (page_owner, page_slot, new_owner.T, store)])


def block_index(steps, other_core):
    index = lax.axis_index("tp")
    core = lax.rem(index, 2)
    if other_core:
        core = 1 - core
    z = lax.rem(index // 2 + jnp.where(core == 0, steps[0], steps[1]), 4)
    return 2 * z + core


def squares_of(rows):
    wide = rows.astype(F32)
    total = None
    for lane in range(0, FEAT, HD):
        part = wide[:, lane : lane + HD]
        total = part * part if total is None else total + part * part
    return total


def weight_copies(refs, buffers, sems, blocks):
    copies = []
    for i, (steps, other) in enumerate(blocks):
        rows = pl.ds(pl.multiple_of(block_index(steps, other) * FEAT, FEAT), FEAT)
        copies.append(
            [
                pltpu.make_async_copy(ref.at[rows, :], buffer.at[i], sems.at[len(refs) * i + j])
                for j, (ref, buffer) in enumerate(zip(refs, buffers))
            ]
        )
    for group in copies:
        for copy in group:
            copy.start()
    return copies


OWN, NEAR, BACK, FAR = (0, 0), (3, 1), (1, 3), (2, 2)
TILE = 128


def project_kernel(blocks, held, has_sums, tokens, ahead, *refs):
    count = len(blocks)
    x_refs, refs = refs[:count], refs[count:]
    wq_ref, wkv_ref, refs = refs[0], refs[1], refs[2:]
    before, refs = (refs[:3], refs[3:]) if has_sums else (None, refs)
    refs = refs[tokens:]
    sums, refs = refs[:3], refs[3:]
    fetched, refs = (refs[:2], refs[2:]) if ahead else (None, refs)
    x_buf, wq_buf, wkv_buf, sems, x_sems, ahead_sems = refs
    copies = weight_copies((wq_ref, wkv_ref), (wq_buf, wkv_buf), sems, blocks)
    x_copies = {}
    for i in range(held, count):
        x_copies[i] = pltpu.make_async_copy(x_refs[i], x_buf.at[i - held], x_sems.at[i - held])
        x_copies[i].start()
    later = weight_copies((wq_ref, wkv_ref), fetched, ahead_sems, ahead) if ahead else []
    for i in range(count):
        copies[i][0].wait()
        copies[i][1].wait()
        if i in x_copies:
            x_copies[i].wait()
        for r in range(0, ROWS, TILE):
            rows = slice(r, r + TILE)
            x = x_refs[i][rows, :] if i < held else x_buf[i - held, rows, :]
            parts = (
                jnp.dot(x, wq_buf[i], preferred_element_type=F32),
                jnp.dot(x, wkv_buf[i], preferred_element_type=F32),
                squares_of(x),
            )
            for j, part in enumerate(parts):
                if i > 0:
                    sums[j][rows, :] += part
                elif has_sums:
                    sums[j][rows, :] = before[j][rows, :] + part
                else:
                    sums[j][rows, :] = part
    for group in later:
        for copy in group:
            copy.wait()


def project(blocks, held, direct, w_query, w_keyval, sums=(), ahead=(), tokens=(), flops=0):
    count = len(blocks)
    shapes = [shape((ROWS, w), F32) for w in (QW, KVW, HD)]
    if ahead:
        shapes += [shape((len(ahead), FEAT, w), BF16) for w in (QW, KVW)]
    return pl.pallas_call(
        functools.partial(project_kernel, blocks, len(held), bool(sums), len(tokens), ahead),
        out_shape=shapes,
        in_specs=[VMEM] * len(held)
        + [HBM] * (len(direct) + 2)
        + [VMEM] * len(sums)
        + [ANY] * len(tokens),
        out_specs=[VMEM] * len(shapes),
        scratch_shapes=[
            pltpu.VMEM((max(len(direct), 1), ROWS, FEAT), BF16),
            pltpu.VMEM((count, FEAT, QW), BF16),
            pltpu.VMEM((count, FEAT, KVW), BF16),
            pltpu.SemaphoreType.DMA((2 * count,)),
            pltpu.SemaphoreType.DMA((max(len(direct), 1),)),
            pltpu.SemaphoreType.DMA((max(2 * len(ahead), 1),)),
        ],
        compiler_params=params(24),
        cost_estimate=cost(flops, 1),
        name="project",
    )(*held, *[hbm(x) for x in (*direct, w_query, w_keyval)], *sums, *tokens)


def far_kernel(x_ref, wq_ref, wkv_ref, *refs):
    before, sums = refs[:3], refs[3:]
    for r in range(0, ROWS, TILE):
        rows = slice(r, r + TILE)
        x = x_ref[rows, :]
        sums[0][rows, :] = before[0][rows, :] + jnp.dot(x, wq_ref[0], preferred_element_type=F32)
        sums[1][rows, :] = before[1][rows, :] + jnp.dot(x, wkv_ref[0], preferred_element_type=F32)
        sums[2][rows, :] = before[2][rows, :] + squares_of(x)


def project_far(block, weights, sums):
    return pl.pallas_call(
        far_kernel,
        out_shape=[pltpu.HBM((ROWS, QW), F32)] + [shape((ROWS, w), F32) for w in (KVW, HD)],
        in_specs=[VMEM] * 6,
        out_specs=[VMEM] * 3,
        compiler_params=params(16),
        cost_estimate=cost(0, 1),
        name="project_far",
    )(block, *weights, *sums)


def after_kernel(*refs):
    pass


def after(tokens, *arrays, flops=0):
    count, skip = len(arrays), len(tokens)
    return pl.pallas_call(
        after_kernel,
        out_shape=[shape(x.shape, x.dtype) for x in arrays],
        in_specs=[ANY] * (count + skip),
        out_specs=[ANY] * count,
        input_output_aliases={i + skip: i for i in range(count)},
        compiler_params=params(1),
        cost_estimate=cost(flops, 1),
        name="after",
    )(*tokens, *arrays)


def turn(values, cosine, sine):
    return values * cosine + pltpu.roll(values, HD // 2, 1) * sine


def keyval_kernel(table_ref, x_ref, kv_in, sq_in, wkv_ref, cos_ref, sin_ref, *refs):
    keys_out, values_out, inv_out, x_out, send_out = refs[:5]
    keys_buf, values_buf, inv_buf, page_buf, index_ref, sems, page_sems = refs[5:]
    indices = pltpu.make_async_copy(table_ref, index_ref, sems.at[0])
    indices.start()
    copies = [pltpu.make_async_copy(x_ref, x_out, sems.at[1])]
    copies[0].start()
    row = lax.broadcasted_iota(jnp.int32, (2 * PAGE, 2 * PAGE), 0)
    column = lax.broadcasted_iota(jnp.int32, (2 * PAGE, 2 * PAGE), 1)
    picker = (column == (row >> 1) + (row & 1) * PAGE).astype(BF16)
    values_buf[:, HD:] = jnp.ones((ROWS, HD), BF16)
    for r in range(0, ROWS, TILE):
        rows = slice(r, r + TILE)
        x = x_ref[rows, :]
        kv_sum = kv_in[rows, :] + jnp.dot(x, wkv_ref[1], preferred_element_type=F32)
        squares = sq_in[rows, :] + squares_of(x)
        mean = jnp.sum(squares, axis=1, keepdims=True) / D
        inv_norm = jnp.broadcast_to(lax.rsqrt(mean + 1e-05), (TILE, HD))
        inv_buf[rows, :] = inv_norm
        keys = turn(kv_sum[:, :HD] * inv_norm, cos_ref[rows, :], sin_ref[rows, :]).astype(BF16)
        values = (kv_sum[:, HD:] * inv_norm).astype(BF16)
        keys_buf[rows, :] = keys
        values_buf[rows, :HD] = values
        if r == 0:
            indices.wait()
        for p in range(0, TILE, PAGE):
            page = (r + p) // PAGE
            both = jnp.concatenate([keys[p : p + PAGE], values[p : p + PAGE]], axis=0)
            page_buf[page] = jnp.dot(picker, both, preferred_element_type=F32).astype(BF16)
            target = send_out.at[index_ref[page, PUSH]]
            copies.append(pltpu.make_async_copy(page_buf.at[page], target, page_sems.at[page]))
            copies[-1].start()
        span = pl.ds(r, TILE)
        results = ((keys_buf, keys_out), (values_buf, values_out), (inv_buf, inv_out))
        for i, (source, target) in enumerate(results):
            sem = sems.at[2 + 3 * (r // TILE) + i]
            copies.append(pltpu.make_async_copy(source.at[span, :], target.at[span, :], sem))
            copies[-1].start()
    for copy in copies:
        copy.wait()


def project_keyval(table, block, sums, weights, cosine, sine):
    kept = [((ROWS, HD), BF16), ((ROWS, 2 * HD), BF16), ((ROWS, HD), F32)]
    sent = (POOL * PUSH_CAP, 2 * PAGE, HD)
    return pl.pallas_call(
        keyval_kernel,
        out_shape=[pltpu.HBM(*x) for x in (*kept, ((ROWS, FEAT), BF16), (sent, BF16))],
        in_specs=[VMEM] * 7,
        out_specs=[HBM] * 5,
        scratch_shapes=[
            *[pltpu.VMEM(*x) for x in kept],
            pltpu.VMEM((NEW_PAGES, 2 * PAGE, HD), BF16),
            pltpu.SMEM((24, HD), jnp.int32),
            pltpu.SemaphoreType.DMA((2 + 3 * ROWS // TILE,)),
            pltpu.SemaphoreType.DMA((NEW_PAGES,)),
        ],
        compiler_params=params(16),
        cost_estimate=cost(0, 1),
        name="project_keyval",
    )(table, block, *sums, weights, cosine, sine)


def dot_nt(a, b):
    return lax.dot_general(a, b, (((1,), (1,)), ((), ())), preferred_element_type=F32)


def attend_kernel(table_ref, *refs):
    sources, wq_ref, pages_ref, out_ref, refs = refs[:7], refs[7], refs[8], refs[9], refs[10:]
    targets, wq_buf, index_ref, page_buf, q_buf, keys, values, sems = refs[:7], *refs[7:]
    q_sum, x, inv_norm, cosine, sine, own_keys, own_values = targets
    indices = pltpu.make_async_copy(table_ref, index_ref, sems.at[8])
    indices.start()
    fetch = pltpu.make_async_copy(pages_ref, page_buf, sems.at[9])
    fetch.start()
    copies = [pltpu.make_async_copy(a, b, sems.at[i]) for i, (a, b) in enumerate(zip(sources, targets))]
    rows = pl.ds(pl.multiple_of(block_index(FAR, True) * FEAT, FEAT), FEAT)
    copies.insert(0, pltpu.make_async_copy(wq_ref.at[rows, :], wq_buf, sems.at[7]))
    for copy in copies:
        copy.start()
    row = lax.broadcasted_iota(jnp.int32, (2 * PAGE, 2 * PAGE), 0)
    column = lax.broadcasted_iota(jnp.int32, (2 * PAGE, 2 * PAGE), 1)
    wanted = jnp.where(row < PAGE, 2 * row, 2 * (row - PAGE) + 1)
    picker = (column == wanted).astype(BF16)
    values[:, HD:] = jnp.ones((PAGES * PAGE, HD), BF16)
    indices.wait()
    fetch.wait()
    for page in range(PAGES):
        both = jnp.dot(picker, page_buf[index_ref[TAKE, page]], preferred_element_type=F32)
        rows = slice(page * PAGE, (page + 1) * PAGE)
        keys[rows, :] = both[:PAGE].astype(BF16)
        values[rows, :HD] = both[PAGE:].astype(BF16)
    for copy in copies:
        copy.wait()
    for r in range(0, ROWS, TILE):
        rows = slice(r, r + TILE)
        total = q_sum[rows, :] + jnp.dot(x[rows, :], wq_buf[...], preferred_element_type=F32)
        for head in range(HEADS):
            part = total[:, head * HD : (head + 1) * HD] * inv_norm[rows, :]
            q_buf[head, rows, :] = turn(part, cosine[rows, :], sine[rows, :]).astype(BF16)
    block = 256
    allowed = lax.broadcasted_iota(jnp.int32, (block, block), 0) >= lax.broadcasted_iota(
        jnp.int32, (block, block), 1
    )
    for head in range(HEADS):
        lanes = slice(head * HD, (head + 1) * HD)
        for b in range(ROWS // block):
            rows = slice(b * block, (b + 1) * block)
            queries = q_buf[head, rows, :]
            own = dot_nt(queries, own_keys[: (b + 1) * block, :])
            diagonal = jnp.where(allowed, own[:, b * block :], -1e30)
            parts = [(diagonal, own_values[rows, :])]
            if b:
                parts.append((own[:, : b * block], own_values[: b * block, :]))
            parts.append((dot_nt(queries, keys[...]), values[...]))
            tops = [jnp.max(scores, axis=1, keepdims=True) for scores, _ in parts]
            top = functools.reduce(jnp.maximum, tops)
            both = jnp.zeros((block, 2 * HD), F32)
            for scores, held in parts:
                weights = jnp.exp2((scores - top) * SCALE).astype(BF16)
                both += jnp.dot(weights, held, preferred_element_type=F32)
            out_ref[rows, lanes] = (both[:, :HD] / both[:, HD:]).astype(BF16)


def attend(table, pages, sources, w_query):
    return pl.pallas_call(
        attend_kernel,
        out_shape=shape((ROWS, QW), BF16),
        in_specs=[VMEM] + [HBM] * (len(sources) + 2),
        out_specs=VMEM,
        scratch_shapes=[
            *[pltpu.VMEM(x.shape, x.dtype) for x in sources],
            pltpu.VMEM((FEAT, QW), BF16),
            pltpu.SMEM((24, HD), jnp.int32),
            pltpu.VMEM(pages.shape, BF16),
            pltpu.VMEM((HEADS, ROWS, HD), BF16),
            pltpu.VMEM((PAGES * PAGE, HD), BF16),
            pltpu.VMEM((PAGES * PAGE, 2 * HD), BF16),
            pltpu.SemaphoreType.DMA((10,)),
        ],
        compiler_params=params(40),
        cost_estimate=cost(2 * ROWS * 4 * 2560 * 512, 8 * MIB),
        name="attend",
    )(table, *[hbm(x) for x in (*sources, w_query, pages)])


def place_kernel(table_ref, received_ref, out_ref, buffer, index_ref, index_sem, sems):
    indices = pltpu.make_async_copy(table_ref, index_ref, index_sem)
    indices.start()
    indices.wait()
    group = 4
    copies = []
    for i in range(SLOTS):
        source = index_ref[PLACE, i]
        page = received_ref[jnp.maximum(source - 1, 0)]
        buffer[i] = jnp.where(source > 0, page, jnp.zeros_like(page))
        if i % group == group - 1:
            slots = pl.ds(i + 1 - group, group)
            copy = pltpu.make_async_copy(
                buffer.at[slots], out_ref.at[slots], sems.at[i // group]
            )
            copy.start()
            copies.append(copy)
    for copy in copies:
        copy.wait()


def place_pages(table, received):
    return pl.pallas_call(
        place_kernel,
        out_shape=pltpu.HBM((SLOTS, 2 * PAGE, HD), BF16),
        in_specs=[VMEM, VMEM],
        out_specs=HBM,
        scratch_shapes=[
            pltpu.VMEM((SLOTS, 2 * PAGE, HD), BF16),
            pltpu.SMEM((24, HD), jnp.int32),
            pltpu.SemaphoreType.DMA,
            pltpu.SemaphoreType.DMA((SLOTS // 4,)),
        ],
        compiler_params=params(8),
        cost_estimate=cost(0, 2 * MIB),
        name="place_pages",
    )(table, received)


def shift(values, steps):
    pairs = [(i, ((i // 2 + steps[i % 2]) % 4) * 2 + i % 2) for i in range(8)]
    return lax.ppermute(values, "tp", pairs)


def swap(values):
    return lax.ppermute(values, "tp", [(i, i ^ 1) for i in range(8)])


def rope_tables(row_count, offset):
    half_dim = HD // 2
    frequency = 500000.0 ** (-(jnp.arange(half_dim, dtype=F32) * (2.0 / HD)))
    place = (offset + jnp.arange(row_count, dtype=jnp.int32)).astype(F32)
    angles = place[:, None] * frequency[None, :]
    cosine, sine = jnp.cos(angles), jnp.sin(angles)
    return jnp.concatenate([cosine, cosine], 1), jnp.concatenate([-sine, sine], 1)


def exchange(values):
    return lax.all_to_all(values, "pool", split_axis=0, concat_axis=0, tiled=True)


def body(hidden, w_query, w_keyval, store, page_owner, page_slot, new_owner):
    near = shift(hidden, (1, -1))
    table, packed = prelude(page_owner, page_slot, new_owner, store.reshape(64, 2 * PAGE, HD))
    pages = exchange(packed)
    sibling = swap(hidden)
    (sibling,) = after((table,), sibling)
    back = shift(sibling, (1, -1))
    tables = rope_tables(ROWS, PAGES * PAGE)
    weights = (w_query, w_keyval)
    blocks = ((OWN, True), (OWN, False))
    sums = project(blocks, [sibling], [hidden], *weights, tokens=tables)
    (near,) = after((sums[2],), near)
    far = shift(near, (1, -1))
    blocks = ((NEAR, False), (BACK, True))
    sums = project(blocks, [near, back], [], *weights, sums, flops=HIDES)
    blocks, ahead = ((NEAR, True), (BACK, False)), ((FAR, False), (FAR, True))
    held = [swap(near), swap(back)]
    *sums, last_q, last_kv = project(blocks, held, [], *weights, sums, ahead)
    (far,) = after((sums[2],), far)
    other = swap(far)
    sums = project_far(far, (last_q, last_kv), sums)
    own_keys, own_values, inv_norm, other, send = project_keyval(
        table, other, sums[1:], last_kv, *tables
    )
    received = exchange(send)
    sources = (sums[0], other, inv_norm, *tables, own_keys, own_values)
    attended = attend(table, pages, sources, w_query)
    placed = place_pages(table, received)
    return attended, placed.reshape(SLOTS, 1, PAGE, 2, HD)


def solution(mesh):
    in_specs = (
        P("pool", "tp"),
        P(None, "tp"),
        P(None, "tp"),
        P("pool", "tp", None, None, None),
        P(),
        P(),
        P(),
    )
    out_specs = (P("pool", "tp"), P("pool", "tp", None, None, None))
    return jax.shard_map(body, mesh=mesh, in_specs=in_specs, out_specs=out_specs, check_vma=False)
```
